32 devices in a mesh: outer: 8 (over z, y), inner: 4 (over x, core).
Axes of the slice: x: 2, y: 2, z: 4, core: 2. Of those that a mesh axis runs over, the one named last changes fastest.
Arguments:
- tokens: bfloat16 [64, 256, 256], P('outer', 'inner'), may hold values from -6 to 6
- timestep: int32 [1], replicated, may hold values from 0 to 999
- mod_weight: bfloat16 [256, 2560], replicated, may hold values from -0.375 to 0.375
- fine_qkv_weight: bfloat16 [256, 768], replicated, may hold values from -8 to 8
- fine_out_weight: bfloat16 [256, 256], replicated, may hold values from -0.375 to 0.375
- merge_one: bfloat16 [1024, 512], replicated, may hold values from -0.1875 to 0.1875
- merge_two: bfloat16 [2048, 1024], replicated, may hold values from -0.125 to 0.125
- coarse_qkv_weight: bfloat16 [1024, 3072], P(None, 'inner'), may hold values from -8 to 8
- coarse_out_weight: bfloat16 [1024, 1024], P('inner'), may hold values from -0.1875 to 0.1875
Outputs:
- fine_skip: bfloat16 [64, 256, 256], P('outer', 'inner')
- coarse_out: bfloat16 [16, 64, 1024], P('outer', 'inner')
The draws below stay inside these ranges and needn't reach their ends.
Inputs may be any that keep to these rules, and one draw needn't show every extreme that they name: `timestep`: the diffusion step's index.
All inputs are finite; a program needn't handle non-finite values.
Results may differ from the reference program's by a relative error of at most 0.015.
Values may be sent and summed in bfloat16 or wider, within the bound.
No kernel may reach another device: no remote copies, remote signals or barrier semaphores. Data moves between devices by JAX's collectives and lax.ppermute only.
A program may use at most 64 MiB of HBM per device.

```python
import math
import jax
import jax.numpy as jnp
from jax import lax

FW = 256
MW = 512
CW = 1024
HD = 64
TEMB = 256
WIN = 3
LAT = 64
LON = 256
CLAT = 16
CLON = 64


def draw_fine_qkv_weight(key, part):
    key = jax.random.fold_in(key, 11)
    base_key = jax.random.fold_in(key, 0)
    result = jnp.clip(jax.random.normal(base_key, (FW, 3 * FW), jnp.float32), -4.0, 4.0) / math.sqrt(FW)
    return result.astype(jnp.bfloat16)


def draw_coarse_qkv_weight(key, part):
    key = jax.random.fold_in(key, 23)
    base_key = jax.random.fold_in(key, 0)
    head_count = CW // HD
    result = jnp.clip(jax.random.normal(base_key, (CW, head_count, 3, HD), jnp.float32), -4.0, 4.0) / math.sqrt(CW)
    return result.reshape(CW, 3 * CW).astype(jnp.bfloat16)


def levels(key, dims, cuts, low, high):
    def one(dim, shards_of):
        draws = jax.random.uniform(jax.random.fold_in(jax.random.fold_in(key, 6), dim), (shards_of,), jnp.float32, low / len(cuts), high / len(cuts))
        return jnp.repeat(jnp.exp(draws), dims[dim] // shards_of).reshape((-1,) + (1,) * (len(dims) - dim - 1))

    loudness = one(*cuts[0])
    for cut in cuts[1:]:
        loudness = loudness * one(*cut)
    return loudness


def noise(stream_key, shape, scale, limit, shards=(), kind=jnp.bfloat16):
    gain = levels(stream_key, shape, shards, -0.22, 0.18) if shards else 1.0
    array = jax.random.normal(stream_key, shape, jnp.float32) * scale * gain
    return jnp.minimum(jnp.maximum(array, -limit), limit).astype(kind)


def setup_inputs(seed: int = 0) -> dict:
    seeds = jax.random.split(jax.random.key(seed), 10)
    return {
        "tokens": noise(seeds[0], (LAT, LON, FW), 1.0, 6.0, ((0, 8), (1, 4))),
        "timestep": jax.random.randint(seeds[1], (1,), 0, 1000).astype(jnp.int32),
        "mod_weight": noise(seeds[2], (TEMB, 2 * FW + 2 * CW), TEMB ** -0.5, 0.375),
        "fine_qkv_weight": draw_fine_qkv_weight(jax.random.fold_in(seeds[9], 71), 0),
        "fine_out_weight": noise(seeds[4], (FW, FW), FW ** -0.5, 0.375),
        "merge_one": noise(seeds[5], (4 * FW, MW), (4 * FW) ** -0.5, 0.1875),
        "merge_two": noise(seeds[6], (4 * MW, CW), (4 * MW) ** -0.5, 0.125),
        "coarse_qkv_weight": draw_coarse_qkv_weight(jax.random.fold_in(seeds[9], 71), 0),
        "coarse_out_weight": noise(seeds[8], (CW, CW), CW ** -0.5, 0.1875, ((0, 4),)),
    }


def layer_norm(values, scale, shift):
    x = values.astype(jnp.float32)
    mean = lax.optimization_barrier(jnp.mean(x, axis=-1, keepdims=True))
    var = lax.optimization_barrier(jnp.mean((x - mean) * (x - mean), axis=-1, keepdims=True))
    return ((x - mean) * lax.rsqrt(var + 1e-06) * (1.0 + scale) + shift).astype(jnp.bfloat16)

def embed(timestep, width):
    half = width // 2
    freq = jnp.exp(-math.log(10000.0) * jnp.arange(half, dtype=jnp.float32) / half)
    angle = timestep.astype(jnp.float32)[0] * freq
    return jnp.concatenate([jnp.cos(angle), jnp.sin(angle)]).astype(jnp.bfloat16)[None, :]

def merged(values):
    rows, cols, width = values.shape
    grid = values.reshape(rows // 2, 2, cols // 2, 2, width).transpose(0, 2, 1, 3, 4)
    return grid.reshape(rows // 2, cols // 2, 4 * width)

def neighbour_attention(query, padded, rows_ok, heads):
    rows, cols, width = query.shape
    size = width // heads
    span = 2 * WIN + 1
    query4 = query.reshape(rows, cols, heads, size).astype(jnp.float32)
    scores = []
    for down in range(span):
        for side in range(span):
            keys = padded[down:down + rows, side:side + cols, :width].reshape(rows, cols, heads, size)
            score = jnp.einsum('rchd,rchd->rch', query4, keys.astype(jnp.float32)) / math.sqrt(size)
            scores.append(jnp.where(rows_ok[down:down + rows][:, None, None], score, -1e+30))
    stacked = jnp.stack(scores)
    weights = jax.nn.softmax(stacked, axis=0).astype(jnp.bfloat16)
    total = jnp.zeros((rows, cols, heads, size), jnp.float32)
    index = 0
    for down in range(span):
        for side in range(span):
            values = padded[down:down + rows, side:side + cols, width:].reshape(rows, cols, heads, size)
            total = total + weights[index][..., None].astype(jnp.float32) * values.astype(jnp.float32)
            index += 1
    return total.astype(jnp.bfloat16).reshape(rows, cols, width)

def reference(tokens, timestep, mod_weight, fine_qkv_weight, fine_out_weight, merge_one, merge_two, coarse_qkv_weight, coarse_out_weight):
    emb = embed(timestep, TEMB)
    mod = jnp.dot(emb, mod_weight, preferred_element_type=jnp.float32)[0]
    fine_scale = mod[:FW]
    fine_shift = mod[FW:2 * FW]
    coarse_scale = mod[2 * FW:2 * FW + CW]
    coarse_shift = mod[2 * FW + CW:]
    rows, cols = (LAT, LON)
    normed = layer_norm(tokens, fine_scale, fine_shift)
    qkv = jnp.dot(normed.reshape(rows * cols, FW), fine_qkv_weight, preferred_element_type=jnp.float32)
    qkv = qkv.astype(jnp.bfloat16).reshape(rows, cols, 3 * FW)
    keyval = jnp.pad(qkv[..., FW:], ((WIN, WIN), (0, 0), (0, 0)))
    keyval = jnp.concatenate([keyval[:, cols - WIN:], keyval, keyval[:, :WIN]], axis=1)
    row_ids = jnp.arange(rows + 2 * WIN) - WIN
    rows_ok = (row_ids >= 0) & (row_ids < rows)
    att = neighbour_attention(qkv[..., :FW], keyval, rows_ok, FW // HD)
    proj = jnp.dot(att.reshape(rows * cols, FW), fine_out_weight, preferred_element_type=jnp.float32)
    fine_skip = (tokens.reshape(rows * cols, FW).astype(jnp.float32) + proj).astype(jnp.bfloat16).reshape(rows, cols, FW)
    middle = jnp.dot(merged(fine_skip).reshape(-1, 4 * FW), merge_one, preferred_element_type=jnp.float32)
    middle = middle.astype(jnp.bfloat16).reshape(rows // 2, cols // 2, MW)
    coarse_in = jnp.dot(merged(middle).reshape(-1, 4 * MW), merge_two, preferred_element_type=jnp.float32)
    coarse_in = coarse_in.astype(jnp.bfloat16)
    count = coarse_in.shape[0]
    cnormed = layer_norm(coarse_in, coarse_scale, coarse_shift)
    cqkv = jnp.dot(cnormed, coarse_qkv_weight, preferred_element_type=jnp.float32).astype(jnp.bfloat16)
    heads_first = cqkv.reshape(count, CW // HD, 3, HD).transpose(1, 2, 0, 3)
    block = math.gcd(count, 1024)

    def head_attention(item):
        keys = item[1]
        values = item[2]

        def one_block(queries):
            score = jnp.dot(queries, keys.T, preferred_element_type=jnp.float32) / math.sqrt(HD)
            weights = jax.nn.softmax(score, axis=-1).astype(jnp.bfloat16)
            return jnp.dot(weights, values, preferred_element_type=jnp.float32).astype(jnp.bfloat16)
        return lax.map(one_block, item[0].reshape(count // block, block, HD)).reshape(count, HD)
    catt = lax.map(head_attention, heads_first).transpose(1, 0, 2).reshape(count, CW)
    cproj = jnp.dot(catt, coarse_out_weight, preferred_element_type=jnp.float32)
    coarse_out = (coarse_in.astype(jnp.float32) + cproj).astype(jnp.bfloat16).reshape(CLAT, CLON, CW)
    return (fine_skip, coarse_out)
```

```python
import math

import jax
import jax.numpy as jnp
from jax import lax
from jax.experimental import pallas as pl
from jax.experimental.pallas import tpu as pltpu
from jax.sharding import PartitionSpec as P

HD = 64
WIN = 3
LEFT = 8
BLOCK = 8
BF = jnp.bfloat16
F32 = jnp.float32
VM = pl.BlockSpec(memory_space=pltpu.VMEM)
SM = pl.BlockSpec(memory_space=pltpu.SMEM)
HB = pl.BlockSpec(memory_space=pl.ANY)
LIMIT = 48 * 1024 * 1024


def embed(timestep, width):
    half = width // 2
    freq = jnp.exp(-math.log(10000.0) * jnp.arange(half, dtype=F32) / half)
    angle = timestep.astype(F32)[0] * freq
    return jnp.concatenate([jnp.cos(angle), jnp.sin(angle)]).astype(BF)[None, :]


def layer_norm(x, scale, shift):
    mean = jnp.mean(x, axis=-1, keepdims=True)
    var = jnp.mean((x - mean) * (x - mean), axis=-1, keepdims=True)
    return ((x - mean) * lax.rsqrt(var + 1e-06) * (1.0 + scale) + shift).astype(BF)


def mm(a, b):
    return jnp.dot(a, b, preferred_element_type=F32)


def mm_t(a, b):
    return lax.dot_general(a, b, (((1,), (1,)), ((), ())), preferred_element_type=F32)


def fine_kernel(
    lim_ref,
    mod_ref,
    tok_ref,
    pad_ref,
    qkvw_ref,
    outw_ref,
    one_hbm,
    two_hbm,
    skip_ref,
    cin_ref,
    cnorm_ref,
    kv_ref,
    q_ref,
    res_ref,
    lane_ref,
    one_ref,
    two_ref,
    sems,
):
    copy_one = pltpu.make_async_copy(one_hbm, one_ref, sems.at[0])
    copy_two = pltpu.make_async_copy(two_hbm, two_ref, sems.at[1])
    copy_one.start()
    copy_two.start()
    rows, cols, width = tok_ref.shape
    prow, pcol = pad_ref.shape[:2]
    cw = cin_ref.shape[1]
    heads = width // HD
    fscale, fshift = mod_ref[:, :width], mod_ref[:, width : 2 * width]
    cscale, cshift = mod_ref[:, 2 * width : 2 * width + cw], mod_ref[:, 2 * width + cw :]

    own = tok_ref[...].astype(F32).reshape(rows * cols, width)
    qn = layer_norm(own, fscale, fshift)
    q = mm(qn, qkvw_ref[:, :width])
    q_ref[...] = q.reshape(rows, cols, width)
    ext = pad_ref[...].astype(F32).reshape(prow * pcol, width)
    kn = layer_norm(ext, fscale, fshift)
    kv_ref[...] = mm(kn, qkvw_ref[:, width:]).reshape(prow, pcol, 2 * width)

    nq = rows * BLOCK
    span = BLOCK + 8
    nk = prow * span
    lo, hi = lim_ref[0], lim_ref[1]
    qi = lax.broadcasted_iota(jnp.int32, (heads * nq, nk), 0) % nq
    ki = lax.broadcasted_iota(jnp.int32, (heads * nq, nk), 1)
    kr, kc = ki // span, ki % span
    dr, dc = kr - qi // BLOCK, kc - qi % BLOCK
    ok = (dr >= 0) & (dr <= 2 * WIN) & (dc >= 0) & (dc <= 2 * WIN) & (kr >= lo) & (kr < hi)
    bias = jnp.where(ok, 0.0, -1e30).astype(F32)
    lane_head = lax.broadcasted_iota(jnp.int32, (nq, width), 1) // HD

    for j in range(cols // BLOCK):
        qb = q_ref[:, j * BLOCK : (j + 1) * BLOCK, :].reshape(nq, width)
        qb = qb.astype(BF).astype(F32) * (1.0 / math.sqrt(HD))
        qs = jnp.concatenate([jnp.where(lane_head == h, qb, 0.0) for h in range(heads)], axis=0)
        kvb = kv_ref[:, j * BLOCK : j * BLOCK + span, :].reshape(nk, 2 * width).astype(BF)
        s = mm_t(qs.astype(BF), kvb[:, :width]) + bias
        p = jnp.exp(s - jnp.max(s, axis=1, keepdims=True))
        o = mm(p.astype(BF), kvb[:, width:]) / jnp.sum(p, axis=1, keepdims=True)
        att = jnp.zeros((nq, width), F32)
        for h in range(heads):
            att = jnp.where(lane_head == h, o[h * nq : (h + 1) * nq], att)
        proj = mm(att.astype(BF), outw_ref[...]).reshape(rows, BLOCK, width)
        res_ref[:, j * BLOCK : (j + 1) * BLOCK, :] = proj
    res = (res_ref[...] + tok_ref[...].astype(F32)).astype(BF)
    skip_ref[...] = res
    for k in range(width // 128):
        lane_ref[k] = res[:, :, k * 128 : (k + 1) * 128].astype(F32)

    copy_one.wait()
    groups = []
    for a in range(2):
        for b in range(2):
            parts = []
            for dr_ in range(2):
                for dc_ in range(2):
                    r, c = 2 * a + dr_, 2 * b + dc_
                    for k in range(width // 128):
                        strips = [
                            lane_ref[k, rr, pl.ds(c, cols // 4, stride=4), :]
                            for rr in range(r, rows, 4)
                        ]
                        parts.append(jnp.concatenate(strips, axis=0))
            groups.append(jnp.concatenate(parts, axis=1))
    count = (rows // 4) * (cols // 4)
    mid = mm(jnp.concatenate(groups, axis=0).astype(BF), one_ref[...]).astype(BF)
    mid = jnp.concatenate([mid[g * count : (g + 1) * count] for g in range(4)], axis=1)
    copy_two.wait()
    cin = mm(mid, two_ref[...]).astype(BF)
    cin_ref[...] = cin
    cnorm_ref[...] = layer_norm(cin.astype(F32), cscale, cshift)


def qkv_kernel(groups, zi_ref, *refs):
    xs, w_ref, out_ref = refs[:-2], refs[-2], refs[-1]
    x = jnp.concatenate([r[...] for r in xs], axis=0)
    y = mm(x, w_ref[...])
    band = y.shape[0]
    half = band // 2
    zi = zi_ref[0]
    for h in range(groups):
        q = y[:, h * 3 * HD : h * 3 * HD + HD]
        kv = y[:, h * 3 * HD + HD : (h + 1) * 3 * HD]
        qp = jnp.concatenate([q[:half], q[half:]], axis=1)
        out_ref[zi ^ h] = jnp.concatenate([kv, qp], axis=0).astype(BF)


def attention_kernel(groups, *refs):
    own, others, out_refs = refs[:groups], refs[groups:-1], refs[-1]
    band = own[0].shape[0] * 2 // 3
    half = band // 2
    lane = lax.broadcasted_iota(jnp.int32, (half, 2 * HD), 1)
    qs = []
    for r in own:
        qp = r[band:, :].astype(F32) * (1.0 / math.sqrt(HD))
        qs.append(jnp.where(lane < HD, qp, 0.0))
        qs.append(jnp.where(lane < HD, pltpu.roll(qp, HD, 1), 0.0))
    kvs = [r[:band, :] for r in own] + [r[...] for r in others]
    kv = jnp.concatenate(kvs, axis=0)
    for g in range(groups):
        q = jnp.concatenate(qs[2 * g : 2 * g + 2], axis=0).astype(BF)
        s = mm_t(q, kv)
        p = jnp.exp(s - jnp.max(s, axis=1, keepdims=True))
        o = mm(p.astype(BF), kv) / jnp.sum(p, axis=1, keepdims=True)
        out_refs[g] = jnp.where(lane < HD, pltpu.roll(o[:half], HD, 1), o[half:]).astype(BF)


def project_kernel(groups, zi_ref, *refs):
    pieces, w_ref, out_ref = refs[:groups], refs[groups], refs[groups + 1]
    zi = zi_ref[0]
    half = pieces[0].shape[0]
    acc = None
    if groups % 2:
        lane = lax.broadcasted_iota(jnp.int32, (half, 2 * HD), 1)
        for g in range(groups):
            w = w_ref[pl.ds(pl.multiple_of((zi ^ g) * HD, HD), HD), :]
            x = pieces[g][...].astype(F32)
            a = jnp.concatenate([x[:, :HD], x[:, HD:]], axis=0).astype(BF)
            y = mm(a, w)
            acc = y if acc is None else acc + y
    else:
        lane = lax.broadcasted_iota(jnp.int32, (half, 2 * HD), 1)
        cols, ws = [], []
        for g in range(0, groups, 2):
            x0, x1 = pieces[g][...].astype(F32), pieces[g + 1][...].astype(F32)
            low = jnp.where(lane < HD, x0, pltpu.roll(x1, HD, 1))
            high = jnp.where(lane < HD, pltpu.roll(x0, HD, 1), x1)
            cols.append(jnp.concatenate([low, high], axis=0))
        for g in range(groups):
            ws.append(w_ref[pl.ds(pl.multiple_of((zi ^ g) * HD, HD), HD), :])
        a = jnp.concatenate(cols, axis=1).astype(BF)
        acc = mm(a, jnp.concatenate(ws, axis=0))
    out_ref[...] = acc.astype(BF).reshape(out_ref.shape)


def sum_kernel(*refs):
    cin_ref, parts, out_ref = refs[0], refs[1:-1], refs[-1]
    total = parts[0][...].astype(F32)
    for r in parts[1:]:
        total = total + r[...].astype(F32)
    out_ref[...] = (cin_ref[...].astype(F32) + total).astype(BF).reshape(out_ref.shape)


def call(kernel, out_shape, in_specs, scratch=(), name=None):
    many = isinstance(out_shape, (tuple, list))
    return pl.pallas_call(
        kernel,
        out_shape=out_shape,
        in_specs=in_specs,
        out_specs=tuple(VM for _ in out_shape) if many else VM,
        scratch_shapes=list(scratch),
        compiler_params=pltpu.CompilerParams(vmem_limit_bytes=LIMIT),
        name=name,
    )


def swap(x, axis, step):
    size = lax.axis_size(axis)
    return lax.ppermute(x, axis, [(i, i ^ step) for i in range(size)])


def body(
    tokens,
    timestep,
    mod_weight,
    fine_qkv_weight,
    fine_out_weight,
    merge_one,
    merge_two,
    coarse_qkv_weight,
    coarse_out_weight,
):
    rows, cols, width = tokens.shape
    cw = merge_two.shape[1]
    no, ni = lax.axis_size("outer"), lax.axis_size("inner")
    oi = lax.axis_index("outer")
    north = lax.ppermute(tokens[rows - WIN :], "outer", [(i, i + 1) for i in range(no - 1)])
    south = lax.ppermute(tokens[:WIN], "outer", [(i + 1, i) for i in range(no - 1)])
    tall = jnp.concatenate([north, tokens, south], axis=0)
    west = lax.ppermute(tall[:, cols - WIN :], "inner", [(i, (i + 1) % ni) for i in range(ni)])
    east = lax.ppermute(tall[:, :WIN], "inner", [((i + 1) % ni, i) for i in range(ni)])
    fill = jnp.zeros((rows + 2 * WIN, 16 - 2 * WIN, width), BF)
    padded = jnp.concatenate([west, tall, east, fill], axis=1)

    emb = embed(timestep, mod_weight.shape[0])
    mod = mm(emb, mod_weight)
    limits = jnp.stack(
        [jnp.where(oi == 0, WIN, 0), jnp.where(oi == no - 1, rows + WIN, rows + 2 * WIN)]
    ).astype(jnp.int32)
    count = (rows // 4) * (cols // 4)
    fine_skip, coarse_in, cnormed = call(
        fine_kernel,
        (
            jax.ShapeDtypeStruct(tokens.shape, BF),
            jax.ShapeDtypeStruct((count, cw), BF),
            jax.ShapeDtypeStruct((count, cw), BF),
        ),
        [SM, VM, VM, VM, VM, VM, HB, HB],
        scratch=[
            pltpu.VMEM((rows + 2 * WIN, cols + 16, 2 * width), F32),
            pltpu.VMEM((rows, cols, width), F32),
            pltpu.VMEM((rows, cols, width), F32),
            pltpu.VMEM((width // 128, rows, cols, 128), F32),
            pltpu.VMEM(merge_one.shape, BF),
            pltpu.VMEM(merge_two.shape, BF),
            pltpu.SemaphoreType.DMA((2,)),
        ],
        name="fine",
    )(limits, mod, tokens, padded, fine_qkv_weight, fine_out_weight, merge_one, merge_two)

    groups = coarse_qkv_weight.shape[1] // (3 * HD)
    sub = no // groups
    zi = (oi // sub).astype(jnp.int32)[None]
    band = ni * count
    gathered = [cnormed] + [swap(cnormed, "inner", k) for k in range(1, ni)]
    pieces = call(
        lambda *r: qkv_kernel(groups, *r),
        jax.ShapeDtypeStruct((groups, band + band // 2, 2 * HD), BF),
        [SM] + [VM] * (ni + 1),
        name="qkv",
    )(zi, *gathered, coarse_qkv_weight)
    own = [pieces[0]] + [swap(pieces[g], "outer", g * sub) for g in range(1, groups)]
    others = [swap(p[:band], "outer", s) for s in range(1, sub) for p in own]
    att = call(
        lambda *r: attention_kernel(groups, *r),
        jax.ShapeDtypeStruct((groups, band // 2, 2 * HD), BF),
        [VM] * (groups + len(others)),
        name="attention",
    )(*own, *others)
    back = [att[0]] + [swap(att[g], "outer", g * sub) for g in range(1, groups)]
    proj = call(
        lambda *r: project_kernel(groups, *r),
        jax.ShapeDtypeStruct((ni, count, cw), BF),
        [SM] + [VM] * (groups + 1),
        name="project",
    )(zi, *back, coarse_out_weight)
    parts = [proj[0]] + [swap(proj[k], "inner", k) for k in range(1, ni)]
    coarse_out = call(
        sum_kernel,
        jax.ShapeDtypeStruct((rows // 4, cols // 4, cw), BF),
        [VM] * (ni + 1),
        name="sum",
    )(coarse_in, *parts)
    return (fine_skip, coarse_out)


def solution(mesh):
    return jax.shard_map(
        body,
        mesh=mesh,
        in_specs=(
            P("outer", "inner", None),
            P(),
            P(),
            P(),
            P(),
            P(),
            P(),
            P(None, "inner"),
            P("inner", None),
        ),
        out_specs=(P("outer", "inner", None), P("outer", "inner", None)),
        check_vma=False,
    )
```

```python
import math

import jax
import jax.numpy as jnp
from jax import lax
from jax.experimental import pallas as pl
from jax.experimental.pallas import tpu as pltpu
from jax.sharding import PartitionSpec as P

HD = 64
WIN = 3
BLOCK = 8
SPAN = 16
BF = jnp.bfloat16
F32 = jnp.float32
VM = pl.BlockSpec(memory_space=pltpu.VMEM)
SM = pl.BlockSpec(memory_space=pltpu.SMEM)
HB = pl.BlockSpec(memory_space=pl.ANY)
HM = pl.BlockSpec(memory_space=pltpu.HBM)
MIB = 1024 * 1024


def embed(timestep, width):
    half = width // 2
    freq = jnp.exp(-math.log(10000.0) * jnp.arange(half, dtype=F32) / half)
    angle = timestep.astype(F32)[0] * freq
    return jnp.concatenate([jnp.cos(angle), jnp.sin(angle)]).astype(BF)[None, :]


def layer_norm(x, scale, shift):
    mean = jnp.mean(x, axis=-1, keepdims=True)
    var = jnp.mean((x - mean) * (x - mean), axis=-1, keepdims=True)
    return ((x - mean) * lax.rsqrt(var + 1e-06) * (1.0 + scale) + shift).astype(BF)


def mm(a, b):
    return jnp.dot(a, b, preferred_element_type=F32)


def mm_t(a, b):
    return lax.dot_general(a, b, (((1,), (1,)), ((), ())), preferred_element_type=F32)


def shifted(x):
    rows, cols, width = x.shape
    left = jnp.zeros((rows, WIN, width), F32)
    right = jnp.zeros((rows, BLOCK - WIN, width), F32)
    return jnp.concatenate([left, x, right], axis=1)


def key_values(x, mod_ref, w_ref):
    rows, cols, width = x.shape
    flat = x.reshape(rows * cols, width)
    n = layer_norm(flat, mod_ref[:, :width], mod_ref[:, width : 2 * width])
    return mm(n, w_ref[...]).reshape(rows, cols, 2 * width)


def sides(lim_ref, far_ref, near_ref):
    odd = jnp.broadcast_to(lim_ref[2], far_ref.shape) == 1
    far, near = far_ref[...].astype(F32), near_ref[...].astype(F32)
    return jnp.where(odd, near, far), jnp.where(odd, far, near)


def columns_kernel(lim_ref, far_ref, near_ref, tok_ref, right_ref, left_ref):
    cols, width = tok_ref.shape[1:]
    for out_ref, at in ((right_ref, cols - 2 * BLOCK), (left_ref, 0)):
        chunk = pl.ds(at, 2 * BLOCK)
        north, south = sides(lim_ref, far_ref.at[:, chunk], near_ref.at[:, chunk])
        x = jnp.concatenate([north, tok_ref[:, chunk].astype(F32), south], axis=0)
        zero = jnp.zeros((x.shape[0], BLOCK, width), F32)
        if at:
            x = jnp.concatenate([x[:, 2 * BLOCK - WIN :], zero[:, WIN:]], axis=1)
        else:
            x = jnp.concatenate([zero[:, :WIN], x[:, :WIN], zero[:, 2 * WIN :]], axis=1)
        out_ref[...] = x.astype(BF)


def own_kernel(
    lim_ref, mod_ref, tok_ref, w_ref, out_ref, q_ref, kv_ref, bias_ref, kvw_ref, outw_ref
):
    kvw_ref[...] = w_ref[:, tok_ref.shape[2] :]
    outw_ref[...] = out_ref[...]
    rows, cols, width = tok_ref.shape
    tok = tok_ref[...].astype(F32)
    fscale, fshift = mod_ref[:, :width], mod_ref[:, width : 2 * width]
    n = layer_norm(tok.reshape(rows * cols, width), fscale, fshift)
    q = mm(n, w_ref[:, :width]).astype(BF).astype(F32) * (1.0 / math.sqrt(HD))
    q_ref[...] = q.reshape(rows, cols, width)
    kv_ref[...] = key_values(shifted(tok), mod_ref, kvw_ref)

    nq, nk = bias_ref.shape
    per = rows * BLOCK
    lo, hi = lim_ref[0], lim_ref[1]
    qi = lax.broadcasted_iota(jnp.int32, (nq, nk), 0) % per
    ki = lax.broadcasted_iota(jnp.int32, (nq, nk), 1)
    kr, kc = ki // SPAN, ki % SPAN
    dr, dc = kr - qi // BLOCK, kc - qi % BLOCK
    ok = (dr >= 0) & (dr <= 2 * WIN) & (dc >= 0) & (dc <= 2 * WIN) & (kr >= lo) & (kr < hi)
    bias_ref[...] = jnp.where(ok, 0.0, -1e30).astype(F32)


def order_kernel(cin_ref, cw_ref, order_ref, keep_ref):
    keep_ref[...] = cin_ref[...]
    groups = cw_ref.shape[1] // (3 * HD)
    kvs, qs = [], []
    for h in range(groups):
        qs.append(cw_ref[:, h * 3 * HD : h * 3 * HD + HD].astype(F32))
        kvs.append(cw_ref[:, h * 3 * HD + HD : (h + 1) * 3 * HD].astype(F32))
    order_ref[...] = jnp.concatenate(kvs + qs, axis=1).astype(BF)


def attend(q_ref, win, bias_ref, outw_ref, j):
    rows, cols, width = q_ref.shape
    heads, nq = width // HD, rows * BLOCK
    lane_head = lax.broadcasted_iota(jnp.int32, (nq, width), 1) // HD
    qb = q_ref[:, j * BLOCK : (j + 1) * BLOCK, :].reshape(nq, width)
    qs = jnp.concatenate([jnp.where(lane_head == h, qb, 0.0) for h in range(heads)], axis=0)
    kvb = win.reshape(win.shape[0] * SPAN, 2 * width).astype(BF)
    s = mm_t(qs.astype(BF), kvb[:, :width]) + bias_ref[...]
    p = jnp.exp(s - jnp.max(s, axis=1, keepdims=True))
    o = mm(p.astype(BF), kvb[:, width:]) / jnp.sum(p, axis=1, keepdims=True)
    att = o[:nq]
    for h in range(1, heads):
        att = jnp.where(lane_head == h, o[h * nq : (h + 1) * nq], att)
    return mm(att.astype(BF), outw_ref[...]).reshape(rows, BLOCK, width)


def inner_kernel(
    lim_ref,
    mod_ref,
    far_ref,
    near_ref,
    w_ref,
    outw_ref,
    q_ref,
    kv_ref,
    bias_ref,
    nkv_ref,
    skv_ref,
    res_ref,
):
    north, south = sides(lim_ref, far_ref, near_ref)
    nkv_ref[...] = key_values(shifted(north), mod_ref, w_ref)
    skv_ref[...] = key_values(shifted(south), mod_ref, w_ref)
    cols = q_ref.shape[1]
    for j in range(1, cols // BLOCK - 1):
        win = jnp.concatenate(
            [r[:, j * BLOCK : j * BLOCK + SPAN, :] for r in (nkv_ref, kv_ref, skv_ref)], axis=0
        )
        res_ref[:, j * BLOCK : (j + 1) * BLOCK, :] = attend(q_ref, win, bias_ref, outw_ref, j)


def edge_kernel(
    mod_ref,
    west_ref,
    east_ref,
    tok_ref,
    w_ref,
    outw_ref,
    q_ref,
    kv_ref,
    bias_ref,
    nkv_ref,
    skv_ref,
    res_ref,
    one_ref,
    two_ref,
    skip_hbm,
    cin_ref,
    skip_ref,
    lane_ref,
    sem,
):
    rows, cols, width = tok_ref.shape
    side = lax.broadcasted_iota(jnp.int32, (rows + 2 * WIN, BLOCK, 2 * width), 1)
    kvs = (nkv_ref, kv_ref, skv_ref)

    def tile(at):
        return jnp.concatenate([r[:, at : at + BLOCK, :] for r in kvs], axis=0)

    wkv = key_values(west_ref[...].astype(F32), mod_ref, w_ref)
    ekv = key_values(east_ref[...].astype(F32), mod_ref, w_ref)
    first = jnp.concatenate([jnp.where(side < WIN, wkv, tile(0)), tile(BLOCK)], axis=1)
    last = jnp.concatenate([tile(cols - BLOCK), jnp.where(side >= WIN, ekv, tile(cols))], axis=1)
    tok = tok_ref[...].astype(F32)
    low = attend(q_ref, first, bias_ref, outw_ref, 0)
    high = attend(q_ref, last, bias_ref, outw_ref, cols // BLOCK - 1)
    proj = jnp.concatenate([low, res_ref[:, BLOCK : cols - BLOCK, :], high], axis=1)
    res = (proj + tok).astype(BF)
    skip_ref[...] = res
    copy_skip = pltpu.make_async_copy(skip_ref, skip_hbm, sem)
    copy_skip.start()
    for k in range(width // 128):
        lane_ref[k] = res[:, :, k * 128 : (k + 1) * 128].astype(F32)

    groups = []
    for a in range(2):
        for b in range(2):
            parts = []
            for dr in range(2):
                for dc in range(2):
                    r, c = 2 * a + dr, 2 * b + dc
                    for k in range(width // 128):
                        strips = [
                            lane_ref[k, rr, pl.ds(c, cols // 4, stride=4), :]
                            for rr in range(r, rows, 4)
                        ]
                        parts.append(jnp.concatenate(strips, axis=0))
            groups.append(jnp.concatenate(parts, axis=1))
    count = (rows // 4) * (cols // 4)
    mid = mm(jnp.concatenate(groups, axis=0).astype(BF), one_ref[...]).astype(BF)
    mid = jnp.concatenate([mid[g * count : (g + 1) * count] for g in range(4)], axis=1)
    cin_ref[...] = mm(mid, two_ref[...]).astype(BF)
    copy_skip.wait()


def halves(low, high, swap_low):
    lane = lax.broadcasted_iota(jnp.int32, low.shape, 1)
    if swap_low:
        return jnp.where(lane < HD, pltpu.roll(low, HD, 1), high)
    return jnp.where(lane < HD, low, pltpu.roll(high, HD, 1))


def qkv_kernel(groups, zi_ref, mod_ref, *refs):
    xs, w_ref, out_refs = refs[: -1 - groups], refs[-1 - groups], refs[-groups:]
    x = jnp.concatenate([r[...] for r in xs], axis=0)
    at = mod_ref.shape[1] - 2 * x.shape[1]
    scale, shift = mod_ref[:, at : at + x.shape[1]], mod_ref[:, at + x.shape[1] :]
    y = mm(layer_norm(x.astype(F32), scale, shift), w_ref[...])
    half = x.shape[0] // 2
    zi = zi_ref[0]
    pieces = []
    for h in range(groups):
        kv = y[:, h * 2 * HD : (h + 1) * 2 * HD]
        if groups % 2:
            q = y[:, groups * 2 * HD + h * HD : groups * 2 * HD + (h + 1) * HD]
            qp = jnp.concatenate([q[:half], q[half:]], axis=1)
        else:
            at = groups * 2 * HD + (h // 2) * 2 * HD
            pair = y[:, at : at + 2 * HD]
            qp = halves(pair[:half], pair[half:], h % 2 == 1)
        pieces.append(jnp.concatenate([kv, qp * (1.0 / math.sqrt(HD))], axis=0).astype(BF))
    for g in range(groups):
        for h in range(groups):

            @pl.when(zi == g ^ h)
            def _(g=g, h=h):
                out_refs[g][...] = pieces[h]


def queries(own):
    band = own[0].shape[0] * 2 // 3
    half = band // 2
    lane = lax.broadcasted_iota(jnp.int32, (half, 2 * HD), 1)
    qs = []
    for r in own:
        qp = r[band:, :].astype(F32)
        qs.append(jnp.where(lane < HD, qp, 0.0))
        qs.append(jnp.where(lane < HD, pltpu.roll(qp, HD, 1), 0.0))
    return jnp.concatenate(qs, axis=0).astype(BF)


def near_kernel(groups, *refs):
    own, (acc_ref, max_ref) = refs[:groups], refs[groups:]
    band = own[0].shape[0] * 2 // 3
    kv = jnp.concatenate([r[:band, :] for r in own], axis=0)
    s = mm_t(queries(own), kv)
    top = jnp.max(s, axis=1, keepdims=True)
    p = jnp.exp(s - top)
    o = mm(p.astype(BF), kv)
    lane = lax.broadcasted_iota(jnp.int32, o.shape, 1)
    acc_ref[...] = jnp.where(lane < HD, jnp.sum(p, axis=1, keepdims=True), o)
    max_ref[...] = jnp.broadcast_to(top, max_ref.shape)


def far_kernel(groups, *refs):
    own, others = refs[:groups], refs[groups : -2 - groups]
    (acc_ref, max_ref), out_refs = refs[-2 - groups : -groups], refs[-groups:]
    kv = jnp.concatenate([r[...] for r in others], axis=0)
    s = mm_t(queries(own), kv)
    before = max_ref[...]
    top = jnp.maximum(before[:, :1], jnp.max(s, axis=1, keepdims=True))
    p = jnp.exp(s - top)
    o = mm(p.astype(BF), kv)
    lane = lax.broadcasted_iota(jnp.int32, o.shape, 1)
    new = jnp.where(lane < HD, jnp.sum(p, axis=1, keepdims=True), o)
    acc = acc_ref[...] * jnp.exp(before - top) + new
    o = acc / jnp.where(lane < HD, 1.0, pltpu.roll(acc, HD, 1))
    half = o.shape[0] // (2 * groups)
    for g in range(groups):
        low, high = o[2 * g * half : (2 * g + 1) * half], o[(2 * g + 1) * half : (2 * g + 2) * half]
        out_refs[g][...] = halves(low, high, True).astype(BF)


def project_kernel(groups, parts, zi_ref, *refs):
    pieces, w_ref, out_refs = refs[:groups], refs[groups], refs[groups + 1 :]
    zi = zi_ref[0]
    if groups % 2:
        acc = None
        for g in range(groups):
            w = w_ref[pl.ds(pl.multiple_of((zi ^ g) * HD, HD), HD), :]
            x = pieces[g][...].astype(F32)
            y = mm(jnp.concatenate([x[:, :HD], x[:, HD:]], axis=0).astype(BF), w)
            acc = y if acc is None else acc + y
    else:
        cols, ws = [], []
        for g in range(0, groups, 2):
            x0, x1 = pieces[g][...].astype(F32), pieces[g + 1][...].astype(F32)
            cols.append(jnp.concatenate([halves(x0, x1, False), halves(x0, x1, True)], axis=0))
        for g in range(groups):
            ws.append(w_ref[pl.ds(pl.multiple_of((zi ^ g) * HD, HD), HD), :])
        acc = mm(jnp.concatenate(cols, axis=1).astype(BF), jnp.concatenate(ws, axis=0))
    count = acc.shape[0] // parts
    for k in range(parts):
        out_refs[k][...] = acc[k * count : (k + 1) * count].astype(BF)


def sum_kernel(*refs):
    cin_ref, parts, out_ref = refs[0], refs[1:-1], refs[-1]
    total = parts[0][...].astype(F32)
    for r in parts[1:]:
        total = total + r[...].astype(F32)
    out_ref[...] = (cin_ref[...].astype(F32) + total).astype(BF).reshape(out_ref.shape)


def call(kernel, out, in_specs, scratch=(), out_specs=None, limit=12, flops=None, name=None):
    cost = flops and pl.CostEstimate(flops=flops, bytes_accessed=MIB, transcendentals=0)
    return pl.pallas_call(
        kernel,
        out_shape=out,
        in_specs=in_specs,
        out_specs=[VM for _ in out] if out_specs is None else out_specs,
        scratch_shapes=list(scratch),
        compiler_params=pltpu.CompilerParams(vmem_limit_bytes=limit * MIB),
        cost_estimate=cost,
        name=name,
    )


def swap(x, axis, step):
    size = lax.axis_size(axis)
    return lax.ppermute(x, axis, [(i, i ^ step) for i in range(size)])


def body(
    tokens,
    timestep,
    mod_weight,
    fine_qkv_weight,
    fine_out_weight,
    merge_one,
    merge_two,
    coarse_qkv_weight,
    coarse_out_weight,
):
    S = jax.ShapeDtypeStruct
    rows, cols, width = tokens.shape
    cw = merge_two.shape[1]
    no, ni = lax.axis_size("outer"), lax.axis_size("inner")
    oi = lax.axis_index("outer")
    odd = oi % 2 == 1
    bottom, top = tokens[rows - WIN :], tokens[:WIN]
    pairs = [(i, i + 1) for i in range(1, no - 1, 2)]
    pairs += [(j, i) for i, j in pairs]
    far = lax.ppermute(jnp.where(odd, bottom, top), "outer", pairs)
    near = swap(jnp.where(odd, top, bottom), "outer", 1)

    emb = embed(timestep, mod_weight.shape[0])
    mod = mm(emb, mod_weight)
    limits = jnp.stack(
        [jnp.where(oi == 0, WIN, 0), jnp.where(oi == no - 1, rows + WIN, rows + 2 * WIN), oi % 2]
    ).astype(jnp.int32)
    tall = rows + 2 * WIN
    heads = width // HD
    q, kv, bias, kvw, outw = call(
        own_kernel,
        [
            S((rows, cols, width), F32),
            S((rows, cols + BLOCK, 2 * width), F32),
            S((heads * rows * BLOCK, tall * SPAN), F32),
            S((width, 2 * width), BF),
            S((width, width), BF),
        ],
        [SM, VM, VM, VM, VM],
        limit=16,
        flops=1000000000,
        name="own",
    )(limits, mod, tokens, fine_qkv_weight, fine_out_weight)

    strip = S((tall, BLOCK, width), BF)
    right, left = call(columns_kernel, [strip] * 2, [SM] + [VM] * 3, name="columns")(
        limits, far, near, tokens
    )
    west = lax.ppermute(right, "inner", [(i, (i + 1) % ni) for i in range(ni)])
    east = lax.ppermute(left, "inner", [((i + 1) % ni, i) for i in range(ni)])
    nkv, skv, res = call(
        inner_kernel,
        [S((WIN, cols + BLOCK, 2 * width), F32)] * 2 + [S((rows, cols, width), F32)],
        [SM] + [VM] * 8,
        limit=16,
        flops=1000000000,
        name="inside",
    )(limits, mod, far, near, kvw, outw, q, kv, bias)
    count = (rows // 4) * (cols // 4)
    fine_skip, coarse_in = call(
        edge_kernel,
        [S(tokens.shape, BF), S((count, cw), BF)],
        [VM] * 14,
        scratch=[
            pltpu.VMEM((rows, cols, width), BF),
            pltpu.VMEM((width // 128, rows, cols, 128), F32),
            pltpu.SemaphoreType.DMA,
        ],
        out_specs=[HB, VM],
        limit=20,
        name="edge",
    )(
        mod, west, east, tokens, kvw, outw, q, kv, bias, nkv, skv, res, merge_one, merge_two
    )

    groups = coarse_qkv_weight.shape[1] // (3 * HD)
    sub = no // groups
    zi = (oi // sub).astype(jnp.int32)[None]
    band = ni * count
    gathered = [coarse_in] + [swap(coarse_in, "inner", k) for k in range(1, ni)]
    order, keep = call(
        order_kernel,
        [S(coarse_qkv_weight.shape, BF), S(coarse_in.shape, BF)],
        [VM, VM],
        flops=1000000000,
        name="order",
    )(coarse_in, coarse_qkv_weight)
    pieces = call(
        lambda *r: qkv_kernel(groups, *r),
        [S((band + band // 2, 2 * HD), BF)] * groups,
        [SM] + [VM] * (ni + 2),
        name="qkv",
    )(zi, mod, *gathered, order)
    own = [pieces[0]] + [swap(pieces[g], "outer", g * sub) for g in range(1, groups)]
    others = [swap(p[:band], "outer", s) for s in range(1, sub) for p in own]
    acc, top = call(
        lambda *r: near_kernel(groups, *r),
        [S((groups * band, 2 * HD), F32)] * 2,
        [VM] * groups,
        limit=16,
        flops=1000000000,
        name="near",
    )(*own)
    att = call(
        lambda *r: far_kernel(groups, *r),
        [S((band // 2, 2 * HD), BF)] * groups,
        [VM] * (groups + len(others) + 2),
        limit=16 if len(others) * band <= 1024 else 56,
        name="far",
    )(*own, *others, acc, top)
    back = [att[0]] + [swap(att[g], "outer", g * sub) for g in range(1, groups)]
    proj = call(
        lambda *r: project_kernel(groups, ni, *r),
        [S((count, cw), BF)] * ni,
        [SM] + [VM] * (groups + 1),
        name="project",
    )(zi, *back, coarse_out_weight)
    parts = [proj[0]] + [swap(proj[k], "inner", k) for k in range(1, ni)]
    (coarse_out,) = call(
        sum_kernel, [S((rows // 4, cols // 4, cw), BF)], [VM] * (ni + 1), name="sum"
    )(keep, *parts)
    return (fine_skip, coarse_out)


def solution(mesh):
    return jax.shard_map(
        body,
        mesh=mesh,
        in_specs=(
            P("outer", "inner", None),
            P(),
            P(),
            P(),
            P(),
            P(),
            P(),
            P(None, "inner"),
            P("inner", None),
        ),
        out_specs=(P("outer", "inner", None), P("outer", "inner", None)),
        check_vma=False,
    )
```

```python
import math

import jax
import jax.numpy as jnp
from jax import lax
from jax.experimental import pallas as pl
from jax.experimental.pallas import tpu as pltpu
from jax.sharding import PartitionSpec as P

HD = 64
WIN = 3
BLOCK = 8
SPAN = 16
STAGE = 6
BF = jnp.bfloat16
F32 = jnp.float32
VM = pl.BlockSpec(memory_space=pltpu.VMEM)
HB = pl.BlockSpec(memory_space=pl.ANY)
HM = pl.BlockSpec(memory_space=pltpu.HBM)
MIB = 1024 * 1024
OUTER = ("head", "sub")


def embed(timestep, width):
    half = width // 2
    freq = jnp.exp(-math.log(10000.0) * jnp.arange(half, dtype=F32) / half)
    angle = timestep.astype(F32)[0] * freq
    return jnp.concatenate([jnp.cos(angle), jnp.sin(angle)]).astype(BF)[None, :]


def layer_norm(x, scale, shift):
    mean = jnp.mean(x, axis=-1, keepdims=True)
    var = jnp.mean((x - mean) * (x - mean), axis=-1, keepdims=True)
    return ((x - mean) * lax.rsqrt(var + 1e-06) * (1.0 + scale) + shift).astype(BF)


def mm(a, b):
    return jnp.dot(a, b, preferred_element_type=F32)


def mm_t(a, b):
    return lax.dot_general(a, b, (((1,), (1,)), ((), ())), preferred_element_type=F32)


def shifted(x):
    rows, cols, width = x.shape
    left = jnp.zeros((rows, WIN, width), F32)
    right = jnp.zeros((rows, BLOCK - WIN, width), F32)
    return jnp.concatenate([left, x, right], axis=1)


def key_values(x, mod_ref, w_ref):
    rows, cols, width = x.shape
    flat = x.reshape(rows * cols, width)
    n = layer_norm(flat, mod_ref[:, :width], mod_ref[:, width : 2 * width])
    return mm(n, w_ref[...]).reshape(rows, cols, 2 * width)


def place(axes):
    at = 0
    for axis in axes:
        at = at * lax.axis_size(axis) + lax.axis_index(axis)
    return at


def sides(far_ref, near_ref):
    odd = jnp.broadcast_to(place(OUTER) % 2, far_ref.shape) == 1
    far, near = far_ref[...].astype(F32), near_ref[...].astype(F32)
    return jnp.where(odd, near, far), jnp.where(odd, far, near)


def columns_kernel(far_ref, near_ref, tok_ref, right_ref, left_ref):
    cols, width = tok_ref.shape[1:]
    for out_ref, at in ((right_ref, cols - 2 * BLOCK), (left_ref, 0)):
        chunk = pl.ds(at, 2 * BLOCK)
        north, south = sides(far_ref.at[:, chunk], near_ref.at[:, chunk])
        x = jnp.concatenate([north, tok_ref[:, chunk].astype(F32), south], axis=0)
        zero = jnp.zeros((x.shape[0], BLOCK, width), F32)
        if at:
            x = jnp.concatenate([x[:, 2 * BLOCK - WIN :], zero[:, WIN:]], axis=1)
        else:
            x = jnp.concatenate([zero[:, :WIN], x[:, :WIN], zero[:, 2 * WIN :]], axis=1)
        out_ref[...] = x.astype(BF)


def own_kernel(
    mod_ref, tok_ref, w_ref, out_ref, q_ref, kv_ref, bias_ref, kvw_ref, outw_ref
):
    kvw_ref[...] = w_ref[:, tok_ref.shape[2] :]
    outw_ref[...] = out_ref[...]
    rows, cols, width = tok_ref.shape
    tok = tok_ref[...].astype(F32)
    fscale, fshift = mod_ref[:, :width], mod_ref[:, width : 2 * width]
    n = layer_norm(tok.reshape(rows * cols, width), fscale, fshift)
    q = mm(n, w_ref[:, :width]).astype(BF).astype(F32) * (1.0 / math.sqrt(HD))
    q_ref[...] = q.reshape(rows, cols, width)
    kv_ref[...] = key_values(shifted(tok), mod_ref, kvw_ref)

    nq, nk = bias_ref.shape
    per = rows * BLOCK
    band, bands = place(OUTER), lax.axis_size(OUTER)
    lo = jnp.where(band == 0, WIN, 0)
    hi = jnp.where(band == bands - 1, rows + WIN, rows + 2 * WIN)
    qi = lax.broadcasted_iota(jnp.int32, (nq, nk), 0) % per
    ki = lax.broadcasted_iota(jnp.int32, (nq, nk), 1)
    kr, kc = ki // SPAN, ki % SPAN
    dr, dc = kr - qi // BLOCK, kc - qi % BLOCK
    ok = (dr >= 0) & (dr <= 2 * WIN) & (dc >= 0) & (dc <= 2 * WIN) & (kr >= lo) & (kr < hi)
    bias_ref[...] = jnp.where(ok, 0.0, -1e30).astype(F32)


def order_kernel(cin_ref, skip_ref, cw_ref, order_ref, keep_ref, skip_hbm, sem):
    copy_skip = pltpu.make_async_copy(skip_ref, skip_hbm, sem)
    copy_skip.start()
    keep_ref[...] = cin_ref[...]
    groups = cw_ref.shape[1] // (3 * HD)
    kvs, qs = [], []
    for h in range(groups):
        qs.append(cw_ref[:, h * 3 * HD : h * 3 * HD + HD].astype(F32))
        kvs.append(cw_ref[:, h * 3 * HD + HD : (h + 1) * 3 * HD].astype(F32))
    order_ref[...] = jnp.concatenate(kvs + qs, axis=1).astype(BF)
    copy_skip.wait()


def attend(q_ref, wins, bias_ref, outw_ref, blocks):
    rows, cols, width = q_ref.shape
    heads, nq = width // HD, rows * BLOCK
    lane_head = lax.broadcasted_iota(jnp.int32, (nq, width), 1) // HD
    kvs, scores = [], []
    for j, win in zip(blocks, wins):
        qb = q_ref[:, j * BLOCK : (j + 1) * BLOCK, :].reshape(nq, width)
        qs = jnp.concatenate([jnp.where(lane_head == h, qb, 0.0) for h in range(heads)], axis=0)
        kvs.append(win.reshape(win.shape[0] * SPAN, 2 * width).astype(BF))
        scores.append(mm_t(qs.astype(BF), kvs[-1][:, :width]) + bias_ref[...])
    ps = [jnp.exp(s - jnp.max(s, axis=1, keepdims=True)) for s in scores]
    outs = [mm(p.astype(BF), kv[:, width:]) for p, kv in zip(ps, kvs)]
    atts = []
    for p, o in zip(ps, outs):
        o = o / jnp.sum(p, axis=1, keepdims=True)
        att = o[:nq]
        for h in range(1, heads):
            att = jnp.where(lane_head == h, o[h * nq : (h + 1) * nq], att)
        atts.append(att.astype(BF))
    proj = mm(jnp.concatenate(atts, axis=0), outw_ref[...])
    return [proj[i * nq : (i + 1) * nq].reshape(rows, BLOCK, width) for i in range(len(atts))]


def inner_kernel(
    mod_ref,
    far_ref,
    near_ref,
    w_ref,
    outw_ref,
    q_ref,
    kv_ref,
    bias_ref,
    nkv_ref,
    skv_ref,
    res_ref,
):
    north, south = sides(far_ref, near_ref)
    nkv_ref[...] = key_values(shifted(north), mod_ref, w_ref)
    skv_ref[...] = key_values(shifted(south), mod_ref, w_ref)
    cols = q_ref.shape[1]
    for lead in range(1, cols // BLOCK - 1, STAGE):
        blocks = range(lead, min(lead + STAGE, cols // BLOCK - 1))
        wins = [
            jnp.concatenate(
                [r[:, j * BLOCK : j * BLOCK + SPAN, :] for r in (nkv_ref, kv_ref, skv_ref)], axis=0
            )
            for j in blocks
        ]
        for j, proj in zip(blocks, attend(q_ref, wins, bias_ref, outw_ref, blocks)):
            res_ref[:, j * BLOCK : (j + 1) * BLOCK, :] = proj


def edge_kernel(
    mod_ref,
    west_ref,
    east_ref,
    tok_ref,
    w_ref,
    outw_ref,
    q_ref,
    kv_ref,
    bias_ref,
    nkv_ref,
    skv_ref,
    res_ref,
    one_ref,
    two_ref,
    skip_ref,
    cin_ref,
    lane_ref,
):
    rows, cols, width = tok_ref.shape
    side = lax.broadcasted_iota(jnp.int32, (rows + 2 * WIN, BLOCK, 2 * width), 1)
    kvs = (nkv_ref, kv_ref, skv_ref)

    def tile(at):
        return jnp.concatenate([r[:, at : at + BLOCK, :] for r in kvs], axis=0)

    wkv = key_values(west_ref[...].astype(F32), mod_ref, w_ref)
    ekv = key_values(east_ref[...].astype(F32), mod_ref, w_ref)
    first = jnp.concatenate([jnp.where(side < WIN, wkv, tile(0)), tile(BLOCK)], axis=1)
    last = jnp.concatenate([tile(cols - BLOCK), jnp.where(side >= WIN, ekv, tile(cols))], axis=1)
    tok = tok_ref[...].astype(F32)
    ends = (0, cols // BLOCK - 1)
    low, high = attend(q_ref, [first, last], bias_ref, outw_ref, ends)
    proj = jnp.concatenate([low, res_ref[:, BLOCK : cols - BLOCK, :], high], axis=1)
    res = (proj + tok).astype(BF)
    skip_ref[...] = res
    for k in range(width // 128):
        lane_ref[k] = res[:, :, k * 128 : (k + 1) * 128].astype(F32)

    groups = []
    for a in range(2):
        for b in range(2):
            parts = []
            for dr in range(2):
                for dc in range(2):
                    r, c = 2 * a + dr, 2 * b + dc
                    for k in range(width // 128):
                        strips = [
                            lane_ref[k, rr, pl.ds(c, cols // 4, stride=4), :]
                            for rr in range(r, rows, 4)
                        ]
                        parts.append(jnp.concatenate(strips, axis=0))
            groups.append(jnp.concatenate(parts, axis=1))
    count = (rows // 4) * (cols // 4)
    mid = mm(jnp.concatenate(groups, axis=0).astype(BF), one_ref[...]).astype(BF)
    mid = jnp.concatenate([mid[g * count : (g + 1) * count] for g in range(4)], axis=1)
    cin_ref[...] = mm(mid, two_ref[...]).astype(BF)


def halves(low, high, swap_low):
    lane = lax.broadcasted_iota(jnp.int32, low.shape, 1)
    if swap_low:
        return jnp.where(lane < HD, pltpu.roll(low, HD, 1), high)
    return jnp.where(lane < HD, low, pltpu.roll(high, HD, 1))


def qkv_kernel(groups, mod_ref, *refs):
    xs, w_ref, out_refs = refs[: -1 - groups], refs[-1 - groups], refs[-groups:]
    x = jnp.concatenate([r[...] for r in xs], axis=0)
    at = mod_ref.shape[1] - 2 * x.shape[1]
    scale, shift = mod_ref[:, at : at + x.shape[1]], mod_ref[:, at + x.shape[1] :]
    y = mm(layer_norm(x.astype(F32), scale, shift), w_ref[...])
    half = x.shape[0] // 2
    zi = lax.axis_index("head")
    pieces = []
    for h in range(groups):
        kv = y[:, h * 2 * HD : (h + 1) * 2 * HD]
        if groups % 2:
            q = y[:, groups * 2 * HD + h * HD : groups * 2 * HD + (h + 1) * HD]
            qp = jnp.concatenate([q[:half], q[half:]], axis=1)
        else:
            at = groups * 2 * HD + (h // 2) * 2 * HD
            pair = y[:, at : at + 2 * HD]
            qp = halves(pair[:half], pair[half:], h % 2 == 1)
        pieces.append(jnp.concatenate([kv, qp * (1.0 / math.sqrt(HD))], axis=0).astype(BF))
    for g in range(groups):
        for h in range(groups):

            @pl.when(zi == g ^ h)
            def _(g=g, h=h):
                out_refs[g][...] = pieces[h]


def queries(own):
    band = own[0].shape[0] * 2 // 3
    half = band // 2
    lane = lax.broadcasted_iota(jnp.int32, (half, 2 * HD), 1)
    qs = []
    for r in own:
        qp = r[band:, :].astype(F32)
        qs.append(jnp.where(lane < HD, qp, 0.0))
        qs.append(jnp.where(lane < HD, pltpu.roll(qp, HD, 1), 0.0))
    return jnp.concatenate(qs, axis=0).astype(BF)


def near_kernel(groups, *refs):
    own, (acc_ref, max_ref) = refs[:groups], refs[groups:]
    band = own[0].shape[0] * 2 // 3
    kv = jnp.concatenate([r[:band, :] for r in own], axis=0)
    s = mm_t(queries(own), kv)
    top = jnp.max(s, axis=1, keepdims=True)
    p = jnp.exp(s - top)
    o = mm(p.astype(BF), kv)
    lane = lax.broadcasted_iota(jnp.int32, o.shape, 1)
    acc_ref[...] = jnp.where(lane < HD, jnp.sum(p, axis=1, keepdims=True), o)
    max_ref[...] = jnp.broadcast_to(top, max_ref.shape)


def far_kernel(groups, parts, *refs):
    own, others = refs[:groups], refs[groups:-3]
    acc_ref, max_ref, out_ref = refs[-3:]
    kv = jnp.concatenate([r[...] for r in others], axis=0)
    s = mm_t(queries(own), kv)
    before = max_ref[...]
    top = jnp.maximum(before[:, :1], jnp.max(s, axis=1, keepdims=True))
    p = jnp.exp(s - top)
    o = mm(p.astype(BF), kv)
    lane = lax.broadcasted_iota(jnp.int32, o.shape, 1)
    new = jnp.where(lane < HD, jnp.sum(p, axis=1, keepdims=True), o)
    acc = acc_ref[...] * jnp.exp(before - top) + new
    o = acc / jnp.where(lane < HD, 1.0, pltpu.roll(acc, HD, 1))
    count = o.shape[0] // (groups * parts)
    zi, ii = lax.axis_index("head"), lax.axis_index("inner")
    for g in range(groups):
        for k in range(parts):
            at = (g * parts + k) * count
            block = halves(o[at : at + count // 2], o[at + count // 2 : at + count], True)
            out_ref[(zi ^ g) * parts + (ii ^ k)] = block.astype(BF)


def project_kernel(groups, parts, cin_ref, att_ref, *refs):
    ws, out_ref = refs[:-1], refs[-1]
    ii = lax.axis_index("inner")
    total = cin_ref[...].astype(F32)
    for k in range(parts):
        xs = [att_ref[g * parts + (ii ^ k)].astype(F32) for g in range(groups)]
        if groups % 2:
            cols = [jnp.concatenate([x[:, :HD], x[:, HD:]], axis=0) for x in xs]
        else:
            cols = [
                jnp.concatenate([halves(a, b, False), halves(a, b, True)], axis=0)
                for a, b in zip(xs[::2], xs[1::2])
            ]
        total = total + mm(jnp.concatenate(cols, axis=1).astype(BF), ws[k][...])
    out_ref[...] = total.astype(BF).reshape(out_ref.shape)


def call(kernel, out, in_specs, scratch=(), out_specs=None, limit=12, flops=None, name=None):
    cost = flops and pl.CostEstimate(flops=flops, bytes_accessed=MIB, transcendentals=0)
    return pl.pallas_call(
        kernel,
        out_shape=out,
        in_specs=in_specs,
        out_specs=[VM for _ in out] if out_specs is None else out_specs,
        scratch_shapes=list(scratch),
        compiler_params=pltpu.CompilerParams(vmem_limit_bytes=limit * MIB),
        cost_estimate=cost,
        name=name,
    )


def swap(x, axis, step):
    size = lax.axis_size(axis)
    return lax.ppermute(x, axis, [(i, i ^ step) for i in range(size)])


def body(
    tokens,
    timestep,
    mod_weight,
    fine_qkv_weight,
    fine_out_weight,
    merge_one,
    merge_two,
    coarse_qkv_weight,
    coarse_out_weight,
):
    S = jax.ShapeDtypeStruct
    rows, cols, width = tokens.shape
    cw = merge_two.shape[1]
    no, ni = lax.axis_size(OUTER), lax.axis_size("inner")
    odd = lax.axis_index(OUTER) % 2 == 1
    bottom, top = tokens[rows - WIN :], tokens[:WIN]
    pairs = [(i, i + 1) for i in range(1, no - 1, 2)]
    pairs += [(j, i) for i, j in pairs]
    far = lax.ppermute(jnp.where(odd, bottom, top), OUTER, pairs)
    near = swap(jnp.where(odd, top, bottom), OUTER, 1)

    emb = embed(timestep, mod_weight.shape[0])
    mod = mm(emb, mod_weight)
    tall = rows + 2 * WIN
    heads = width // HD
    q, kv, bias, kvw, outw = call(
        own_kernel,
        [
            S((rows, cols, width), F32),
            S((rows, cols + BLOCK, 2 * width), F32),
            S((heads * rows * BLOCK, tall * SPAN), F32),
            S((width, 2 * width), BF),
            S((width, width), BF),
        ],
        [VM] * 4,
        limit=16,
        flops=1000000000,
        name="own",
    )(mod, tokens, fine_qkv_weight, fine_out_weight)

    strip = S((tall, BLOCK, width), BF)
    right, left = call(columns_kernel, [strip] * 2, [VM] * 3, name="columns")(
        far, near, tokens
    )
    west = lax.ppermute(right, "inner", [(i, (i + 1) % ni) for i in range(ni)])
    east = lax.ppermute(left, "inner", [((i + 1) % ni, i) for i in range(ni)])
    nkv, skv, res = call(
        inner_kernel,
        [S((WIN, cols + BLOCK, 2 * width), F32)] * 2 + [S((rows, cols, width), F32)],
        [VM] * 8,
        limit=16,
        flops=1000000000,
        name="inside",
    )(mod, far, near, kvw, outw, q, kv, bias)
    count = (rows // 4) * (cols // 4)
    skip, coarse_in = call(
        edge_kernel,
        [S(tokens.shape, BF), S((count, cw), BF)],
        [VM] * 14,
        scratch=[
            pltpu.VMEM((width // 128, rows, cols, 128), F32),
        ],
        limit=20,
        name="edge",
    )(
        mod, west, east, tokens, kvw, outw, q, kv, bias, nkv, skv, res, merge_one, merge_two
    )

    groups = coarse_qkv_weight.shape[1] // (3 * HD)
    sub = no // groups
    band = ni * count
    gathered = [coarse_in] + [swap(coarse_in, "inner", k) for k in range(1, ni)]
    order, keep, fine_skip = call(
        order_kernel,
        [S(coarse_qkv_weight.shape, BF), S(coarse_in.shape, BF), S(tokens.shape, BF)],
        [VM] * 3,
        scratch=[pltpu.SemaphoreType.DMA],
        out_specs=[VM, VM, HB],
        flops=1000000000,
        name="order",
    )(coarse_in, skip, coarse_qkv_weight)
    pieces = call(
        lambda *r: qkv_kernel(groups, *r),
        [S((band + band // 2, 2 * HD), BF)] * groups,
        [VM] * (ni + 2),
        name="qkv",
    )(mod, *gathered, order)
    weight, unused = lax.optimization_barrier((coarse_out_weight, pieces[0]))
    step = ni // 2
    whole = [weight, swap(weight, "inner", step)]
    own = [pieces[0]] + [swap(pieces[g], OUTER, g * sub) for g in range(1, groups)]
    others = [swap(p[:band], OUTER, s) for s in range(1, sub) for p in own]
    acc, top = call(
        lambda *r: near_kernel(groups, *r),
        [S((groups * band, 2 * HD), F32)] * 2,
        [VM] * groups,
        limit=16,
        flops=1000000000,
        name="near",
    )(*own)
    att = call(
        lambda *r: far_kernel(groups, ni, *r),
        [S((groups * ni, count // 2, 2 * HD), BF)],
        [VM] * (groups + len(others) + 2),
        limit=16 if len(others) * band <= 1024 else 56,
        name="far",
    )(*own, *others, acc, top)
    far_weight, att = lax.optimization_barrier((whole[1], att))
    whole[1] = far_weight
    while step > 1:
        step //= 2
        whole = [w for x in whole for w in (x, swap(x, "inner", step))]
    att = lax.all_to_all(att[0], ("head", "inner"), 0, 0, tiled=True)
    (coarse_out,) = call(
        lambda *r: project_kernel(groups, ni, *r),
        [S((rows // 4, cols // 4, cw), BF)],
        [VM] * (ni + 2),
        name="project",
    )(keep, att, *whole)
    return (fine_skip, coarse_out)


def solution(mesh):
    inner = mesh.shape["inner"]
    heads = 16 // inner
    devices = mesh.devices.reshape(heads, mesh.shape["outer"] // heads, inner)
    return jax.shard_map(
        body,
        mesh=jax.sharding.Mesh(devices, OUTER + ("inner",)),
        in_specs=(
            P(OUTER, "inner", None),
            P(),
            P(),
            P(),
            P(),
            P(),
            P(),
            P(None, "inner"),
            P("inner", None),
        ),
        out_specs=(P(OUTER, "inner", None), P(OUTER, "inner", None)),
        check_vma=False,
    )
```

```python
import math

import jax
import jax.numpy as jnp
from jax import lax
from jax.experimental import pallas as pl
from jax.experimental.pallas import tpu as pltpu
from jax.sharding import PartitionSpec as P

HD = 64
WIN = 3
BLOCK = 8
SPAN = 16
STAGE = 6
EARLY = 1
BF = jnp.bfloat16
F32 = jnp.float32
VM = pl.BlockSpec(memory_space=pltpu.VMEM)
HB = pl.BlockSpec(memory_space=pl.ANY)
HM = pl.BlockSpec(memory_space=pltpu.HBM)
MIB = 1024 * 1024
OUTER = ("head", "sub")


def embed(timestep, width):
    half = width // 2
    freq = jnp.exp(-math.log(10000.0) * jnp.arange(half, dtype=F32) / half)
    angle = timestep.astype(F32)[0] * freq
    return jnp.concatenate([jnp.cos(angle), jnp.sin(angle)]).astype(BF)[None, :]


def layer_norm(x, scale, shift):
    mean = jnp.mean(x, axis=-1, keepdims=True)
    var = jnp.mean((x - mean) * (x - mean), axis=-1, keepdims=True)
    return ((x - mean) * lax.rsqrt(var + 1e-06) * (1.0 + scale) + shift).astype(BF)


def mm(a, b):
    return jnp.dot(a, b, preferred_element_type=F32)


def mm_t(a, b):
    return lax.dot_general(a, b, (((1,), (1,)), ((), ())), preferred_element_type=F32)


def shifted(x):
    rows, cols, width = x.shape
    left = jnp.zeros((rows, WIN, width), F32)
    right = jnp.zeros((rows, BLOCK - WIN, width), F32)
    return jnp.concatenate([left, x, right], axis=1)


def key_values(x, mod_ref, w_ref):
    rows, cols, width = x.shape
    flat = x.reshape(rows * cols, width)
    n = layer_norm(flat, mod_ref[:, :width], mod_ref[:, width : 2 * width])
    return mm(n, w_ref[...]).reshape(rows, cols, 2 * width)


def place(axes):
    at = 0
    for axis in axes:
        at = at * lax.axis_size(axis) + lax.axis_index(axis)
    return at


def sides(far_ref, near_ref):
    odd = jnp.broadcast_to(place(OUTER) % 2, far_ref.shape) == 1
    far, near = far_ref[...].astype(F32), near_ref[...].astype(F32)
    return jnp.where(odd, near, far), jnp.where(odd, far, near)


def columns_kernel(far_ref, near_ref, tok_ref, right_ref, left_ref):
    cols, width = tok_ref.shape[1:]
    half = BLOCK // 2
    for out_ref, at, lead in ((right_ref, cols - 2 * BLOCK, 2 * BLOCK - WIN), (left_ref, 0, 0)):
        chunk = pl.ds(at, 2 * BLOCK)
        north, south = sides(far_ref.at[:, chunk], near_ref.at[:, chunk])
        x = jnp.concatenate([north, tok_ref[:, chunk].astype(F32), south], axis=0)
        x = jnp.concatenate([x[:, lead : lead + WIN], x[:, : half - WIN]], axis=1)
        x = jnp.concatenate([x[:, :, k : k + width // 2] for k in (0, width // 2)], axis=1)
        out_ref[...] = x.astype(BF)


def strip_columns(ref, lead):
    x = ref[...].astype(F32)
    half = BLOCK // 2
    x = jnp.concatenate([x[:, :half], x[:, half:]], axis=2)[:, :WIN]
    zero = jnp.zeros((x.shape[0], BLOCK, x.shape[2]), F32)
    parts = [zero[:, :lead]] * (lead > 0) + [x, zero[:, lead + WIN :]]
    return jnp.concatenate(parts, axis=1)


def own_kernel(
    mod_ref, tok_ref, w_ref, out_ref, q_ref, kv_ref, bias_ref, kvw_ref, outw_ref
):
    kvw_ref[...] = w_ref[:, tok_ref.shape[2] :]
    outw_ref[...] = out_ref[...]
    rows, cols, width = tok_ref.shape
    tok = tok_ref[...].astype(F32)
    fscale, fshift = mod_ref[:, :width], mod_ref[:, width : 2 * width]
    n = layer_norm(tok.reshape(rows * cols, width), fscale, fshift)
    q = mm(n, w_ref[:, :width]).astype(BF).astype(F32) * (1.0 / math.sqrt(HD))
    q_ref[...] = q.reshape(rows, cols, width)
    kv_ref[...] = key_values(shifted(tok), mod_ref, kvw_ref)

    nq, nk = bias_ref.shape
    per = rows * BLOCK
    band, bands = place(OUTER), lax.axis_size(OUTER)
    lo = jnp.where(band == 0, WIN, 0)
    hi = jnp.where(band == bands - 1, rows + WIN, rows + 2 * WIN)
    qi = lax.broadcasted_iota(jnp.int32, (nq, nk), 0) % per
    ki = lax.broadcasted_iota(jnp.int32, (nq, nk), 1)
    kr, kc = ki // SPAN, ki % SPAN
    dr, dc = kr - qi // BLOCK, kc - qi % BLOCK
    ok = (dr >= 0) & (dr <= 2 * WIN) & (dc >= 0) & (dc <= 2 * WIN) & (kr >= lo) & (kr < hi)
    bias_ref[...] = jnp.where(ok, 0.0, -1e30).astype(F32)


def order_kernel(cin_ref, skip_ref, cw_ref, order_ref, keep_ref, skip_hbm, sem):
    copy_skip = pltpu.make_async_copy(skip_ref, skip_hbm, sem)
    copy_skip.start()
    keep_ref[...] = cin_ref[...]
    groups = cw_ref.shape[1] // (3 * HD)
    kvs, qs = [], []
    for h in range(groups):
        qs.append(cw_ref[:, h * 3 * HD : h * 3 * HD + HD].astype(F32))
        kvs.append(cw_ref[:, h * 3 * HD + HD : (h + 1) * 3 * HD].astype(F32))
    order_ref[...] = jnp.concatenate(kvs + qs, axis=1).astype(BF)
    copy_skip.wait()


def attend(q_ref, wins, bias_ref, outw_ref, blocks):
    rows, cols, width = q_ref.shape
    heads, nq = width // HD, rows * BLOCK
    lane_head = lax.broadcasted_iota(jnp.int32, (nq, width), 1) // HD
    kvs, scores = [], []
    for j, win in zip(blocks, wins):
        qb = q_ref[:, j * BLOCK : (j + 1) * BLOCK, :].reshape(nq, width)
        qs = jnp.concatenate([jnp.where(lane_head == h, qb, 0.0) for h in range(heads)], axis=0)
        kvs.append(win.reshape(win.shape[0] * SPAN, 2 * width).astype(BF))
        scores.append(mm_t(qs.astype(BF), kvs[-1][:, :width]) + bias_ref[...])
    ps = [jnp.exp(s - jnp.max(s, axis=1, keepdims=True)) for s in scores]
    outs = [mm(p.astype(BF), kv[:, width:]) for p, kv in zip(ps, kvs)]
    atts = []
    for p, o in zip(ps, outs):
        o = o / jnp.sum(p, axis=1, keepdims=True)
        att = o[:nq]
        for h in range(1, heads):
            att = jnp.where(lane_head == h, o[h * nq : (h + 1) * nq], att)
        atts.append(att.astype(BF))
    proj = mm(jnp.concatenate(atts, axis=0), outw_ref[...])
    return [proj[i * nq : (i + 1) * nq].reshape(rows, BLOCK, width) for i in range(len(atts))]


def inner_kernel(
    mod_ref,
    far_ref,
    near_ref,
    w_ref,
    outw_ref,
    q_ref,
    kv_ref,
    bias_ref,
    nkv_ref,
    skv_ref,
    res_ref,
):
    north, south = sides(far_ref, near_ref)
    nkv_ref[...] = key_values(shifted(north), mod_ref, w_ref)
    skv_ref[...] = key_values(shifted(south), mod_ref, w_ref)
    cols = q_ref.shape[1]
    for lead in range(1, cols // BLOCK - 1, STAGE):
        blocks = range(lead, min(lead + STAGE, cols // BLOCK - 1))
        wins = [
            jnp.concatenate(
                [r[:, j * BLOCK : j * BLOCK + SPAN, :] for r in (nkv_ref, kv_ref, skv_ref)], axis=0
            )
            for j in blocks
        ]
        for j, proj in zip(blocks, attend(q_ref, wins, bias_ref, outw_ref, blocks)):
            res_ref[:, j * BLOCK : (j + 1) * BLOCK, :] = proj


def edge_kernel(
    mod_ref,
    west_ref,
    east_ref,
    tok_ref,
    w_ref,
    outw_ref,
    q_ref,
    kv_ref,
    bias_ref,
    nkv_ref,
    skv_ref,
    res_ref,
    one_ref,
    two_ref,
    skip_ref,
    cin_ref,
    lane_ref,
):
    rows, cols, width = tok_ref.shape
    side = lax.broadcasted_iota(jnp.int32, (rows + 2 * WIN, BLOCK, 2 * width), 1)
    kvs = (nkv_ref, kv_ref, skv_ref)

    def tile(at):
        return jnp.concatenate([r[:, at : at + BLOCK, :] for r in kvs], axis=0)

    strips = [strip_columns(west_ref, 0), strip_columns(east_ref, WIN)]
    strips = key_values(jnp.concatenate(strips, axis=0), mod_ref, w_ref)
    wkv, ekv = strips[: rows + 2 * WIN], strips[rows + 2 * WIN :]
    first = jnp.concatenate([jnp.where(side < WIN, wkv, tile(0)), tile(BLOCK)], axis=1)
    last = jnp.concatenate([tile(cols - BLOCK), jnp.where(side >= WIN, ekv, tile(cols))], axis=1)
    tok = tok_ref[...].astype(F32)
    ends = (0, cols // BLOCK - 1)
    low, high = attend(q_ref, [first, last], bias_ref, outw_ref, ends)
    proj = jnp.concatenate([low, res_ref[:, BLOCK : cols - BLOCK, :], high], axis=1)
    res = (proj + tok).astype(BF)
    skip_ref[...] = res
    for k in range(width // 128):
        lane_ref[k] = res[:, :, k * 128 : (k + 1) * 128].astype(F32)

    groups = []
    for a in range(2):
        for b in range(2):
            parts = []
            for dr in range(2):
                for dc in range(2):
                    r, c = 2 * a + dr, 2 * b + dc
                    for k in range(width // 128):
                        strips = [
                            lane_ref[k, rr, pl.ds(c, cols // 4, stride=4), :]
                            for rr in range(r, rows, 4)
                        ]
                        parts.append(jnp.concatenate(strips, axis=0))
            groups.append(jnp.concatenate(parts, axis=1))
    count = (rows // 4) * (cols // 4)
    mid = mm(jnp.concatenate(groups, axis=0).astype(BF), one_ref[...]).astype(BF)
    mid = jnp.concatenate([mid[g * count : (g + 1) * count] for g in range(4)], axis=1)
    cin_ref[...] = mm(mid, two_ref[...]).astype(BF)


def halves(low, high, swap_low):
    lane = lax.broadcasted_iota(jnp.int32, low.shape, 1)
    if swap_low:
        return jnp.where(lane < HD, pltpu.roll(low, HD, 1), high)
    return jnp.where(lane < HD, low, pltpu.roll(high, HD, 1))


def qkv_kernel(groups, mod_ref, *refs):
    xs, w_ref, out_refs = refs[: -1 - groups], refs[-1 - groups], refs[-groups:]
    x = jnp.concatenate([r[...] for r in xs], axis=0)
    at = mod_ref.shape[1] - 2 * x.shape[1]
    scale, shift = mod_ref[:, at : at + x.shape[1]], mod_ref[:, at + x.shape[1] :]
    y = mm(layer_norm(x.astype(F32), scale, shift), w_ref[...])
    half = x.shape[0] // 2
    zi = lax.axis_index("head")
    pieces = []
    for h in range(groups):
        kv = y[:, h * 2 * HD : (h + 1) * 2 * HD]
        if groups % 2:
            q = y[:, groups * 2 * HD + h * HD : groups * 2 * HD + (h + 1) * HD]
            qp = jnp.concatenate([q[:half], q[half:]], axis=1)
        else:
            at = groups * 2 * HD + (h // 2) * 2 * HD
            pair = y[:, at : at + 2 * HD]
            qp = halves(pair[:half], pair[half:], h % 2 == 1)
        pieces.append(jnp.concatenate([kv, qp * (1.0 / math.sqrt(HD))], axis=0).astype(BF))
    for g in range(groups):
        for h in range(groups):

            @pl.when(zi == g ^ h)
            def _(g=g, h=h):
                out_refs[g][...] = pieces[h]


def queries(own):
    band = own[0].shape[0] * 2 // 3
    half = band // 2
    lane = lax.broadcasted_iota(jnp.int32, (half, 2 * HD), 1)
    qs = []
    for r in own:
        qp = r[band:, :].astype(F32)
        qs.append(jnp.where(lane < HD, qp, 0.0))
        qs.append(jnp.where(lane < HD, pltpu.roll(qp, HD, 1), 0.0))
    return jnp.concatenate(qs, axis=0).astype(BF)


def near_kernel(groups, *refs):
    own, others, (acc_ref, max_ref) = refs[:groups], refs[groups:-2], refs[-2:]
    band = own[0].shape[0] * 2 // 3
    kv = jnp.concatenate([r[:band, :] for r in own] + [r[...] for r in others], axis=0)
    s = mm_t(queries(own), kv)
    top = jnp.max(s, axis=1, keepdims=True)
    p = jnp.exp(s - top)
    o = mm(p.astype(BF), kv)
    lane = lax.broadcasted_iota(jnp.int32, o.shape, 1)
    acc_ref[...] = jnp.where(lane < HD, jnp.sum(p, axis=1, keepdims=True), o)
    max_ref[...] = jnp.broadcast_to(top, max_ref.shape)


def far_kernel(steps, parts, *refs):
    groups = len(steps)
    own, others = refs[:groups], refs[groups:-3]
    acc_ref, max_ref, out_ref = refs[-3:]
    kv = jnp.concatenate([r[...] for r in others], axis=0)
    s = mm_t(queries(own), kv)
    before = max_ref[...]
    top = jnp.maximum(before[:, :1], jnp.max(s, axis=1, keepdims=True))
    p = jnp.exp(s - top)
    o = mm(p.astype(BF), kv)
    lane = lax.broadcasted_iota(jnp.int32, o.shape, 1)
    new = jnp.where(lane < HD, jnp.sum(p, axis=1, keepdims=True), o)
    acc = acc_ref[...] * jnp.exp(before - top) + new
    o = acc / jnp.where(lane < HD, 1.0, pltpu.roll(acc, HD, 1))
    count = o.shape[0] // (groups * parts)
    zi, ii = lax.axis_index("head"), lax.axis_index("inner")
    for g in range(groups):
        for k in range(parts):
            at = (g * parts + k) * count
            block = halves(o[at : at + count // 2], o[at + count // 2 : at + count], True)
            out_ref[(zi ^ steps[g]) * parts + (ii ^ k)] = block.astype(BF)


def project_kernel(groups, parts, cin_ref, att_ref, *refs):
    ws, out_ref = refs[:-1], refs[-1]
    ii = lax.axis_index("inner")
    total = cin_ref[...].astype(F32)
    for k in range(parts):
        xs = [att_ref[g * parts + (ii ^ k)].astype(F32) for g in range(groups)]
        if groups % 2:
            cols = [jnp.concatenate([x[:, :HD], x[:, HD:]], axis=0) for x in xs]
        else:
            cols = [
                jnp.concatenate([halves(a, b, False), halves(a, b, True)], axis=0)
                for a, b in zip(xs[::2], xs[1::2])
            ]
        total = total + mm(jnp.concatenate(cols, axis=1).astype(BF), ws[k][...])
    out_ref[...] = total.astype(BF).reshape(out_ref.shape)


def call(kernel, out, in_specs, scratch=(), out_specs=None, limit=12, flops=None, name=None):
    cost = flops and pl.CostEstimate(flops=flops, bytes_accessed=MIB, transcendentals=0)
    return pl.pallas_call(
        kernel,
        out_shape=out,
        in_specs=in_specs,
        out_specs=[VM for _ in out] if out_specs is None else out_specs,
        scratch_shapes=list(scratch),
        compiler_params=pltpu.CompilerParams(vmem_limit_bytes=limit * MIB),
        cost_estimate=cost,
        name=name,
    )


def swap(x, axis, step):
    size = lax.axis_size(axis)
    return lax.ppermute(x, axis, [(i, i ^ step) for i in range(size)])


def body(
    tokens,
    timestep,
    mod_weight,
    fine_qkv_weight,
    fine_out_weight,
    merge_one,
    merge_two,
    coarse_qkv_weight,
    coarse_out_weight,
):
    S = jax.ShapeDtypeStruct
    rows, cols, width = tokens.shape
    cw = merge_two.shape[1]
    no, ni = lax.axis_size(OUTER), lax.axis_size("inner")
    odd = lax.axis_index(OUTER) % 2 == 1
    bottom, top = tokens[rows - WIN :], tokens[:WIN]
    pairs = [(i, i + 1) for i in range(1, no - 1, 2)]
    pairs += [(j, i) for i, j in pairs]
    far = lax.ppermute(jnp.where(odd, bottom, top), OUTER, pairs)
    near = swap(jnp.where(odd, top, bottom), OUTER, 1)

    emb = embed(timestep, mod_weight.shape[0])
    mod = mm(emb, mod_weight)
    tall = rows + 2 * WIN
    heads = width // HD
    q, kv, bias, kvw, outw = call(
        own_kernel,
        [
            S((rows, cols, width), F32),
            S((rows, cols + BLOCK, 2 * width), F32),
            S((heads * rows * BLOCK, tall * SPAN), F32),
            S((width, 2 * width), BF),
            S((width, width), BF),
        ],
        [VM] * 4,
        limit=16,
        flops=1000000000,
        name="own",
    )(mod, tokens, fine_qkv_weight, fine_out_weight)

    strip = S((tall, BLOCK, width // 2), BF)
    right, left = call(columns_kernel, [strip] * 2, [VM] * 3, name="columns")(
        far, near, tokens
    )
    west = lax.ppermute(right, "inner", [(i, (i + 1) % ni) for i in range(ni)])
    east = lax.ppermute(left, "inner", [((i + 1) % ni, i) for i in range(ni)])
    nkv, skv, res = call(
        inner_kernel,
        [S((WIN, cols + BLOCK, 2 * width), F32)] * 2 + [S((rows, cols, width), F32)],
        [VM] * 8,
        limit=16,
        flops=1000000000,
        name="inside",
    )(mod, far, near, kvw, outw, q, kv, bias)
    count = (rows // 4) * (cols // 4)
    skip, coarse_in = call(
        edge_kernel,
        [S(tokens.shape, BF), S((count, cw), BF)],
        [VM] * 14,
        scratch=[
            pltpu.VMEM((width // 128, rows, cols, 128), F32),
        ],
        limit=20,
        name="edge",
    )(
        mod, west, east, tokens, kvw, outw, q, kv, bias, nkv, skv, res, merge_one, merge_two
    )

    groups = coarse_qkv_weight.shape[1] // (3 * HD)
    sub = no // groups
    band = ni * count
    order, keep, fine_skip = call(
        order_kernel,
        [S(coarse_qkv_weight.shape, BF), S(coarse_in.shape, BF), S(tokens.shape, BF)],
        [VM] * 3,
        scratch=[pltpu.SemaphoreType.DMA],
        out_specs=[VM, VM, HB],
        flops=1000000000,
        name="order",
    )(coarse_in, skip, coarse_qkv_weight)
    gathered, step = [coarse_in], ni // 2
    beside = swap(coarse_in, "inner", 1)
    while step > 1:
        gathered = [w for x in gathered for w in (x, swap(x, "inner", step))]
        step //= 2
    weight, order, beside, gathered[1] = lax.optimization_barrier((coarse_out_weight, order, beside, gathered[1]))
    gathered = [w for x in gathered for w in (x, beside if x is coarse_in else swap(x, "inner", 1))]
    step = ni // 2
    whole = [weight, swap(weight, "inner", step)]
    pieces = call(
        lambda *r: qkv_kernel(groups, *r),
        [S((band + band // 2, 2 * HD), BF)] * groups,
        [VM] * (ni + 2),
        name="qkv",
    )(mod, *gathered, order)
    steps = [0] + list(range(groups - 1, 0, -1))
    own = [swap(pieces[g], OUTER, g * sub) if g else pieces[0] for g in steps]
    held = [own[0][:band]]
    if groups > 1:
        held.append(jnp.concatenate([p[:band] for p in own[1:]], axis=0))
    others = [swap(p, OUTER, k) for k in range(1, sub) for p in held]
    acc, top = call(
        lambda *r: near_kernel(groups, *r),
        [S((groups * band, 2 * HD), F32)] * 2,
        [VM] * (groups + EARLY),
        limit=16,
        flops=1000000000,
        name="near",
    )(*own, *others[:EARLY])
    others = others[EARLY:]
    att = call(
        lambda *r: far_kernel(steps, ni, *r),
        [S((groups * ni, count // 2, 2 * HD), BF)],
        [VM] * (groups + len(others) + 2),
        limit=16 if no * band <= 1024 else 56,
        name="far",
    )(*own, *others, acc, top)
    far_weight, att = lax.optimization_barrier((whole[1], att))
    whole[1] = far_weight
    while step > 1:
        step //= 2
        whole = [w for x in whole for w in (x, swap(x, "inner", step))]
    att = lax.all_to_all(att[0], ("head", "inner"), 0, 0, tiled=True)
    (coarse_out,) = call(
        lambda *r: project_kernel(groups, ni, *r),
        [S((rows // 4, cols // 4, cw), BF)],
        [VM] * (ni + 2),
        name="project",
    )(keep, att, *whole)
    return (fine_skip, coarse_out)


def solution(mesh):
    inner = mesh.shape["inner"]
    heads = 16 // inner
    devices = mesh.devices.reshape(heads, mesh.shape["outer"] // heads, inner)
    return jax.shard_map(
        body,
        mesh=jax.sharding.Mesh(devices, OUTER + ("inner",)),
        in_specs=(
            P(OUTER, "inner", None),
            P(),
            P(),
            P(),
            P(),
            P(),
            P(),
            P(None, "inner"),
            P("inner", None),
        ),
        out_specs=(P(OUTER, "inner", None), P(OUTER, "inner", None)),
        check_vma=False,
    )
```

```python
import math

import jax
import jax.numpy as jnp
from jax import lax
from jax.experimental import pallas as pl
from jax.experimental.pallas import tpu as pltpu
from jax.sharding import PartitionSpec as P

HD = 64
WIN = 3
BLOCK = 8
SPAN = 16
STAGE = 6
EARLY = 1
BF = jnp.bfloat16
F32 = jnp.float32
VM = pl.BlockSpec(memory_space=pltpu.VMEM)
HB = pl.BlockSpec(memory_space=pl.ANY)
HM = pl.BlockSpec(memory_space=pltpu.HBM)
MIB = 1024 * 1024
OUTER = ("head", "sub")


def embed(timestep, width):
    half = width // 2
    freq = jnp.exp(-math.log(10000.0) * jnp.arange(half, dtype=F32) / half)
    angle = timestep.astype(F32)[0] * freq
    return jnp.concatenate([jnp.cos(angle), jnp.sin(angle)]).astype(BF)[None, :]


def layer_norm(x, scale, shift):
    mean = jnp.mean(x, axis=-1, keepdims=True)
    var = jnp.mean((x - mean) * (x - mean), axis=-1, keepdims=True)
    return ((x - mean) * lax.rsqrt(var + 1e-06) * (1.0 + scale) + shift).astype(BF)


def mm(a, b):
    return jnp.dot(a, b, preferred_element_type=F32)


def mm_t(a, b):
    return lax.dot_general(a, b, (((1,), (1,)), ((), ())), preferred_element_type=F32)


def shifted(x):
    rows, cols, width = x.shape
    left = jnp.zeros((rows, WIN, width), F32)
    right = jnp.zeros((rows, BLOCK - WIN, width), F32)
    return jnp.concatenate([left, x, right], axis=1)


def key_values(x, mod_ref, w_ref):
    rows, cols, width = x.shape
    flat = x.reshape(rows * cols, width)
    n = layer_norm(flat, mod_ref[:, :width], mod_ref[:, width : 2 * width])
    return mm(n, w_ref[...]).reshape(rows, cols, 2 * width)


def place(axes):
    at = 0
    for axis in axes:
        at = at * lax.axis_size(axis) + lax.axis_index(axis)
    return at


def sides(far_ref, near_ref):
    odd = jnp.broadcast_to(place(OUTER) % 2, far_ref.shape) == 1
    far, near = far_ref[...].astype(F32), near_ref[...].astype(F32)
    return jnp.where(odd, near, far), jnp.where(odd, far, near)


def columns_kernel(far_ref, near_ref, tok_ref, right_ref, left_ref):
    cols, width = tok_ref.shape[1:]
    half = BLOCK // 2
    for out_ref, at, lead in ((right_ref, cols - 2 * BLOCK, 2 * BLOCK - WIN), (left_ref, 0, 0)):
        chunk = pl.ds(at, 2 * BLOCK)
        north, south = sides(far_ref.at[:, chunk], near_ref.at[:, chunk])
        x = jnp.concatenate([north, tok_ref[:, chunk].astype(F32), south], axis=0)
        x = jnp.concatenate([x[:, lead : lead + WIN], x[:, : half - WIN]], axis=1)
        x = jnp.concatenate([x[:, :, k : k + width // 2] for k in (0, width // 2)], axis=1)
        out_ref[...] = x.astype(BF)


def strip_columns(ref, lead):
    x = ref[...].astype(F32)
    half = BLOCK // 2
    x = jnp.concatenate([x[:, :half], x[:, half:]], axis=2)[:, :WIN]
    zero = jnp.zeros((x.shape[0], BLOCK, x.shape[2]), F32)
    parts = [zero[:, :lead]] * (lead > 0) + [x, zero[:, lead + WIN :]]
    return jnp.concatenate(parts, axis=1)


def own_kernel(
    mod_ref, tok_ref, w_ref, out_ref, q_ref, kv_ref, bias_ref, kvw_ref, outw_ref
):
    kvw_ref[...] = w_ref[:, tok_ref.shape[2] :]
    outw_ref[...] = out_ref[...]
    rows, cols, width = tok_ref.shape
    tok = tok_ref[...].astype(F32)
    fscale, fshift = mod_ref[:, :width], mod_ref[:, width : 2 * width]
    n = layer_norm(tok.reshape(rows * cols, width), fscale, fshift)
    q = mm(n, w_ref[:, :width]).astype(BF).astype(F32) * (1.0 / math.sqrt(HD))
    q_ref[...] = q.reshape(rows, cols, width)
    kv_ref[...] = key_values(shifted(tok), mod_ref, kvw_ref)

    nq, nk = bias_ref.shape
    per = rows * BLOCK
    band, bands = place(OUTER), lax.axis_size(OUTER)
    lo = jnp.where(band == 0, WIN, 0)
    hi = jnp.where(band == bands - 1, rows + WIN, rows + 2 * WIN)
    qi = lax.broadcasted_iota(jnp.int32, (nq, nk), 0) % per
    ki = lax.broadcasted_iota(jnp.int32, (nq, nk), 1)
    kr, kc = ki // SPAN, ki % SPAN
    dr, dc = kr - qi // BLOCK, kc - qi % BLOCK
    ok = (dr >= 0) & (dr <= 2 * WIN) & (dc >= 0) & (dc <= 2 * WIN) & (kr >= lo) & (kr < hi)
    bias_ref[...] = jnp.where(ok, 0.0, -1e30).astype(F32)


def order_kernel(cin_ref, skip_ref, cw_ref, order_ref, keep_ref, skip_hbm, sem):
    copy_skip = pltpu.make_async_copy(skip_ref, skip_hbm, sem)
    copy_skip.start()
    keep_ref[...] = cin_ref[...]
    groups = cw_ref.shape[1] // (3 * HD)
    kvs, qs = [], []
    for h in range(groups):
        qs.append(cw_ref[:, h * 3 * HD : h * 3 * HD + HD].astype(F32))
        kvs.append(cw_ref[:, h * 3 * HD + HD : (h + 1) * 3 * HD].astype(F32))
    order_ref[...] = jnp.concatenate(kvs + qs, axis=1).astype(BF)
    copy_skip.wait()


def attend(q_ref, wins, bias_ref, outw_ref, blocks):
    rows, cols, width = q_ref.shape
    heads, nq = width // HD, rows * BLOCK
    lane_head = lax.broadcasted_iota(jnp.int32, (nq, width), 1) // HD
    kvs, scores = [], []
    for j, win in zip(blocks, wins):
        qb = q_ref[:, j * BLOCK : (j + 1) * BLOCK, :].reshape(nq, width)
        qs = jnp.concatenate([jnp.where(lane_head == h, qb, 0.0) for h in range(heads)], axis=0)
        kvs.append(win.reshape(win.shape[0] * SPAN, 2 * width).astype(BF))
        scores.append(mm_t(qs.astype(BF), kvs[-1][:, :width]) + bias_ref[...])
    ps = [jnp.exp(s - jnp.max(s, axis=1, keepdims=True)) for s in scores]
    outs = [mm(p.astype(BF), kv[:, width:]) for p, kv in zip(ps, kvs)]
    atts = []
    for p, o in zip(ps, outs):
        o = o / jnp.sum(p, axis=1, keepdims=True)
        att = o[:nq]
        for h in range(1, heads):
            att = jnp.where(lane_head == h, o[h * nq : (h + 1) * nq], att)
        atts.append(att.astype(BF))
    proj = mm(jnp.concatenate(atts, axis=0), outw_ref[...])
    return [proj[i * nq : (i + 1) * nq].reshape(rows, BLOCK, width) for i in range(len(atts))]


def inner_kernel(
    mod_ref,
    far_ref,
    near_ref,
    w_ref,
    outw_ref,
    q_ref,
    kv_ref,
    bias_ref,
    nkv_ref,
    skv_ref,
    res_ref,
):
    north, south = sides(far_ref, near_ref)
    nkv_ref[...] = key_values(shifted(north), mod_ref, w_ref)
    skv_ref[...] = key_values(shifted(south), mod_ref, w_ref)
    cols = q_ref.shape[1]
    for lead in range(1, cols // BLOCK - 1, STAGE):
        blocks = range(lead, min(lead + STAGE, cols // BLOCK - 1))
        wins = [
            jnp.concatenate(
                [r[:, j * BLOCK : j * BLOCK + SPAN, :] for r in (nkv_ref, kv_ref, skv_ref)], axis=0
            )
            for j in blocks
        ]
        for j, proj in zip(blocks, attend(q_ref, wins, bias_ref, outw_ref, blocks)):
            res_ref[:, j * BLOCK : (j + 1) * BLOCK, :] = proj


def edge_kernel(
    mod_ref,
    west_ref,
    east_ref,
    tok_ref,
    w_ref,
    outw_ref,
    q_ref,
    kv_ref,
    bias_ref,
    nkv_ref,
    skv_ref,
    res_ref,
    one_ref,
    two_ref,
    skip_ref,
    cin_ref,
    lane_ref,
):
    rows, cols, width = tok_ref.shape
    side = lax.broadcasted_iota(jnp.int32, (rows + 2 * WIN, BLOCK, 2 * width), 1)
    kvs = (nkv_ref, kv_ref, skv_ref)

    def tile(at):
        return jnp.concatenate([r[:, at : at + BLOCK, :] for r in kvs], axis=0)

    strips = [strip_columns(west_ref, 0), strip_columns(east_ref, WIN)]
    strips = key_values(jnp.concatenate(strips, axis=0), mod_ref, w_ref)
    wkv, ekv = strips[: rows + 2 * WIN], strips[rows + 2 * WIN :]
    first = jnp.concatenate([jnp.where(side < WIN, wkv, tile(0)), tile(BLOCK)], axis=1)
    last = jnp.concatenate([tile(cols - BLOCK), jnp.where(side >= WIN, ekv, tile(cols))], axis=1)
    tok = tok_ref[...].astype(F32)
    ends = (0, cols // BLOCK - 1)
    low, high = attend(q_ref, [first, last], bias_ref, outw_ref, ends)
    proj = jnp.concatenate([low, res_ref[:, BLOCK : cols - BLOCK, :], high], axis=1)
    res = (proj + tok).astype(BF)
    skip_ref[...] = res
    for k in range(width // 128):
        lane_ref[k] = res[:, :, k * 128 : (k + 1) * 128].astype(F32)

    groups = []
    for a in range(2):
        for b in range(2):
            parts = []
            for dr in range(2):
                for dc in range(2):
                    r, c = 2 * a + dr, 2 * b + dc
                    for k in range(width // 128):
                        strips = [
                            lane_ref[k, rr, pl.ds(c, cols // 4, stride=4), :]
                            for rr in range(r, rows, 4)
                        ]
                        parts.append(jnp.concatenate(strips, axis=0))
            groups.append(jnp.concatenate(parts, axis=1))
    count = (rows // 4) * (cols // 4)
    mid = mm(jnp.concatenate(groups, axis=0).astype(BF), one_ref[...]).astype(BF)
    mid = jnp.concatenate([mid[g * count : (g + 1) * count] for g in range(4)], axis=1)
    cin_ref[...] = mm(mid, two_ref[...]).astype(BF)


def halves(low, high, swap_low):
    lane = lax.broadcasted_iota(jnp.int32, low.shape, 1)
    if swap_low:
        return jnp.where(lane < HD, pltpu.roll(low, HD, 1), high)
    return jnp.where(lane < HD, low, pltpu.roll(high, HD, 1))


def qkv_kernel(groups, mod_ref, *refs):
    xs, w_ref, out_refs = refs[: -1 - groups], refs[-1 - groups], refs[-groups:]
    x = jnp.concatenate([r[...] for r in xs], axis=0)
    at = mod_ref.shape[1] - 2 * x.shape[1]
    scale, shift = mod_ref[:, at : at + x.shape[1]], mod_ref[:, at + x.shape[1] :]
    y = mm(layer_norm(x.astype(F32), scale, shift), w_ref[...])
    half = x.shape[0] // 2
    zi = lax.axis_index("head")
    pieces = []
    for h in range(groups):
        kv = y[:, h * 2 * HD : (h + 1) * 2 * HD]
        if groups % 2:
            q = y[:, groups * 2 * HD + h * HD : groups * 2 * HD + (h + 1) * HD]
            qp = jnp.concatenate([q[:half], q[half:]], axis=1)
        else:
            at = groups * 2 * HD + (h // 2) * 2 * HD
            pair = y[:, at : at + 2 * HD]
            qp = halves(pair[:half], pair[half:], h % 2 == 1)
        pieces.append(jnp.concatenate([kv, qp * (1.0 / math.sqrt(HD))], axis=0).astype(BF))
    for g in range(groups):
        for h in range(groups):

            @pl.when(zi == g ^ h)
            def _(g=g, h=h):
                out_refs[g][...] = pieces[h]


def queries(own):
    band = own[0].shape[0] * 2 // 3
    half = band // 2
    lane = lax.broadcasted_iota(jnp.int32, (half, 2 * HD), 1)
    qs = []
    for r in own:
        qp = r[band:, :].astype(F32)
        qs.append(jnp.where(lane < HD, qp, 0.0))
        qs.append(jnp.where(lane < HD, pltpu.roll(qp, HD, 1), 0.0))
    return jnp.concatenate(qs, axis=0).astype(BF)


def near_kernel(groups, *refs):
    own, others, (acc_ref, max_ref) = refs[:groups], refs[groups:-2], refs[-2:]
    band = own[0].shape[0] * 2 // 3
    kv = jnp.concatenate([r[:band, :] for r in own] + [r[...] for r in others], axis=0)
    s = mm_t(queries(own), kv)
    top = jnp.max(s, axis=1, keepdims=True)
    p = jnp.exp(s - top)
    o = mm(p.astype(BF), kv)
    lane = lax.broadcasted_iota(jnp.int32, o.shape, 1)
    acc_ref[...] = jnp.where(lane < HD, jnp.sum(p, axis=1, keepdims=True), o)
    max_ref[...] = jnp.broadcast_to(top, max_ref.shape)


def far_kernel(steps, parts, *refs):
    groups = len(steps)
    own, others = refs[:groups], refs[groups:-3]
    acc_ref, max_ref, out_ref = refs[-3:]
    kv = jnp.concatenate([r[...] for r in others], axis=0)
    s = mm_t(queries(own), kv)
    before = max_ref[...]
    top = jnp.maximum(before[:, :1], jnp.max(s, axis=1, keepdims=True))
    p = jnp.exp(s - top)
    o = mm(p.astype(BF), kv)
    lane = lax.broadcasted_iota(jnp.int32, o.shape, 1)
    new = jnp.where(lane < HD, jnp.sum(p, axis=1, keepdims=True), o)
    acc = acc_ref[...] * jnp.exp(before - top) + new
    o = acc / jnp.where(lane < HD, 1.0, pltpu.roll(acc, HD, 1))
    count = o.shape[0] // (groups * parts)
    zi, ii = lax.axis_index("head"), lax.axis_index("inner")
    for g in range(groups):
        for k in range(parts):
            at = (g * parts + k) * count
            block = halves(o[at : at + count // 2], o[at + count // 2 : at + count], True)
            out_ref[(zi ^ steps[g]) * parts + (ii ^ k)] = block.astype(BF)


def project_kernel(groups, parts, cin_ref, att_ref, *refs):
    ws, out_ref = refs[:-1], refs[-1]
    ii = lax.axis_index("inner")
    total = cin_ref[...].astype(F32)
    for k in range(parts):
        xs = [att_ref[g * parts + (ii ^ k)].astype(F32) for g in range(groups)]
        if groups % 2:
            cols = [jnp.concatenate([x[:, :HD], x[:, HD:]], axis=0) for x in xs]
        else:
            cols = [
                jnp.concatenate([halves(a, b, False), halves(a, b, True)], axis=0)
                for a, b in zip(xs[::2], xs[1::2])
            ]
        total = total + mm(jnp.concatenate(cols, axis=1).astype(BF), ws[k][...])
    out_ref[...] = total.astype(BF).reshape(out_ref.shape)


def call(kernel, out, in_specs, scratch=(), out_specs=None, limit=12, flops=None, name=None):
    cost = flops and pl.CostEstimate(flops=flops, bytes_accessed=MIB, transcendentals=0)
    return pl.pallas_call(
        kernel,
        out_shape=out,
        in_specs=in_specs,
        out_specs=[VM for _ in out] if out_specs is None else out_specs,
        scratch_shapes=list(scratch),
        compiler_params=pltpu.CompilerParams(vmem_limit_bytes=limit * MIB),
        cost_estimate=cost,
        name=name,
    )


def swap(x, axis, step):
    size = lax.axis_size(axis)
    return lax.ppermute(x, axis, [(i, i ^ step) for i in range(size)])


def body(
    tokens,
    timestep,
    mod_weight,
    fine_qkv_weight,
    fine_out_weight,
    merge_one,
    merge_two,
    coarse_qkv_weight,
    coarse_out_weight,
):
    S = jax.ShapeDtypeStruct
    rows, cols, width = tokens.shape
    cw = merge_two.shape[1]
    no, ni = lax.axis_size(OUTER), lax.axis_size("inner")
    odd = lax.axis_index(OUTER) % 2 == 1
    bottom, top = tokens[rows - WIN :], tokens[:WIN]
    pairs = []
    for i in range(no * ni):
        band, column = i // ni, i % ni
        if band in (0, no - 1):
            pairs.append((i, band * ni + (column ^ 1)))
        else:
            pairs.append((i, i + ni if band % 2 else i - ni))
    far = lax.ppermute(jnp.where(odd, bottom, top), OUTER + ("inner",), pairs)
    near = swap(jnp.where(odd, top, bottom), OUTER, 1)

    emb = embed(timestep, mod_weight.shape[0])
    mod = mm(emb, mod_weight)
    tall = rows + 2 * WIN
    heads = width // HD
    q, kv, bias, kvw, outw = call(
        own_kernel,
        [
            S((rows, cols, width), F32),
            S((rows, cols + BLOCK, 2 * width), F32),
            S((heads * rows * BLOCK, tall * SPAN), F32),
            S((width, 2 * width), BF),
            S((width, width), BF),
        ],
        [VM] * 4,
        limit=16,
        flops=1000000000,
        name="own",
    )(mod, tokens, fine_qkv_weight, fine_out_weight)

    strip = S((tall, BLOCK, width // 2), BF)
    right, left = call(columns_kernel, [strip] * 2, [VM] * 3, name="columns")(
        far, near, tokens
    )
    west = lax.ppermute(right, "inner", [(i, (i + 1) % ni) for i in range(ni)])
    east = lax.ppermute(left, "inner", [((i + 1) % ni, i) for i in range(ni)])
    nkv, skv, res = call(
        inner_kernel,
        [S((WIN, cols + BLOCK, 2 * width), F32)] * 2 + [S((rows, cols, width), F32)],
        [VM] * 8,
        limit=16,
        flops=1000000000,
        name="inside",
    )(mod, far, near, kvw, outw, q, kv, bias)
    count = (rows // 4) * (cols // 4)
    skip, coarse_in = call(
        edge_kernel,
        [S(tokens.shape, BF), S((count, cw), BF)],
        [VM] * 14,
        scratch=[
            pltpu.VMEM((width // 128, rows, cols, 128), F32),
        ],
        limit=20,
        name="edge",
    )(
        mod, west, east, tokens, kvw, outw, q, kv, bias, nkv, skv, res, merge_one, merge_two
    )

    groups = coarse_qkv_weight.shape[1] // (3 * HD)
    sub = no // groups
    band = ni * count
    order, keep, fine_skip = call(
        order_kernel,
        [S(coarse_qkv_weight.shape, BF), S(coarse_in.shape, BF), S(tokens.shape, BF)],
        [VM] * 3,
        scratch=[pltpu.SemaphoreType.DMA],
        out_specs=[VM, VM, HB],
        flops=1000000000,
        name="order",
    )(coarse_in, skip, coarse_qkv_weight)
    gathered, step = [coarse_in], ni // 2
    beside = swap(coarse_in, "inner", 1)
    while step > 1:
        gathered = [w for x in gathered for w in (x, swap(x, "inner", step))]
        step //= 2
    weight, order, beside, gathered[1] = lax.optimization_barrier((coarse_out_weight, order, beside, gathered[1]))
    gathered = [w for x in gathered for w in (x, beside if x is coarse_in else swap(x, "inner", 1))]
    step = ni // 2
    whole = [weight, swap(weight, "inner", step)]
    pieces = call(
        lambda *r: qkv_kernel(groups, *r),
        [S((band + band // 2, 2 * HD), BF)] * groups,
        [VM] * (ni + 2),
        name="qkv",
    )(mod, *gathered, order)
    steps = [0] + list(range(groups - 1, 0, -1))
    own = [swap(pieces[g], OUTER, g * sub) if g else pieces[0] for g in steps]
    held = [own[0][:band]]
    if groups > 1:
        held.append(jnp.concatenate([p[:band] for p in own[1:]], axis=0))
    others = [swap(p, OUTER, k) for k in range(1, sub) for p in held]
    acc, top = call(
        lambda *r: near_kernel(groups, *r),
        [S((groups * band, 2 * HD), F32)] * 2,
        [VM] * (groups + EARLY),
        limit=16,
        flops=1000000000,
        name="near",
    )(*own, *others[:EARLY])
    others = others[EARLY:]
    att = call(
        lambda *r: far_kernel(steps, ni, *r),
        [S((groups * ni, count // 2, 2 * HD), BF)],
        [VM] * (groups + len(others) + 2),
        limit=16 if no * band <= 1024 else 56,
        name="far",
    )(*own, *others, acc, top)
    far_weight, att = lax.optimization_barrier((whole[1], att))
    whole[1] = far_weight
    while step > 1:
        step //= 2
        whole = [w for x in whole for w in (x, swap(x, "inner", step))]
    att = lax.all_to_all(att[0], ("head", "inner"), 0, 0, tiled=True)
    (coarse_out,) = call(
        lambda *r: project_kernel(groups, ni, *r),
        [S((rows // 4, cols // 4, cw), BF)],
        [VM] * (ni + 2),
        name="project",
    )(keep, att, *whole)
    return (fine_skip, coarse_out)


def solution(mesh):
    inner = mesh.shape["inner"]
    heads = 16 // inner
    devices = mesh.devices.reshape(heads, mesh.shape["outer"] // heads, inner)
    return jax.shard_map(
        body,
        mesh=jax.sharding.Mesh(devices, OUTER + ("inner",)),
        in_specs=(
            P(OUTER, "inner", None),
            P(),
            P(),
            P(),
            P(),
            P(),
            P(),
            P(None, "inner"),
            P("inner", None),
        ),
        out_specs=(P(OUTER, "inner", None), P(OUTER, "inner", None)),
        check_vma=False,
    )
```

```python
import math

import jax
import jax.numpy as jnp
from jax import lax
from jax.experimental import pallas as pl
from jax.experimental.pallas import tpu as pltpu
from jax.sharding import PartitionSpec as P

HD = 64
WIN = 3
BLOCK = 8
SPAN = 16
STAGE = 6
EARLY = 1
BF = jnp.bfloat16
F32 = jnp.float32
VM = pl.BlockSpec(memory_space=pltpu.VMEM)
HB = pl.BlockSpec(memory_space=pl.ANY)
HM = pl.BlockSpec(memory_space=pltpu.HBM)
MIB = 1024 * 1024
OUTER = ("head", "sub")


def embed(timestep, width):
    half = width // 2
    freq = jnp.exp(-math.log(10000.0) * jnp.arange(half, dtype=F32) / half)
    angle = timestep.astype(F32)[0] * freq
    return jnp.concatenate([jnp.cos(angle), jnp.sin(angle)]).astype(BF)[None, :]


def layer_norm(x, scale, shift):
    mean = jnp.mean(x, axis=-1, keepdims=True)
    var = jnp.mean((x - mean) * (x - mean), axis=-1, keepdims=True)
    return ((x - mean) * lax.rsqrt(var + 1e-06) * (1.0 + scale) + shift).astype(BF)


def mm(a, b):
    return jnp.dot(a, b, preferred_element_type=F32)


def mm_t(a, b):
    return lax.dot_general(a, b, (((1,), (1,)), ((), ())), preferred_element_type=F32)


def shifted(x):
    rows, cols, width = x.shape
    left = jnp.zeros((rows, WIN, width), F32)
    right = jnp.zeros((rows, BLOCK - WIN, width), F32)
    return jnp.concatenate([left, x, right], axis=1)


def key_values(x, mod_ref, w_ref):
    rows, cols, width = x.shape
    flat = x.reshape(rows * cols, width)
    n = layer_norm(flat, mod_ref[:, :width], mod_ref[:, width : 2 * width])
    return mm(n, w_ref[...]).reshape(rows, cols, 2 * width)


def place(axes):
    at = 0
    for axis in axes:
        at = at * lax.axis_size(axis) + lax.axis_index(axis)
    return at


def sides(far_ref, near_ref):
    odd = jnp.broadcast_to(place(OUTER) % 2, far_ref.shape) == 1
    far, near = far_ref[...].astype(F32), near_ref[...].astype(F32)
    return jnp.where(odd, near, far), jnp.where(odd, far, near)


def columns_kernel(far_ref, near_ref, tok_ref, chip_ref, link_ref):
    cols, width = tok_ref.shape[1:]
    half = BLOCK // 2
    strips = []
    for at, lead in ((cols - 2 * BLOCK, 2 * BLOCK - WIN), (0, 0)):
        chunk = pl.ds(at, 2 * BLOCK)
        north, south = sides(far_ref.at[:, chunk], near_ref.at[:, chunk])
        x = jnp.concatenate([north, tok_ref[:, chunk].astype(F32), south], axis=0)
        x = jnp.concatenate([x[:, lead : lead + WIN], x[:, : half - WIN]], axis=1)
        strips.append(jnp.concatenate([x[:, :, k : k + width // 2] for k in (0, width // 2)], axis=1))
    odd = jnp.broadcast_to(lax.axis_index("inner") % 2, strips[0].shape) == 1
    chip_ref[...] = jnp.where(odd, strips[1], strips[0]).astype(BF)
    link_ref[...] = jnp.where(odd, strips[0], strips[1]).astype(BF)


def strip_columns(x, lead):
    half = BLOCK // 2
    x = jnp.concatenate([x[:, :half], x[:, half:]], axis=2)[:, :WIN]
    zero = jnp.zeros((x.shape[0], BLOCK, x.shape[2]), F32)
    parts = [zero[:, :lead]] * (lead > 0) + [x, zero[:, lead + WIN :]]
    return jnp.concatenate(parts, axis=1)


def own_kernel(
    mod_ref, tok_ref, w_ref, out_ref, q_ref, kv_ref, bias_ref, kvw_ref, outw_ref
):
    kvw_ref[...] = w_ref[:, tok_ref.shape[2] :]
    outw_ref[...] = out_ref[...]
    rows, cols, width = tok_ref.shape
    tok = tok_ref[...].astype(F32)
    fscale, fshift = mod_ref[:, :width], mod_ref[:, width : 2 * width]
    n = layer_norm(tok.reshape(rows * cols, width), fscale, fshift)
    q = mm(n, w_ref[:, :width]).astype(BF).astype(F32) * (1.0 / math.sqrt(HD))
    q_ref[...] = q.reshape(rows, cols, width)
    kv_ref[...] = key_values(shifted(tok), mod_ref, kvw_ref)

    nq, nk = bias_ref.shape
    per = rows * BLOCK
    band, bands = place(OUTER), lax.axis_size(OUTER)
    lo = jnp.where(band == 0, WIN, 0)
    hi = jnp.where(band == bands - 1, rows + WIN, rows + 2 * WIN)
    qi = lax.broadcasted_iota(jnp.int32, (nq, nk), 0) % per
    ki = lax.broadcasted_iota(jnp.int32, (nq, nk), 1)
    kr, kc = ki // SPAN, ki % SPAN
    dr, dc = kr - qi // BLOCK, kc - qi % BLOCK
    ok = (dr >= 0) & (dr <= 2 * WIN) & (dc >= 0) & (dc <= 2 * WIN) & (kr >= lo) & (kr < hi)
    bias_ref[...] = jnp.where(ok, 0.0, -1e30).astype(F32)


def order_kernel(cin_ref, skip_ref, cw_ref, order_ref, keep_ref, skip_hbm, sem):
    copy_skip = pltpu.make_async_copy(skip_ref, skip_hbm, sem)
    copy_skip.start()
    keep_ref[...] = cin_ref[...]
    groups = cw_ref.shape[1] // (3 * HD)
    kvs, qs = [], []
    for h in range(groups):
        qs.append(cw_ref[:, h * 3 * HD : h * 3 * HD + HD].astype(F32))
        kvs.append(cw_ref[:, h * 3 * HD + HD : (h + 1) * 3 * HD].astype(F32))
    order_ref[...] = jnp.concatenate(kvs + qs, axis=1).astype(BF)
    copy_skip.wait()


def attend(q_ref, wins, bias_ref, outw_ref, blocks):
    rows, cols, width = q_ref.shape
    heads, nq = width // HD, rows * BLOCK
    lane_head = lax.broadcasted_iota(jnp.int32, (nq, width), 1) // HD
    kvs, scores = [], []
    for j, win in zip(blocks, wins):
        qb = q_ref[:, j * BLOCK : (j + 1) * BLOCK, :].reshape(nq, width)
        qs = jnp.concatenate([jnp.where(lane_head == h, qb, 0.0) for h in range(heads)], axis=0)
        kvs.append(win.reshape(win.shape[0] * SPAN, 2 * width).astype(BF))
        scores.append(mm_t(qs.astype(BF), kvs[-1][:, :width]) + bias_ref[...])
    ps = [jnp.exp(s - jnp.max(s, axis=1, keepdims=True)) for s in scores]
    outs = [mm(p.astype(BF), kv[:, width:]) for p, kv in zip(ps, kvs)]
    atts = []
    for p, o in zip(ps, outs):
        o = o / jnp.sum(p, axis=1, keepdims=True)
        att = o[:nq]
        for h in range(1, heads):
            att = jnp.where(lane_head == h, o[h * nq : (h + 1) * nq], att)
        atts.append(att.astype(BF))
    proj = mm(jnp.concatenate(atts, axis=0), outw_ref[...])
    return [proj[i * nq : (i + 1) * nq].reshape(rows, BLOCK, width) for i in range(len(atts))]


def inner_kernel(
    mod_ref,
    far_ref,
    near_ref,
    w_ref,
    outw_ref,
    q_ref,
    kv_ref,
    bias_ref,
    nkv_ref,
    skv_ref,
    res_ref,
):
    north, south = sides(far_ref, near_ref)
    nkv_ref[...] = key_values(shifted(north), mod_ref, w_ref)
    skv_ref[...] = key_values(shifted(south), mod_ref, w_ref)
    cols = q_ref.shape[1]
    for lead in range(1, cols // BLOCK - 1, STAGE):
        blocks = range(lead, min(lead + STAGE, cols // BLOCK - 1))
        wins = [
            jnp.concatenate(
                [r[:, j * BLOCK : j * BLOCK + SPAN, :] for r in (nkv_ref, kv_ref, skv_ref)], axis=0
            )
            for j in blocks
        ]
        for j, proj in zip(blocks, attend(q_ref, wins, bias_ref, outw_ref, blocks)):
            res_ref[:, j * BLOCK : (j + 1) * BLOCK, :] = proj


def edge_kernel(
    mod_ref,
    chip_ref,
    link_ref,
    tok_ref,
    w_ref,
    outw_ref,
    q_ref,
    kv_ref,
    bias_ref,
    nkv_ref,
    skv_ref,
    res_ref,
    one_ref,
    two_ref,
    skip_ref,
    cin_ref,
    lane_ref,
):
    rows, cols, width = tok_ref.shape
    side = lax.broadcasted_iota(jnp.int32, (rows + 2 * WIN, BLOCK, 2 * width), 1)
    kvs = (nkv_ref, kv_ref, skv_ref)

    def tile(at):
        return jnp.concatenate([r[:, at : at + BLOCK, :] for r in kvs], axis=0)

    odd = jnp.broadcast_to(lax.axis_index("inner") % 2, chip_ref.shape) == 1
    chip, link = chip_ref[...].astype(F32), link_ref[...].astype(F32)
    west, east = jnp.where(odd, chip, link), jnp.where(odd, link, chip)
    strips = [strip_columns(west, 0), strip_columns(east, WIN)]
    strips = key_values(jnp.concatenate(strips, axis=0), mod_ref, w_ref)
    wkv, ekv = strips[: rows + 2 * WIN], strips[rows + 2 * WIN :]
    first = jnp.concatenate([jnp.where(side < WIN, wkv, tile(0)), tile(BLOCK)], axis=1)
    last = jnp.concatenate([tile(cols - BLOCK), jnp.where(side >= WIN, ekv, tile(cols))], axis=1)
    tok = tok_ref[...].astype(F32)
    ends = (0, cols // BLOCK - 1)
    low, high = attend(q_ref, [first, last], bias_ref, outw_ref, ends)
    proj = jnp.concatenate([low, res_ref[:, BLOCK : cols - BLOCK, :], high], axis=1)
    res = (proj + tok).astype(BF)
    skip_ref[...] = res
    for k in range(width // 128):
        lane_ref[k, :, :cols, :] = res[:, :, k * 128 : (k + 1) * 128].astype(F32)

    groups = []
    for a in range(2):
        for b in range(2):
            parts = []
            for dr in range(2):
                for dc in range(2):
                    r, c = 2 * a + dr, 2 * b + dc
                    for k in range(width // 128):
                        strips = [
                            lane_ref[k, rr, pl.ds(c, cols // 4, stride=4), :]
                            for rr in range(r, rows, 4)
                        ]
                        parts.append(jnp.concatenate(strips, axis=0))
            groups.append(jnp.concatenate(parts, axis=1))
    count = (rows // 4) * (cols // 4)
    mid = mm(jnp.concatenate(groups, axis=0).astype(BF), one_ref[...]).astype(BF)
    mid = jnp.concatenate([mid[g * count : (g + 1) * count] for g in range(4)], axis=1)
    cin_ref[...] = mm(mid, two_ref[...]).astype(BF)


def halves(low, high, swap_low):
    lane = lax.broadcasted_iota(jnp.int32, low.shape, 1)
    if swap_low:
        return jnp.where(lane < HD, pltpu.roll(low, HD, 1), high)
    return jnp.where(lane < HD, low, pltpu.roll(high, HD, 1))


def qkv_kernel(groups, mod_ref, *refs):
    xs, w_ref, out_refs = refs[: -1 - groups], refs[-1 - groups], refs[-groups:]
    x = jnp.concatenate([r[...] for r in xs], axis=0)
    at = mod_ref.shape[1] - 2 * x.shape[1]
    scale, shift = mod_ref[:, at : at + x.shape[1]], mod_ref[:, at + x.shape[1] :]
    y = mm(layer_norm(x.astype(F32), scale, shift), w_ref[...])
    half = x.shape[0] // 2
    zi = lax.axis_index("head")
    pieces = []
    for h in range(groups):
        kv = y[:, h * 2 * HD : (h + 1) * 2 * HD]
        if groups % 2:
            q = y[:, groups * 2 * HD + h * HD : groups * 2 * HD + (h + 1) * HD]
            qp = jnp.concatenate([q[:half], q[half:]], axis=1)
        else:
            at = groups * 2 * HD + (h // 2) * 2 * HD
            pair = y[:, at : at + 2 * HD]
            qp = halves(pair[:half], pair[half:], h % 2 == 1)
        pieces.append(jnp.concatenate([kv, qp * (1.0 / math.sqrt(HD))], axis=0).astype(BF))
    for g in range(groups):
        for h in range(groups):

            @pl.when(zi == g ^ h)
            def _(g=g, h=h):
                out_refs[g][...] = pieces[h]


def queries(own):
    band = own[0].shape[0] * 2 // 3
    half = band // 2
    lane = lax.broadcasted_iota(jnp.int32, (half, 2 * HD), 1)
    qs = []
    for r in own:
        qp = r[band:, :].astype(F32)
        qs.append(jnp.where(lane < HD, qp, 0.0))
        qs.append(jnp.where(lane < HD, pltpu.roll(qp, HD, 1), 0.0))
    return jnp.concatenate(qs, axis=0).astype(BF)


def values(kv):
    lane = lax.broadcasted_iota(jnp.int32, kv.shape, 1)
    return jnp.where(lane < HD, jnp.ones_like(kv), kv)


def near_kernel(groups, *refs):
    own, others, (acc_ref, max_ref) = refs[:groups], refs[groups:-2], refs[-2:]
    band = own[0].shape[0] * 2 // 3
    kv = jnp.concatenate([r[:band, :] for r in own] + [r[...] for r in others], axis=0)
    s = mm_t(queries(own), kv)
    top = jnp.max(s, axis=1, keepdims=True)
    p = jnp.exp(s - top)
    acc_ref[...] = mm(p.astype(BF), values(kv))
    max_ref[...] = jnp.broadcast_to(top, max_ref.shape)


def far_kernel(steps, parts, *refs):
    groups = len(steps)
    own, others = refs[:groups], refs[groups:-3]
    acc_ref, max_ref, out_ref = refs[-3:]
    kv = jnp.concatenate([r[...] for r in others], axis=0)
    s = mm_t(queries(own), kv)
    before = max_ref[...]
    top = jnp.maximum(before[:, :1], jnp.max(s, axis=1, keepdims=True))
    p = jnp.exp(s - top)
    acc = acc_ref[...] * jnp.exp(before - top) + mm(p.astype(BF), values(kv))
    count = acc.shape[0] // (groups * parts)
    zi, ii = lax.axis_index("head"), lax.axis_index("inner")
    for g in range(groups):
        for k in range(parts):
            at = (g * parts + k) * count
            low, high = acc[at : at + count // 2], acc[at + count // 2 : at + count]
            block = halves(low, high, True) / halves(low, high, False)
            out_ref[(zi ^ steps[g]) * parts + (ii ^ k)] = block.astype(BF)


def project_kernel(groups, parts, cin_ref, att_ref, *refs):
    ws, out_ref = refs[:-1], refs[-1]
    ii = lax.axis_index("inner")
    total = cin_ref[...].astype(F32)
    for k in range(parts):
        xs = [att_ref[g * parts + (ii ^ k)].astype(F32) for g in range(groups)]
        if groups % 2:
            cols = [jnp.concatenate([x[:, :HD], x[:, HD:]], axis=0) for x in xs]
        else:
            cols = [
                jnp.concatenate([halves(a, b, False), halves(a, b, True)], axis=0)
                for a, b in zip(xs[::2], xs[1::2])
            ]
        total = total + mm(jnp.concatenate(cols, axis=1).astype(BF), ws[k][...])
    out_ref[...] = total.astype(BF).reshape(out_ref.shape)


def call(kernel, out, in_specs, scratch=(), out_specs=None, limit=12, flops=None, name=None):
    cost = flops and pl.CostEstimate(flops=flops, bytes_accessed=MIB, transcendentals=0)
    return pl.pallas_call(
        kernel,
        out_shape=out,
        in_specs=in_specs,
        out_specs=[VM for _ in out] if out_specs is None else out_specs,
        scratch_shapes=list(scratch),
        compiler_params=pltpu.CompilerParams(vmem_limit_bytes=limit * MIB),
        cost_estimate=cost,
        name=name,
    )


def swap(x, axis, step):
    size = lax.axis_size(axis)
    return lax.ppermute(x, axis, [(i, i ^ step) for i in range(size)])


def body(
    tokens,
    timestep,
    mod_weight,
    fine_qkv_weight,
    fine_out_weight,
    merge_one,
    merge_two,
    coarse_qkv_weight,
    coarse_out_weight,
):
    S = jax.ShapeDtypeStruct
    rows, cols, width = tokens.shape
    cw = merge_two.shape[1]
    no, ni = lax.axis_size(OUTER), lax.axis_size("inner")
    odd = lax.axis_index(OUTER) % 2 == 1
    bottom, top = tokens[rows - WIN :], tokens[:WIN]
    pairs = []
    for i in range(no * ni):
        band, column = i // ni, i % ni
        if band in (0, no - 1):
            pairs.append((i, band * ni + (column ^ 1)))
        else:
            pairs.append((i, i + ni if band % 2 else i - ni))
    far = lax.ppermute(jnp.where(odd, bottom, top), OUTER + ("inner",), pairs)
    near = swap(jnp.where(odd, top, bottom), OUTER, 1)

    emb = embed(timestep, mod_weight.shape[0])
    mod = mm(emb, mod_weight)
    tall = rows + 2 * WIN
    heads = width // HD
    q, kv, bias, kvw, outw = call(
        own_kernel,
        [
            S((rows, cols, width), F32),
            S((rows, cols + BLOCK, 2 * width), F32),
            S((heads * rows * BLOCK, tall * SPAN), F32),
            S((width, 2 * width), BF),
            S((width, width), BF),
        ],
        [VM] * 4,
        limit=16,
        flops=1000000000,
        name="own",
    )(mod, tokens, fine_qkv_weight, fine_out_weight)

    strip = S((tall, BLOCK, width // 2), BF)
    chip, link = call(columns_kernel, [strip] * 2, [VM] * 3, name="columns")(
        far, near, tokens
    )
    chip = swap(chip, "inner", 1)
    link = lax.ppermute(link, "inner", [(i, (i + (1 if i % 2 else -1)) % ni) for i in range(ni)])
    nkv, skv, res = call(
        inner_kernel,
        [S((WIN, cols + BLOCK, 2 * width), F32)] * 2 + [S((rows, cols, width), F32)],
        [VM] * 8,
        limit=16,
        flops=1000000000,
        name="inside",
    )(mod, far, near, kvw, outw, q, kv, bias)
    count = (rows // 4) * (cols // 4)
    skip, coarse_in = call(
        edge_kernel,
        [S(tokens.shape, BF), S((count, cw), BF)],
        [VM] * 14,
        scratch=[
            pltpu.VMEM((width // 128, rows, cols + BLOCK, 128), F32),
        ],
        limit=20,
        name="edge",
    )(
        mod, chip, link, tokens, kvw, outw, q, kv, bias, nkv, skv, res, merge_one, merge_two
    )

    groups = coarse_qkv_weight.shape[1] // (3 * HD)
    sub = no // groups
    band = ni * count
    order, keep, fine_skip = call(
        order_kernel,
        [S(coarse_qkv_weight.shape, BF), S(coarse_in.shape, BF), S(tokens.shape, BF)],
        [VM] * 3,
        scratch=[pltpu.SemaphoreType.DMA],
        out_specs=[VM, VM, HB],
        flops=1000000000,
        name="order",
    )(coarse_in, skip, coarse_qkv_weight)
    gathered, step = [coarse_in], ni // 2
    beside = swap(coarse_in, "inner", 1)
    while step > 1:
        gathered = [w for x in gathered for w in (x, swap(x, "inner", step))]
        step //= 2
    weight, order, beside, gathered[1] = lax.optimization_barrier((coarse_out_weight, order, beside, gathered[1]))
    gathered = [w for x in gathered for w in (x, beside if x is coarse_in else swap(x, "inner", 1))]
    step = ni // 2
    whole = [weight, swap(weight, "inner", step)]
    pieces = call(
        lambda *r: qkv_kernel(groups, *r),
        [S((band + band // 2, 2 * HD), BF)] * groups,
        [VM] * (ni + 2),
        name="qkv",
    )(mod, *gathered, order)
    steps = [0] + list(range(groups - 1, 0, -1))
    own = [swap(pieces[g], OUTER, g * sub) if g else pieces[0] for g in steps]
    held = [own[0][:band]]
    if groups > 1:
        held.append(jnp.concatenate([p[:band] for p in own[1:]], axis=0))
    others = [swap(p, OUTER, k) for k in range(1, sub) for p in held]
    acc, top = call(
        lambda *r: near_kernel(groups, *r),
        [S((groups * band, 2 * HD), F32)] * 2,
        [VM] * (groups + EARLY),
        limit=16,
        flops=1000000000,
        name="near",
    )(*own, *others[:EARLY])
    others = others[EARLY:]
    att = call(
        lambda *r: far_kernel(steps, ni, *r),
        [S((groups * ni, count // 2, 2 * HD), BF)],
        [VM] * (groups + len(others) + 2),
        limit=16 if no * band <= 1024 else 56,
        name="far",
    )(*own, *others, acc, top)
    far_weight, att = lax.optimization_barrier((whole[1], att))
    whole[1] = far_weight
    while step > 1:
        step //= 2
        whole = [w for x in whole for w in (x, swap(x, "inner", step))]
    att = lax.all_to_all(att[0], ("head", "inner"), 0, 0, tiled=True)
    (coarse_out,) = call(
        lambda *r: project_kernel(groups, ni, *r),
        [S((rows // 4, cols // 4, cw), BF)],
        [VM] * (ni + 2),
        name="project",
    )(keep, att, *whole)
    return (fine_skip, coarse_out)


def solution(mesh):
    inner = mesh.shape["inner"]
    heads = 16 // inner
    devices = mesh.devices.reshape(heads, mesh.shape["outer"] // heads, inner)
    return jax.shard_map(
        body,
        mesh=jax.sharding.Mesh(devices, OUTER + ("inner",)),
        in_specs=(
            P(OUTER, "inner", None),
            P(),
            P(),
            P(),
            P(),
            P(),
            P(),
            P(None, "inner"),
            P("inner", None),
        ),
        out_specs=(P(OUTER, "inner", None), P(OUTER, "inner", None)),
        check_vma=False,
    )
```

```python
import math

import jax
import jax.numpy as jnp
from jax import lax
from jax.experimental import pallas as pl
from jax.experimental.pallas import tpu as pltpu
from jax.sharding import PartitionSpec as P

HD = 64
WIN = 3
BLOCK = 8
SPAN = 16
STAGE = 6
EARLY = 1
BF = jnp.bfloat16
F32 = jnp.float32
VM = pl.BlockSpec(memory_space=pltpu.VMEM)
HB = pl.BlockSpec(memory_space=pl.ANY)
HM = pl.BlockSpec(memory_space=pltpu.HBM)
MIB = 1024 * 1024
OUTER = ("head", "sub")


def embed(timestep, width):
    half = width // 2
    freq = jnp.exp(-math.log(10000.0) * jnp.arange(half, dtype=F32) / half)
    angle = timestep.astype(F32)[0] * freq
    return jnp.concatenate([jnp.cos(angle), jnp.sin(angle)]).astype(BF)[None, :]


def layer_norm(x, scale, shift):
    mean = jnp.mean(x, axis=-1, keepdims=True)
    var = jnp.mean((x - mean) * (x - mean), axis=-1, keepdims=True)
    return ((x - mean) * lax.rsqrt(var + 1e-06) * (1.0 + scale) + shift).astype(BF)


def mm(a, b):
    return jnp.dot(a, b, preferred_element_type=F32)


def mm_t(a, b):
    return lax.dot_general(a, b, (((1,), (1,)), ((), ())), preferred_element_type=F32)


def shifted(x):
    rows, cols, width = x.shape
    left = jnp.zeros((rows, WIN, width), F32)
    right = jnp.zeros((rows, BLOCK - WIN, width), F32)
    return jnp.concatenate([left, x, right], axis=1)


def key_values(x, mod_ref, w_ref):
    rows, cols, width = x.shape
    flat = x.reshape(rows * cols, width)
    n = layer_norm(flat, mod_ref[:, :width], mod_ref[:, width : 2 * width])
    return mm(n, w_ref[...]).reshape(rows, cols, 2 * width)


def place(axes):
    at = 0
    for axis in axes:
        at = at * lax.axis_size(axis) + lax.axis_index(axis)
    return at


def sides(far_ref, near_ref):
    odd = jnp.broadcast_to(place(OUTER) % 2, far_ref.shape) == 1
    far, near = far_ref[...].astype(F32), near_ref[...].astype(F32)
    return jnp.where(odd, near, far), jnp.where(odd, far, near)


def columns_kernel(far_ref, near_ref, tok_ref, chip_ref, link_ref):
    cols, width = tok_ref.shape[1:]
    half = BLOCK // 2
    strips = []
    for at, lead in ((cols - 2 * BLOCK, 2 * BLOCK - WIN), (0, 0)):
        chunk = pl.ds(at, 2 * BLOCK)
        north, south = sides(far_ref.at[:, chunk], near_ref.at[:, chunk])
        x = jnp.concatenate([north, tok_ref[:, chunk].astype(F32), south], axis=0)
        x = jnp.concatenate([x[:, lead : lead + WIN], x[:, : half - WIN]], axis=1)
        strips.append(jnp.concatenate([x[:, :, k : k + width // 2] for k in (0, width // 2)], axis=1))
    odd = jnp.broadcast_to(lax.axis_index("inner") % 2, strips[0].shape) == 1
    chip_ref[...] = jnp.where(odd, strips[1], strips[0]).astype(BF)
    link_ref[...] = jnp.where(odd, strips[0], strips[1]).astype(BF)


def strip_columns(x, lead):
    half = BLOCK // 2
    x = jnp.concatenate([x[:, :half], x[:, half:]], axis=2)[:, :WIN]
    zero = jnp.zeros((x.shape[0], BLOCK, x.shape[2]), F32)
    parts = [zero[:, :lead]] * (lead > 0) + [x, zero[:, lead + WIN :]]
    return jnp.concatenate(parts, axis=1)


def own_kernel(
    mod_ref, tok_ref, w_ref, out_ref, q_ref, kv_ref, bias_ref, kvw_ref, outw_ref
):
    kvw_ref[...] = w_ref[:, tok_ref.shape[2] :]
    outw_ref[...] = out_ref[...]
    rows, cols, width = tok_ref.shape
    tok = tok_ref[...].astype(F32)
    fscale, fshift = mod_ref[:, :width], mod_ref[:, width : 2 * width]
    n = layer_norm(tok.reshape(rows * cols, width), fscale, fshift)
    q = mm(n, w_ref[:, :width]).astype(BF).astype(F32) * (1.0 / math.sqrt(HD))
    q_ref[...] = q.reshape(rows, cols, width)
    kv_ref[...] = key_values(shifted(tok), mod_ref, kvw_ref)

    nq, nk = bias_ref.shape
    per = rows * BLOCK
    band, bands = place(OUTER), lax.axis_size(OUTER)
    lo = jnp.where(band == 0, WIN, 0)
    hi = jnp.where(band == bands - 1, rows + WIN, rows + 2 * WIN)
    qi = lax.broadcasted_iota(jnp.int32, (nq, nk), 0) % per
    ki = lax.broadcasted_iota(jnp.int32, (nq, nk), 1)
    kr, kc = ki // SPAN, ki % SPAN
    dr, dc = kr - qi // BLOCK, kc - qi % BLOCK
    ok = (dr >= 0) & (dr <= 2 * WIN) & (dc >= 0) & (dc <= 2 * WIN) & (kr >= lo) & (kr < hi)
    bias_ref[...] = jnp.where(ok, 0.0, -1e30).astype(F32)


def order_kernel(cin_ref, skip_ref, cw_ref, order_ref, keep_ref, skip_hbm, sem):
    copy_skip = pltpu.make_async_copy(skip_ref, skip_hbm, sem)
    copy_skip.start()
    keep_ref[...] = cin_ref[...]
    groups = cw_ref.shape[1] // (3 * HD)
    kvs, qs = [], []
    for h in range(groups):
        qs.append(cw_ref[:, h * 3 * HD : h * 3 * HD + HD].astype(F32))
        kvs.append(cw_ref[:, h * 3 * HD + HD : (h + 1) * 3 * HD].astype(F32))
    order_ref[...] = jnp.concatenate(kvs + qs, axis=1).astype(BF)
    copy_skip.wait()


def attend(q_ref, wins, bias_ref, outw_ref, blocks):
    rows, cols, width = q_ref.shape
    heads, nq = width // HD, rows * BLOCK
    lane_head = lax.broadcasted_iota(jnp.int32, (nq, width), 1) // HD
    kvs, scores = [], []
    for j, win in zip(blocks, wins):
        qb = q_ref[:, j * BLOCK : (j + 1) * BLOCK, :].reshape(nq, width)
        qs = jnp.concatenate([jnp.where(lane_head == h, qb, 0.0) for h in range(heads)], axis=0)
        kvs.append(win.reshape(win.shape[0] * SPAN, 2 * width).astype(BF))
        scores.append(mm_t(qs.astype(BF), kvs[-1][:, :width]) + bias_ref[...])
    ps = [jnp.exp(s - jnp.max(s, axis=1, keepdims=True)) for s in scores]
    outs = [mm(p.astype(BF), kv[:, width:]) for p, kv in zip(ps, kvs)]
    atts = []
    for p, o in zip(ps, outs):
        o = o / jnp.sum(p, axis=1, keepdims=True)
        att = o[:nq]
        for h in range(1, heads):
            att = jnp.where(lane_head == h, o[h * nq : (h + 1) * nq], att)
        atts.append(att.astype(BF))
    proj = mm(jnp.concatenate(atts, axis=0), outw_ref[...])
    return [proj[i * nq : (i + 1) * nq].reshape(rows, BLOCK, width) for i in range(len(atts))]


def inner_kernel(
    mod_ref,
    far_ref,
    near_ref,
    w_ref,
    outw_ref,
    q_ref,
    kv_ref,
    bias_ref,
    nkv_ref,
    skv_ref,
    res_ref,
):
    north, south = sides(far_ref, near_ref)
    nkv_ref[...] = key_values(shifted(north), mod_ref, w_ref)
    skv_ref[...] = key_values(shifted(south), mod_ref, w_ref)
    cols = q_ref.shape[1]
    for lead in range(1, cols // BLOCK - 1, STAGE):
        blocks = range(lead, min(lead + STAGE, cols // BLOCK - 1))
        wins = [
            jnp.concatenate(
                [r[:, j * BLOCK : j * BLOCK + SPAN, :] for r in (nkv_ref, kv_ref, skv_ref)], axis=0
            )
            for j in blocks
        ]
        for j, proj in zip(blocks, attend(q_ref, wins, bias_ref, outw_ref, blocks)):
            res_ref[:, j * BLOCK : (j + 1) * BLOCK, :] = proj


def edge_kernel(
    mod_ref,
    chip_ref,
    link_ref,
    tok_ref,
    w_ref,
    outw_ref,
    q_ref,
    kv_ref,
    bias_ref,
    nkv_ref,
    skv_ref,
    res_ref,
    one_ref,
    two_ref,
    skip_ref,
    cin_ref,
    lane_ref,
):
    rows, cols, width = tok_ref.shape
    side = lax.broadcasted_iota(jnp.int32, (rows + 2 * WIN, BLOCK, 2 * width), 1)
    kvs = (nkv_ref, kv_ref, skv_ref)

    def tile(at):
        return jnp.concatenate([r[:, at : at + BLOCK, :] for r in kvs], axis=0)

    odd = jnp.broadcast_to(lax.axis_index("inner") % 2, chip_ref.shape) == 1
    chip, link = chip_ref[...].astype(F32), link_ref[...].astype(F32)
    west, east = jnp.where(odd, chip, link), jnp.where(odd, link, chip)
    strips = [strip_columns(west, 0), strip_columns(east, WIN)]
    strips = key_values(jnp.concatenate(strips, axis=0), mod_ref, w_ref)
    wkv, ekv = strips[: rows + 2 * WIN], strips[rows + 2 * WIN :]
    first = jnp.concatenate([jnp.where(side < WIN, wkv, tile(0)), tile(BLOCK)], axis=1)
    last = jnp.concatenate([tile(cols - BLOCK), jnp.where(side >= WIN, ekv, tile(cols))], axis=1)
    tok = tok_ref[...].astype(F32)
    ends = (0, cols // BLOCK - 1)
    low, high = attend(q_ref, [first, last], bias_ref, outw_ref, ends)
    proj = jnp.concatenate([low, res_ref[:, BLOCK : cols - BLOCK, :], high], axis=1)
    res = (proj + tok).astype(BF)
    skip_ref[...] = res
    for k in range(width // 128):
        lane_ref[k, :, :cols, :] = res[:, :, k * 128 : (k + 1) * 128].astype(F32)

    groups = []
    for a in range(2):
        for b in range(2):
            parts = []
            for dr in range(2):
                for dc in range(2):
                    r, c = 2 * a + dr, 2 * b + dc
                    for k in range(width // 128):
                        strips = [
                            lane_ref[k, rr, pl.ds(c, cols // 4, stride=4), :]
                            for rr in range(r, rows, 4)
                        ]
                        parts.append(jnp.concatenate(strips, axis=0))
            groups.append(jnp.concatenate(parts, axis=1))
    count = (rows // 4) * (cols // 4)
    mid = mm(jnp.concatenate(groups, axis=0).astype(BF), one_ref[...]).astype(BF)
    mid = jnp.concatenate([mid[g * count : (g + 1) * count] for g in range(4)], axis=1)
    cin_ref[...] = mm(mid, two_ref[...]).astype(BF)


def halves(low, high, swap_low):
    lane = lax.broadcasted_iota(jnp.int32, low.shape, 1)
    if swap_low:
        return jnp.where(lane < HD, pltpu.roll(low, HD, 1), high)
    return jnp.where(lane < HD, low, pltpu.roll(high, HD, 1))


def qkv_kernel(groups, mod_ref, *refs):
    xs, w_ref, out_refs = refs[: -1 - groups], refs[-1 - groups], refs[-groups:]
    x = jnp.concatenate([r[...] for r in xs], axis=0)
    at = mod_ref.shape[1] - 2 * x.shape[1]
    scale, shift = mod_ref[:, at : at + x.shape[1]], mod_ref[:, at + x.shape[1] :]
    y = mm(layer_norm(x.astype(F32), scale, shift), w_ref[...])
    half = x.shape[0] // 2
    zi = lax.axis_index("head")
    pieces = []
    for h in range(groups):
        kv = y[:, h * 2 * HD : (h + 1) * 2 * HD]
        if groups % 2:
            q = y[:, groups * 2 * HD + h * HD : groups * 2 * HD + (h + 1) * HD]
            qp = jnp.concatenate([q[:half], q[half:]], axis=1)
        else:
            at = groups * 2 * HD + (h // 2) * 2 * HD
            pair = y[:, at : at + 2 * HD]
            qp = halves(pair[:half], pair[half:], h % 2 == 1)
        pieces.append(jnp.concatenate([kv, qp * (1.0 / math.sqrt(HD))], axis=0).astype(BF))
    for g in range(groups):
        for h in range(groups):

            @pl.when(zi == g ^ h)
            def _(g=g, h=h):
                out_refs[g][...] = pieces[h]


def queries(own):
    band = own[0].shape[0] * 2 // 3
    half = band // 2
    lane = lax.broadcasted_iota(jnp.int32, (half, 2 * HD), 1)
    qs = []
    for r in own:
        qp = r[band:, :].astype(F32)
        qs.append(jnp.where(lane < HD, qp, 0.0))
        qs.append(jnp.where(lane < HD, pltpu.roll(qp, HD, 1), 0.0))
    return jnp.concatenate(qs, axis=0).astype(BF)


def values(kv):
    lane = lax.broadcasted_iota(jnp.int32, kv.shape, 1)
    return jnp.where(lane < HD, jnp.ones_like(kv), kv)


def near_kernel(groups, *refs):
    own, others, (acc_ref, max_ref) = refs[:groups], refs[groups:-2], refs[-2:]
    band = own[0].shape[0] * 2 // 3
    kv = jnp.concatenate([r[:band, :] for r in own] + [r[...] for r in others], axis=0)
    s = mm_t(queries(own), kv)
    top = jnp.max(s, axis=1, keepdims=True)
    p = jnp.exp(s - top)
    acc_ref[...] = mm(p.astype(BF), values(kv))
    max_ref[...] = jnp.broadcast_to(top, max_ref.shape)


def far_kernel(steps, parts, *refs):
    groups = len(steps)
    own, others = refs[:groups], refs[groups:-3]
    acc_ref, max_ref, out_ref = refs[-3:]
    kv = jnp.concatenate([r[...] for r in others], axis=0)
    s = mm_t(queries(own), kv)
    before = max_ref[...]
    top = jnp.maximum(before[:, :1], jnp.max(s, axis=1, keepdims=True))
    p = jnp.exp(s - top)
    acc = acc_ref[...] * jnp.exp(before - top) + mm(p.astype(BF), values(kv))
    count = acc.shape[0] // (groups * parts)
    zi, ii = lax.axis_index("head"), lax.axis_index("inner")
    for g in range(groups):
        for k in range(parts):
            at = (g * parts + k) * count
            low, high = acc[at : at + count // 2], acc[at + count // 2 : at + count]
            block = halves(low, high, True) / halves(low, high, False)
            out_ref[(zi ^ steps[g]) * parts + (ii ^ k)] = block.astype(BF)


def project_kernel(groups, parts, cin_ref, att_ref, *refs):
    ws, out_ref = refs[:-1], refs[-1]
    ii = lax.axis_index("inner")
    total = cin_ref[...].astype(F32)
    for k in range(parts):
        xs = [att_ref[g * parts + (ii ^ k)].astype(F32) for g in range(groups)]
        if groups % 2:
            cols = [jnp.concatenate([x[:, :HD], x[:, HD:]], axis=0) for x in xs]
        else:
            cols = [
                jnp.concatenate([halves(a, b, False), halves(a, b, True)], axis=0)
                for a, b in zip(xs[::2], xs[1::2])
            ]
        total = total + mm(jnp.concatenate(cols, axis=1).astype(BF), ws[k][...])
    out_ref[...] = total.astype(BF).reshape(out_ref.shape)


def call(kernel, out, in_specs, scratch=(), out_specs=None, limit=12, flops=None, name=None):
    cost = flops and pl.CostEstimate(flops=flops, bytes_accessed=MIB, transcendentals=0)
    return pl.pallas_call(
        kernel,
        out_shape=out,
        in_specs=in_specs,
        out_specs=[VM for _ in out] if out_specs is None else out_specs,
        scratch_shapes=list(scratch),
        compiler_params=pltpu.CompilerParams(vmem_limit_bytes=limit * MIB),
        cost_estimate=cost,
        name=name,
    )


def swap(x, axis, step):
    size = lax.axis_size(axis)
    return lax.ppermute(x, axis, [(i, i ^ step) for i in range(size)])


def body(
    tokens,
    timestep,
    mod_weight,
    fine_qkv_weight,
    fine_out_weight,
    merge_one,
    merge_two,
    coarse_qkv_weight,
    coarse_out_weight,
):
    S = jax.ShapeDtypeStruct
    rows, cols, width = tokens.shape
    cw = merge_two.shape[1]
    no, ni = lax.axis_size(OUTER), lax.axis_size("inner")
    odd = lax.axis_index(OUTER) % 2 == 1
    bottom, top = tokens[rows - WIN :], tokens[:WIN]
    pairs = []
    for i in range(no * ni):
        band, column = i // ni, i % ni
        if band in (0, no - 1):
            pairs.append((i, band * ni + (column ^ 1)))
        else:
            pairs.append((i, i + ni if band % 2 else i - ni))
    far = lax.ppermute(jnp.where(odd, bottom, top), OUTER + ("inner",), pairs)
    near = swap(jnp.where(odd, top, bottom), OUTER, 1)

    emb = embed(timestep, mod_weight.shape[0])
    mod = mm(emb, mod_weight)
    tall = rows + 2 * WIN
    heads = width // HD
    q, kv, bias, kvw, outw = call(
        own_kernel,
        [
            S((rows, cols, width), F32),
            S((rows, cols + BLOCK, 2 * width), F32),
            S((heads * rows * BLOCK, tall * SPAN), F32),
            S((width, 2 * width), BF),
            S((width, width), BF),
        ],
        [VM] * 4,
        limit=16,
        flops=1000000000,
        name="own",
    )(mod, tokens, fine_qkv_weight, fine_out_weight)

    strip = S((tall, BLOCK, width // 2), BF)
    chip, link = call(columns_kernel, [strip] * 2, [VM] * 3, name="columns")(
        far, near, tokens
    )
    chip = swap(chip, "inner", 1)
    link = lax.ppermute(link, "inner", [(i, (i + (1 if i % 2 else -1)) % ni) for i in range(ni)])
    nkv, skv, res = call(
        inner_kernel,
        [S((WIN, cols + BLOCK, 2 * width), F32)] * 2 + [S((rows, cols, width), F32)],
        [VM] * 8,
        limit=16,
        flops=1000000000,
        name="inside",
    )(mod, far, near, kvw, outw, q, kv, bias)
    count = (rows // 4) * (cols // 4)
    skip, coarse_in = call(
        edge_kernel,
        [S(tokens.shape, BF), S((count, cw), BF)],
        [VM] * 14,
        scratch=[
            pltpu.VMEM((width // 128, rows, cols + BLOCK, 128), F32),
        ],
        limit=20,
        name="edge",
    )(
        mod, chip, link, tokens, kvw, outw, q, kv, bias, nkv, skv, res, merge_one, merge_two
    )

    groups = coarse_qkv_weight.shape[1] // (3 * HD)
    sub = no // groups
    band = ni * count
    order, keep, fine_skip = call(
        order_kernel,
        [S(coarse_qkv_weight.shape, BF), S(coarse_in.shape, BF), S(tokens.shape, BF)],
        [VM] * 3,
        scratch=[pltpu.SemaphoreType.DMA],
        out_specs=[VM, VM, HB],
        flops=1000000000,
        name="order",
    )(coarse_in, skip, coarse_qkv_weight)
    gathered, step = [coarse_in], ni // 2
    beside = swap(coarse_in, "inner", 1)
    while step > 1:
        gathered = [w for x in gathered for w in (x, swap(x, "inner", step))]
        step //= 2
    weight, order, beside, gathered[1] = lax.optimization_barrier((coarse_out_weight, order, beside, gathered[1]))
    gathered = [w for x in gathered for w in (x, beside if x is coarse_in else swap(x, "inner", 1))]
    step = ni // 2
    whole = [weight, swap(weight, "inner", step)]
    pieces = call(
        lambda *r: qkv_kernel(groups, *r),
        [S((band + band // 2, 2 * HD), BF)] * groups,
        [VM] * (ni + 2),
        name="qkv",
    )(mod, *gathered, order)
    steps = [0] + list(range(groups - 1, 0, -1))
    own = [swap(pieces[g], OUTER, g * sub) if g else pieces[0] for g in steps]
    aside = swap(weight, "inner", 1)
    held = [own[0][:band]]
    if groups > 1:
        held.append(jnp.concatenate([p[:band] for p in own[1:]], axis=0))
    others = [swap(p, OUTER, k) for k in range(1, sub) for p in held]
    aside, others[0] = lax.optimization_barrier((aside, others[0]))
    acc, top = call(
        lambda *r: near_kernel(groups, *r),
        [S((groups * band, 2 * HD), F32)] * 2,
        [VM] * (groups + EARLY),
        limit=16,
        flops=1000000000,
        name="near",
    )(*own, *others[:EARLY])
    others = others[EARLY:]
    att = call(
        lambda *r: far_kernel(steps, ni, *r),
        [S((groups * ni, count // 2, 2 * HD), BF)],
        [VM] * (groups + len(others) + 2),
        limit=16 if no * band <= 1024 else 56,
        name="far",
    )(*own, *others, acc, top)
    far_weight, att = lax.optimization_barrier((whole[1], att))
    whole[1] = far_weight
    while step > 1:
        step //= 2
        whole = [w for x in whole for w in (x, aside if step == 1 and x is weight else swap(x, "inner", step))]
    att = lax.all_to_all(att[0], ("head", "inner"), 0, 0, tiled=True)
    (coarse_out,) = call(
        lambda *r: project_kernel(groups, ni, *r),
        [S((rows // 4, cols // 4, cw), BF)],
        [VM] * (ni + 2),
        name="project",
    )(keep, att, *whole)
    return (fine_skip, coarse_out)


def solution(mesh):
    inner = mesh.shape["inner"]
    heads = 16 // inner
    devices = mesh.devices.reshape(heads, mesh.shape["outer"] // heads, inner)
    return jax.shard_map(
        body,
        mesh=jax.sharding.Mesh(devices, OUTER + ("inner",)),
        in_specs=(
            P(OUTER, "inner", None),
            P(),
            P(),
            P(),
            P(),
            P(),
            P(),
            P(None, "inner"),
            P("inner", None),
        ),
        out_specs=(P(OUTER, "inner", None), P(OUTER, "inner", None)),
        check_vma=False,
    )
```

```python
import math

import jax
import jax.numpy as jnp
from jax import lax
from jax.experimental import pallas as pl
from jax.experimental.pallas import tpu as pltpu
from jax.sharding import PartitionSpec as P

HD = 64
WIN = 3
BLOCK = 8
SPAN = 16
STAGE = 6
EARLY = 1
BF = jnp.bfloat16
F32 = jnp.float32
VM = pl.BlockSpec(memory_space=pltpu.VMEM)
HB = pl.BlockSpec(memory_space=pl.ANY)
HM = pl.BlockSpec(memory_space=pltpu.HBM)
MIB = 1024 * 1024
OUTER = ("head", "sub")


def embed(timestep, width):
    half = width // 2
    freq = jnp.exp(-math.log(10000.0) * jnp.arange(half, dtype=F32) / half)
    angle = timestep.astype(F32)[0] * freq
    return jnp.concatenate([jnp.cos(angle), jnp.sin(angle)]).astype(BF)[None, :]


def layer_norm(x, scale, shift):
    mean = jnp.mean(x, axis=-1, keepdims=True)
    var = jnp.mean((x - mean) * (x - mean), axis=-1, keepdims=True)
    return ((x - mean) * lax.rsqrt(var + 1e-06) * (1.0 + scale) + shift).astype(BF)


def mm(a, b):
    return jnp.dot(a, b, preferred_element_type=F32)


def mm_t(a, b):
    return lax.dot_general(a, b, (((1,), (1,)), ((), ())), preferred_element_type=F32)


def shifted(x):
    rows, cols, width = x.shape
    left = jnp.zeros((rows, WIN, width), F32)
    right = jnp.zeros((rows, BLOCK - WIN, width), F32)
    return jnp.concatenate([left, x, right], axis=1)


def key_values(x, mod_ref, w_ref):
    rows, cols, width = x.shape
    flat = x.reshape(rows * cols, width)
    n = layer_norm(flat, mod_ref[:, :width], mod_ref[:, width : 2 * width])
    return mm(n, w_ref[...]).reshape(rows, cols, 2 * width)


def place(axes):
    at = 0
    for axis in axes:
        at = at * lax.axis_size(axis) + lax.axis_index(axis)
    return at


def sides(far_ref, near_ref):
    odd = jnp.broadcast_to(place(OUTER) % 2, far_ref.shape) == 1
    far, near = far_ref[...].astype(F32), near_ref[...].astype(F32)
    return jnp.where(odd, near, far), jnp.where(odd, far, near)


def columns_kernel(far_ref, near_ref, tok_ref, chip_ref, link_ref):
    cols, width = tok_ref.shape[1:]
    half = BLOCK // 2
    strips = []
    for at, lead in ((cols - 2 * BLOCK, 2 * BLOCK - WIN), (0, 0)):
        chunk = pl.ds(at, 2 * BLOCK)
        north, south = sides(far_ref.at[:, chunk], near_ref.at[:, chunk])
        x = jnp.concatenate([north, tok_ref[:, chunk].astype(F32), south], axis=0)
        x = jnp.concatenate([x[:, lead : lead + WIN], x[:, : half - WIN]], axis=1)
        strips.append(jnp.concatenate([x[:, :, k : k + width // 2] for k in (0, width // 2)], axis=1))
    odd = jnp.broadcast_to(lax.axis_index("inner") % 2, strips[0].shape) == 1
    chip_ref[...] = jnp.where(odd, strips[1], strips[0]).astype(BF)
    link_ref[...] = jnp.where(odd, strips[0], strips[1]).astype(BF)


def strip_columns(x, lead):
    half = BLOCK // 2
    x = jnp.concatenate([x[:, :half], x[:, half:]], axis=2)[:, :WIN]
    zero = jnp.zeros((x.shape[0], BLOCK, x.shape[2]), F32)
    parts = [zero[:, :lead]] * (lead > 0) + [x, zero[:, lead + WIN :]]
    return jnp.concatenate(parts, axis=1)


def own_kernel(
    mod_ref, tok_ref, w_ref, out_ref, q_ref, kv_ref, bias_ref, kvw_ref, outw_ref
):
    kvw_ref[...] = w_ref[:, tok_ref.shape[2] :]
    outw_ref[...] = out_ref[...]
    rows, cols, width = tok_ref.shape
    tok = tok_ref[...].astype(F32)
    fscale, fshift = mod_ref[:, :width], mod_ref[:, width : 2 * width]
    n = layer_norm(tok.reshape(rows * cols, width), fscale, fshift)
    q = mm(n, w_ref[:, :width]).astype(BF).astype(F32) * (1.0 / math.sqrt(HD))
    q_ref[...] = q.reshape(rows, cols, width)
    kv_ref[...] = key_values(shifted(tok), mod_ref, kvw_ref)

    nq, nk = bias_ref.shape
    per = rows * BLOCK
    band, bands = place(OUTER), lax.axis_size(OUTER)
    lo = jnp.where(band == 0, WIN, 0)
    hi = jnp.where(band == bands - 1, rows + WIN, rows + 2 * WIN)
    qi = lax.broadcasted_iota(jnp.int32, (nq, nk), 0) % per
    ki = lax.broadcasted_iota(jnp.int32, (nq, nk), 1)
    kr, kc = ki // SPAN, ki % SPAN
    dr, dc = kr - qi // BLOCK, kc - qi % BLOCK
    ok = (dr >= 0) & (dr <= 2 * WIN) & (dc >= 0) & (dc <= 2 * WIN) & (kr >= lo) & (kr < hi)
    bias_ref[...] = jnp.where(ok, 0.0, -1e30).astype(F32)


def order_kernel(cin_ref, skip_ref, cw_ref, order_ref, keep_ref, skip_hbm, sem):
    copy_skip = pltpu.make_async_copy(skip_ref, skip_hbm, sem)
    copy_skip.start()
    keep_ref[...] = cin_ref[...]
    groups = cw_ref.shape[1] // (3 * HD)
    kvs, qs = [], []
    for h in range(groups):
        qs.append(cw_ref[:, h * 3 * HD : h * 3 * HD + HD].astype(F32))
        kvs.append(cw_ref[:, h * 3 * HD + HD : (h + 1) * 3 * HD].astype(F32))
    order_ref[...] = jnp.concatenate(kvs + qs, axis=1).astype(BF)
    copy_skip.wait()


def attend(q_ref, wins, bias_ref, outw_ref, blocks):
    rows, cols, width = q_ref.shape
    heads, nq = width // HD, rows * BLOCK
    lane_head = lax.broadcasted_iota(jnp.int32, (nq, width), 1) // HD
    kvs, scores = [], []
    for j, win in zip(blocks, wins):
        qb = q_ref[:, j * BLOCK : (j + 1) * BLOCK, :].reshape(nq, width)
        qs = jnp.concatenate([jnp.where(lane_head == h, qb, 0.0) for h in range(heads)], axis=0)
        kvs.append(win.reshape(win.shape[0] * SPAN, 2 * width).astype(BF))
        scores.append(mm_t(qs.astype(BF), kvs[-1][:, :width]) + bias_ref[...])
    ps = [jnp.exp(s - jnp.max(s, axis=1, keepdims=True)) for s in scores]
    outs = [mm(p.astype(BF), kv[:, width:]) for p, kv in zip(ps, kvs)]
    atts = []
    for p, o in zip(ps, outs):
        o = o / jnp.sum(p, axis=1, keepdims=True)
        att = o[:nq]
        for h in range(1, heads):
            att = jnp.where(lane_head == h, o[h * nq : (h + 1) * nq], att)
        atts.append(att.astype(BF))
    proj = mm(jnp.concatenate(atts, axis=0), outw_ref[...])
    return [proj[i * nq : (i + 1) * nq].reshape(rows, BLOCK, width) for i in range(len(atts))]


def inner_kernel(
    mod_ref,
    far_ref,
    near_ref,
    w_ref,
    outw_ref,
    q_ref,
    kv_ref,
    bias_ref,
    nkv_ref,
    skv_ref,
    res_ref,
):
    north, south = sides(far_ref, near_ref)
    nkv_ref[...] = key_values(shifted(north), mod_ref, w_ref)
    skv_ref[...] = key_values(shifted(south), mod_ref, w_ref)
    cols = q_ref.shape[1]
    for lead in range(1, cols // BLOCK - 1, STAGE):
        blocks = range(lead, min(lead + STAGE, cols // BLOCK - 1))
        wins = [
            jnp.concatenate(
                [r[:, j * BLOCK : j * BLOCK + SPAN, :] for r in (nkv_ref, kv_ref, skv_ref)], axis=0
            )
            for j in blocks
        ]
        for j, proj in zip(blocks, attend(q_ref, wins, bias_ref, outw_ref, blocks)):
            res_ref[:, j * BLOCK : (j + 1) * BLOCK, :] = proj


def edge_kernel(
    mod_ref,
    chip_ref,
    link_ref,
    tok_ref,
    w_ref,
    outw_ref,
    q_ref,
    kv_ref,
    bias_ref,
    nkv_ref,
    skv_ref,
    res_ref,
    one_ref,
    two_ref,
    skip_ref,
    cin_ref,
    lane_ref,
):
    rows, cols, width = tok_ref.shape
    side = lax.broadcasted_iota(jnp.int32, (rows + 2 * WIN, BLOCK, 2 * width), 1)
    kvs = (nkv_ref, kv_ref, skv_ref)

    def tile(at):
        return jnp.concatenate([r[:, at : at + BLOCK, :] for r in kvs], axis=0)

    odd = jnp.broadcast_to(lax.axis_index("inner") % 2, chip_ref.shape) == 1
    chip, link = chip_ref[...].astype(F32), link_ref[...].astype(F32)
    west, east = jnp.where(odd, chip, link), jnp.where(odd, link, chip)
    strips = [strip_columns(west, 0), strip_columns(east, WIN)]
    strips = key_values(jnp.concatenate(strips, axis=0), mod_ref, w_ref)
    wkv, ekv = strips[: rows + 2 * WIN], strips[rows + 2 * WIN :]
    first = jnp.concatenate([jnp.where(side < WIN, wkv, tile(0)), tile(BLOCK)], axis=1)
    last = jnp.concatenate([tile(cols - BLOCK), jnp.where(side >= WIN, ekv, tile(cols))], axis=1)
    tok = tok_ref[...].astype(F32)
    ends = (0, cols // BLOCK - 1)
    low, high = attend(q_ref, [first, last], bias_ref, outw_ref, ends)
    proj = jnp.concatenate([low, res_ref[:, BLOCK : cols - BLOCK, :], high], axis=1)
    res = (proj + tok).astype(BF)
    skip_ref[...] = res
    for k in range(width // 128):
        lane_ref[k, :, :cols, :] = res[:, :, k * 128 : (k + 1) * 128].astype(F32)

    groups = []
    for a in range(2):
        for b in range(2):
            parts = []
            for dr in range(2):
                for dc in range(2):
                    r, c = 2 * a + dr, 2 * b + dc
                    for k in range(width // 128):
                        strips = [
                            lane_ref[k, rr, pl.ds(c, cols // 4, stride=4), :]
                            for rr in range(r, rows, 4)
                        ]
                        parts.append(jnp.concatenate(strips, axis=0))
            groups.append(jnp.concatenate(parts, axis=1))
    count = (rows // 4) * (cols // 4)
    mid = mm(jnp.concatenate(groups, axis=0).astype(BF), one_ref[...]).astype(BF)
    mid = jnp.concatenate([mid[g * count : (g + 1) * count] for g in range(4)], axis=1)
    cin_ref[...] = mm(mid, two_ref[...]).astype(BF)


def halves(low, high, swap_low):
    lane = lax.broadcasted_iota(jnp.int32, low.shape, 1)
    if swap_low:
        return jnp.where(lane < HD, pltpu.roll(low, HD, 1), high)
    return jnp.where(lane < HD, low, pltpu.roll(high, HD, 1))


def qkv_kernel(groups, mod_ref, *refs):
    xs, w_ref, out_refs = refs[: -1 - groups], refs[-1 - groups], refs[-groups:]
    x = jnp.concatenate([r[...] for r in xs], axis=0)
    at = mod_ref.shape[1] - 2 * x.shape[1]
    scale, shift = mod_ref[:, at : at + x.shape[1]], mod_ref[:, at + x.shape[1] :]
    y = mm(layer_norm(x.astype(F32), scale, shift), w_ref[...])
    half = x.shape[0] // 2
    zi = lax.axis_index("head")
    pieces = []
    for h in range(groups):
        kv = y[:, h * 2 * HD : (h + 1) * 2 * HD]
        if groups % 2:
            q = y[:, groups * 2 * HD + h * HD : groups * 2 * HD + (h + 1) * HD]
            qp = jnp.concatenate([q[:half], q[half:]], axis=1)
        else:
            at = groups * 2 * HD + (h // 2) * 2 * HD
            pair = y[:, at : at + 2 * HD]
            qp = halves(pair[:half], pair[half:], h % 2 == 1)
        pieces.append(jnp.concatenate([kv, qp * (1.0 / math.sqrt(HD))], axis=0).astype(BF))
    for g in range(groups):
        for h in range(groups):

            @pl.when(zi == g ^ h)
            def _(g=g, h=h):
                out_refs[g][...] = pieces[h]


def queries(own):
    band = own[0].shape[0] * 2 // 3
    half = band // 2
    lane = lax.broadcasted_iota(jnp.int32, (half, 2 * HD), 1)
    qs = []
    for r in own:
        qp = r[band:, :].astype(F32)
        qs.append(jnp.where(lane < HD, qp, 0.0))
        qs.append(jnp.where(lane < HD, pltpu.roll(qp, HD, 1), 0.0))
    return jnp.concatenate(qs, axis=0).astype(BF)


def values(kv):
    lane = lax.broadcasted_iota(jnp.int32, kv.shape, 1)
    return jnp.where(lane < HD, jnp.ones_like(kv), kv)


def near_kernel(groups, *refs):
    own, others, (acc_ref, max_ref) = refs[:groups], refs[groups:-2], refs[-2:]
    band = own[0].shape[0] * 2 // 3
    kv = jnp.concatenate([r[:band, :] for r in own] + [r[...] for r in others], axis=0)
    s = mm_t(queries(own), kv)
    top = jnp.max(s, axis=1, keepdims=True)
    p = jnp.exp(s - top)
    acc_ref[...] = mm(p.astype(BF), values(kv))
    max_ref[...] = jnp.broadcast_to(top, max_ref.shape)


def far_kernel(steps, parts, *refs):
    groups = len(steps)
    own, others = refs[:groups], refs[groups:-3]
    acc_ref, max_ref, out_ref = refs[-3:]
    kv = jnp.concatenate([r[...] for r in others], axis=0)
    s = mm_t(queries(own), kv)
    before = max_ref[...]
    top = jnp.maximum(before[:, :1], jnp.max(s, axis=1, keepdims=True))
    p = jnp.exp(s - top)
    acc = acc_ref[...] * jnp.exp(before - top) + mm(p.astype(BF), values(kv))
    count = acc.shape[0] // (groups * parts)
    zi, ii = lax.axis_index("head"), lax.axis_index("inner")
    for g in range(groups):
        for k in range(parts):
            at = (g * parts + k) * count
            low, high = acc[at : at + count // 2], acc[at + count // 2 : at + count]
            block = halves(low, high, True) / halves(low, high, False)
            out_ref[(zi ^ steps[g]) * parts + (ii ^ k)] = block.astype(BF)


def project_kernel(groups, parts, cin_ref, att_ref, *refs):
    ws, (out_hbm, out_ref, sems) = refs[:-3], refs[-3:]
    ii = lax.axis_index("inner")
    rows = []
    for k in range(parts):
        xs = [att_ref[g * parts + (ii ^ k)].astype(F32) for g in range(groups)]
        if groups % 2:
            cols = [jnp.concatenate([x[:, :HD], x[:, HD:]], axis=0) for x in xs]
        else:
            cols = [
                jnp.concatenate([halves(a, b, False), halves(a, b, True)], axis=0)
                for a, b in zip(xs[::2], xs[1::2])
            ]
        rows.append(jnp.concatenate(cols, axis=1).astype(BF))
    width = out_ref.shape[3]
    copies = []
    for n in range(2):
        part = pl.ds(n * width, width)
        total = cin_ref[:, part].astype(F32)
        for k in range(parts):
            total = total + mm(rows[k], ws[k][:, part])
        out_ref[n] = total.astype(BF).reshape(out_ref.shape[1:])
        copies.append(
            pltpu.make_async_copy(out_ref.at[n], out_hbm.at[:, :, part], sems.at[n])
        )
        copies[-1].start()
    for copy in copies:
        copy.wait()


def call(kernel, out, in_specs, scratch=(), out_specs=None, limit=12, flops=None, name=None):
    cost = flops and pl.CostEstimate(flops=flops, bytes_accessed=MIB, transcendentals=0)
    return pl.pallas_call(
        kernel,
        out_shape=out,
        in_specs=in_specs,
        out_specs=[VM for _ in out] if out_specs is None else out_specs,
        scratch_shapes=list(scratch),
        compiler_params=pltpu.CompilerParams(vmem_limit_bytes=limit * MIB),
        cost_estimate=cost,
        name=name,
    )


def swap(x, axis, step):
    size = lax.axis_size(axis)
    return lax.ppermute(x, axis, [(i, i ^ step) for i in range(size)])


def body(
    tokens,
    timestep,
    mod_weight,
    fine_qkv_weight,
    fine_out_weight,
    merge_one,
    merge_two,
    coarse_qkv_weight,
    coarse_out_weight,
):
    S = jax.ShapeDtypeStruct
    rows, cols, width = tokens.shape
    cw = merge_two.shape[1]
    no, ni = lax.axis_size(OUTER), lax.axis_size("inner")
    odd = lax.axis_index(OUTER) % 2 == 1
    bottom, top = tokens[rows - WIN :], tokens[:WIN]
    pairs = []
    for i in range(no * ni):
        band, column = i // ni, i % ni
        if band in (0, no - 1):
            pairs.append((i, band * ni + (column ^ 1)))
        else:
            pairs.append((i, i + ni if band % 2 else i - ni))
    far = lax.ppermute(jnp.where(odd, bottom, top), OUTER + ("inner",), pairs)
    near = swap(jnp.where(odd, top, bottom), OUTER, 1)

    emb = embed(timestep, mod_weight.shape[0])
    mod = mm(emb, mod_weight)
    tall = rows + 2 * WIN
    heads = width // HD
    q, kv, bias, kvw, outw = call(
        own_kernel,
        [
            S((rows, cols, width), F32),
            S((rows, cols + BLOCK, 2 * width), F32),
            S((heads * rows * BLOCK, tall * SPAN), F32),
            S((width, 2 * width), BF),
            S((width, width), BF),
        ],
        [VM] * 4,
        limit=16,
        flops=1000000000,
        name="own",
    )(mod, tokens, fine_qkv_weight, fine_out_weight)

    strip = S((tall, BLOCK, width // 2), BF)
    chip, link = call(columns_kernel, [strip] * 2, [VM] * 3, name="columns")(
        far, near, tokens
    )
    chip = swap(chip, "inner", 1)
    link = lax.ppermute(link, "inner", [(i, (i + (1 if i % 2 else -1)) % ni) for i in range(ni)])
    nkv, skv, res = call(
        inner_kernel,
        [S((WIN, cols + BLOCK, 2 * width), F32)] * 2 + [S((rows, cols, width), F32)],
        [VM] * 8,
        limit=16,
        flops=1000000000,
        name="inside",
    )(mod, far, near, kvw, outw, q, kv, bias)
    count = (rows // 4) * (cols // 4)
    skip, coarse_in = call(
        edge_kernel,
        [S(tokens.shape, BF), S((count, cw), BF)],
        [VM] * 14,
        scratch=[
            pltpu.VMEM((width // 128, rows, cols + BLOCK, 128), F32),
        ],
        limit=20,
        name="edge",
    )(
        mod, chip, link, tokens, kvw, outw, q, kv, bias, nkv, skv, res, merge_one, merge_two
    )

    groups = coarse_qkv_weight.shape[1] // (3 * HD)
    sub = no // groups
    band = ni * count
    order, keep, fine_skip = call(
        order_kernel,
        [S(coarse_qkv_weight.shape, BF), S(coarse_in.shape, BF), S(tokens.shape, BF)],
        [VM] * 3,
        scratch=[pltpu.SemaphoreType.DMA],
        out_specs=[VM, VM, HB],
        flops=1000000000,
        name="order",
    )(coarse_in, skip, coarse_qkv_weight)
    gathered, step = [coarse_in], ni // 2
    beside = swap(coarse_in, "inner", 1)
    while step > 1:
        gathered = [w for x in gathered for w in (x, swap(x, "inner", step))]
        step //= 2
    weight, order, beside, gathered[1] = lax.optimization_barrier((coarse_out_weight, order, beside, gathered[1]))
    gathered = [w for x in gathered for w in (x, beside if x is coarse_in else swap(x, "inner", 1))]
    step = ni // 2
    whole = [weight, swap(weight, "inner", step)]
    pieces = call(
        lambda *r: qkv_kernel(groups, *r),
        [S((band + band // 2, 2 * HD), BF)] * groups,
        [VM] * (ni + 2),
        name="qkv",
    )(mod, *gathered, order)
    steps = [0] + list(range(groups - 1, 0, -1))
    own = [swap(pieces[g], OUTER, g * sub) if g else pieces[0] for g in steps]
    aside = swap(weight, "inner", 1)
    held = [own[0][:band]]
    if groups > 1:
        held.append(jnp.concatenate([p[:band] for p in own[1:]], axis=0))
    others = [swap(p, OUTER, k) for k in range(1, sub) for p in held]
    aside, others[0] = lax.optimization_barrier((aside, others[0]))
    acc, top = call(
        lambda *r: near_kernel(groups, *r),
        [S((groups * band, 2 * HD), F32)] * 2,
        [VM] * (groups + EARLY),
        limit=16,
        flops=1000000000,
        name="near",
    )(*own, *others[:EARLY])
    others = others[EARLY:]
    att = call(
        lambda *r: far_kernel(steps, ni, *r),
        [S((groups * ni, count // 2, 2 * HD), BF)],
        [VM] * (groups + len(others) + 2),
        limit=16 if no * band <= 1024 else 56,
        name="far",
    )(*own, *others, acc, top)
    far_weight, att = lax.optimization_barrier((whole[1], att))
    whole[1] = far_weight
    while step > 1:
        step //= 2
        whole = [w for x in whole for w in (x, aside if step == 1 and x is weight else swap(x, "inner", step))]
    att = lax.all_to_all(att[0], ("head", "inner"), 0, 0, tiled=True)
    (coarse_out,) = call(
        lambda *r: project_kernel(groups, ni, *r),
        [S((rows // 4, cols // 4, cw), BF)],
        [VM] * (ni + 2),
        scratch=[pltpu.VMEM((2, rows // 4, cols // 4, cw // 2), BF), pltpu.SemaphoreType.DMA((2,))],
        out_specs=[HB],
        name="project",
    )(keep, att, *whole)
    return (fine_skip, coarse_out)


def solution(mesh):
    inner = mesh.shape["inner"]
    heads = 16 // inner
    devices = mesh.devices.reshape(heads, mesh.shape["outer"] // heads, inner)
    return jax.shard_map(
        body,
        mesh=jax.sharding.Mesh(devices, OUTER + ("inner",)),
        in_specs=(
            P(OUTER, "inner", None),
            P(),
            P(),
            P(),
            P(),
            P(),
            P(),
            P(None, "inner"),
            P("inner", None),
        ),
        out_specs=(P(OUTER, "inner", None), P(OUTER, "inner", None)),
        check_vma=False,
    )
```

```python
import math

import jax
import jax.numpy as jnp
from jax import lax
from jax.experimental import pallas as pl
from jax.experimental.pallas import tpu as pltpu
from jax.sharding import PartitionSpec as P

HD = 64
WIN = 3
BLOCK = 8
SPAN = 16
STAGE = 6
EARLY = 1
BF = jnp.bfloat16
F32 = jnp.float32
VM = pl.BlockSpec(memory_space=pltpu.VMEM)
HB = pl.BlockSpec(memory_space=pl.ANY)
HM = pl.BlockSpec(memory_space=pltpu.HBM)
MIB = 1024 * 1024
OUTER = ("head", "sub")


def embed(timestep, width):
    half = width // 2
    freq = jnp.exp(-math.log(10000.0) * jnp.arange(half, dtype=F32) / half)
    angle = timestep.astype(F32)[0] * freq
    return jnp.concatenate([jnp.cos(angle), jnp.sin(angle)]).astype(BF)[None, :]


def layer_norm(x, scale, shift):
    mean = jnp.mean(x, axis=-1, keepdims=True)
    var = jnp.mean((x - mean) * (x - mean), axis=-1, keepdims=True)
    return ((x - mean) * lax.rsqrt(var + 1e-06) * (1.0 + scale) + shift).astype(BF)


def mm(a, b):
    return jnp.dot(a, b, preferred_element_type=F32)


def mm_t(a, b):
    return lax.dot_general(a, b, (((1,), (1,)), ((), ())), preferred_element_type=F32)


def shifted(x):
    rows, cols, width = x.shape
    left = jnp.zeros((rows, WIN, width), F32)
    right = jnp.zeros((rows, BLOCK - WIN, width), F32)
    return jnp.concatenate([left, x, right], axis=1)


def key_values(x, mod_ref, w_ref):
    rows, cols, width = x.shape
    flat = x.reshape(rows * cols, width)
    n = layer_norm(flat, mod_ref[:, :width], mod_ref[:, width : 2 * width])
    return mm(n, w_ref[...]).reshape(rows, cols, 2 * width)


def place(axes):
    at = 0
    for axis in axes:
        at = at * lax.axis_size(axis) + lax.axis_index(axis)
    return at


def sides(far_ref, near_ref):
    odd = jnp.broadcast_to(place(OUTER) % 2, far_ref.shape) == 1
    far, near = far_ref[...].astype(F32), near_ref[...].astype(F32)
    return jnp.where(odd, near, far), jnp.where(odd, far, near)


def columns_kernel(far_ref, near_ref, tok_ref, chip_ref, link_ref):
    cols, width = tok_ref.shape[1:]
    half = BLOCK // 2
    strips = []
    for at, lead in ((cols - 2 * BLOCK, 2 * BLOCK - WIN), (0, 0)):
        chunk = pl.ds(at, 2 * BLOCK)
        north, south = sides(far_ref.at[:, chunk], near_ref.at[:, chunk])
        x = jnp.concatenate([north, tok_ref[:, chunk].astype(F32), south], axis=0)
        x = jnp.concatenate([x[:, lead : lead + WIN], x[:, : half - WIN]], axis=1)
        strips.append(jnp.concatenate([x[:, :, k : k + width // 2] for k in (0, width // 2)], axis=1))
    odd = jnp.broadcast_to(lax.axis_index("inner") % 2, strips[0].shape) == 1
    chip_ref[...] = jnp.where(odd, strips[1], strips[0]).astype(BF)
    link_ref[...] = jnp.where(odd, strips[0], strips[1]).astype(BF)


def strip_columns(x, lead):
    half = BLOCK // 2
    x = jnp.concatenate([x[:, :half], x[:, half:]], axis=2)[:, :WIN]
    zero = jnp.zeros((x.shape[0], BLOCK, x.shape[2]), F32)
    parts = [zero[:, :lead]] * (lead > 0) + [x, zero[:, lead + WIN :]]
    return jnp.concatenate(parts, axis=1)


def own_kernel(
    mod_ref, tok_ref, w_ref, out_ref, q_ref, kv_ref, bias_ref, kvw_ref, outw_ref
):
    kvw_ref[...] = w_ref[:, tok_ref.shape[2] :]
    outw_ref[...] = out_ref[...]
    rows, cols, width = tok_ref.shape
    tok = tok_ref[...].astype(F32)
    fscale, fshift = mod_ref[:, :width], mod_ref[:, width : 2 * width]
    n = layer_norm(tok.reshape(rows * cols, width), fscale, fshift)
    q = mm(n, w_ref[:, :width]).astype(BF).astype(F32) * (1.0 / math.sqrt(HD))
    q_ref[...] = q.reshape(rows, cols, width)
    kv_ref[...] = key_values(shifted(tok), mod_ref, kvw_ref)

    nq, nk = bias_ref.shape
    per = rows * BLOCK
    band, bands = place(OUTER), lax.axis_size(OUTER)
    lo = jnp.where(band == 0, WIN, 0)
    hi = jnp.where(band == bands - 1, rows + WIN, rows + 2 * WIN)
    qi = lax.broadcasted_iota(jnp.int32, (nq, nk), 0) % per
    ki = lax.broadcasted_iota(jnp.int32, (nq, nk), 1)
    kr, kc = ki // SPAN, ki % SPAN
    dr, dc = kr - qi // BLOCK, kc - qi % BLOCK
    ok = (dr >= 0) & (dr <= 2 * WIN) & (dc >= 0) & (dc <= 2 * WIN) & (kr >= lo) & (kr < hi)
    bias_ref[...] = jnp.where(ok, 0.0, -1e30).astype(F32)


def order_kernel(cin_ref, skip_ref, cw_ref, order_ref, keep_ref, skip_hbm, sem):
    copy_skip = pltpu.make_async_copy(skip_ref, skip_hbm, sem)
    copy_skip.start()
    keep_ref[...] = cin_ref[...]
    groups = cw_ref.shape[1] // (3 * HD)
    kvs, qs = [], []
    for h in range(groups):
        qs.append(cw_ref[:, h * 3 * HD : h * 3 * HD + HD].astype(F32))
        kvs.append(cw_ref[:, h * 3 * HD + HD : (h + 1) * 3 * HD].astype(F32))
    order_ref[...] = jnp.concatenate(kvs + qs, axis=1).astype(BF)
    copy_skip.wait()


def attend(q_ref, wins, bias_ref, outw_ref, blocks):
    rows, cols, width = q_ref.shape
    heads, nq = width // HD, rows * BLOCK
    lane_head = lax.broadcasted_iota(jnp.int32, (nq, width), 1) // HD
    kvs, scores = [], []
    for j, win in zip(blocks, wins):
        qb = q_ref[:, j * BLOCK : (j + 1) * BLOCK, :].reshape(nq, width)
        qs = jnp.concatenate([jnp.where(lane_head == h, qb, 0.0) for h in range(heads)], axis=0)
        kvs.append(win.reshape(win.shape[0] * SPAN, 2 * width).astype(BF))
        scores.append(mm_t(qs.astype(BF), kvs[-1][:, :width]) + bias_ref[...])
    ps = [jnp.exp(s - jnp.max(s, axis=1, keepdims=True)) for s in scores]
    outs = [mm(p.astype(BF), kv[:, width:]) for p, kv in zip(ps, kvs)]
    atts = []
    for p, o in zip(ps, outs):
        o = o / jnp.sum(p, axis=1, keepdims=True)
        att = o[:nq]
        for h in range(1, heads):
            att = jnp.where(lane_head == h, o[h * nq : (h + 1) * nq], att)
        atts.append(att.astype(BF))
    proj = mm(jnp.concatenate(atts, axis=0), outw_ref[...])
    return [proj[i * nq : (i + 1) * nq].reshape(rows, BLOCK, width) for i in range(len(atts))]


def inner_kernel(
    mod_ref,
    far_ref,
    near_ref,
    w_ref,
    outw_ref,
    q_ref,
    kv_ref,
    bias_ref,
    nkv_ref,
    skv_ref,
    res_ref,
):
    north, south = sides(far_ref, near_ref)
    nkv_ref[...] = key_values(shifted(north), mod_ref, w_ref)
    skv_ref[...] = key_values(shifted(south), mod_ref, w_ref)
    cols = q_ref.shape[1]
    for lead in range(1, cols // BLOCK - 1, STAGE):
        blocks = range(lead, min(lead + STAGE, cols // BLOCK - 1))
        wins = [
            jnp.concatenate(
                [r[:, j * BLOCK : j * BLOCK + SPAN, :] for r in (nkv_ref, kv_ref, skv_ref)], axis=0
            )
            for j in blocks
        ]
        for j, proj in zip(blocks, attend(q_ref, wins, bias_ref, outw_ref, blocks)):
            res_ref[:, j * BLOCK : (j + 1) * BLOCK, :] = proj


def edge_kernel(
    mod_ref,
    chip_ref,
    link_ref,
    tok_ref,
    w_ref,
    outw_ref,
    q_ref,
    kv_ref,
    bias_ref,
    nkv_ref,
    skv_ref,
    res_ref,
    one_ref,
    two_ref,
    skip_ref,
    cin_ref,
    lane_ref,
):
    rows, cols, width = tok_ref.shape
    side = lax.broadcasted_iota(jnp.int32, (rows + 2 * WIN, BLOCK, 2 * width), 1)
    kvs = (nkv_ref, kv_ref, skv_ref)

    def tile(at):
        return jnp.concatenate([r[:, at : at + BLOCK, :] for r in kvs], axis=0)

    odd = jnp.broadcast_to(lax.axis_index("inner") % 2, chip_ref.shape) == 1
    chip, link = chip_ref[...].astype(F32), link_ref[...].astype(F32)
    west, east = jnp.where(odd, chip, link), jnp.where(odd, link, chip)
    strips = [strip_columns(west, 0), strip_columns(east, WIN)]
    strips = key_values(jnp.concatenate(strips, axis=0), mod_ref, w_ref)
    wkv, ekv = strips[: rows + 2 * WIN], strips[rows + 2 * WIN :]
    first = jnp.concatenate([jnp.where(side < WIN, wkv, tile(0)), tile(BLOCK)], axis=1)
    last = jnp.concatenate([tile(cols - BLOCK), jnp.where(side >= WIN, ekv, tile(cols))], axis=1)
    tok = tok_ref[...].astype(F32)
    ends = (0, cols // BLOCK - 1)
    low, high = attend(q_ref, [first, last], bias_ref, outw_ref, ends)
    proj = jnp.concatenate([low, res_ref[:, BLOCK : cols - BLOCK, :], high], axis=1)
    res = (proj + tok).astype(BF)
    skip_ref[...] = res
    for k in range(width // 128):
        lane_ref[k, :, :cols, :] = res[:, :, k * 128 : (k + 1) * 128].astype(F32)

    groups = []
    for a in range(2):
        for b in range(2):
            parts = []
            for dr in range(2):
                for dc in range(2):
                    r, c = 2 * a + dr, 2 * b + dc
                    for k in range(width // 128):
                        strips = [
                            lane_ref[k, rr, pl.ds(c, cols // 4, stride=4), :]
                            for rr in range(r, rows, 4)
                        ]
                        parts.append(jnp.concatenate(strips, axis=0))
            groups.append(jnp.concatenate(parts, axis=1))
    count = (rows // 4) * (cols // 4)
    mid = mm(jnp.concatenate(groups, axis=0).astype(BF), one_ref[...]).astype(BF)
    mid = jnp.concatenate([mid[g * count : (g + 1) * count] for g in range(4)], axis=1)
    cin_ref[...] = mm(mid, two_ref[...]).astype(BF)


def halves(low, high, swap_low):
    lane = lax.broadcasted_iota(jnp.int32, low.shape, 1)
    if swap_low:
        return jnp.where(lane < HD, pltpu.roll(low, HD, 1), high)
    return jnp.where(lane < HD, low, pltpu.roll(high, HD, 1))


def qkv_kernel(groups, mod_ref, *refs):
    xs, w_ref, out_refs = refs[: -1 - groups], refs[-1 - groups], refs[-groups:]
    x = jnp.concatenate([r[...] for r in xs], axis=0)
    at = mod_ref.shape[1] - 2 * x.shape[1]
    scale, shift = mod_ref[:, at : at + x.shape[1]], mod_ref[:, at + x.shape[1] :]
    y = mm(layer_norm(x.astype(F32), scale, shift), w_ref[...])
    half = x.shape[0] // 2
    zi = lax.axis_index("head")
    pieces = []
    for h in range(groups):
        kv = y[:, h * 2 * HD : (h + 1) * 2 * HD]
        if groups % 2:
            q = y[:, groups * 2 * HD + h * HD : groups * 2 * HD + (h + 1) * HD]
            qp = jnp.concatenate([q[:half], q[half:]], axis=1)
        else:
            at = groups * 2 * HD + (h // 2) * 2 * HD
            pair = y[:, at : at + 2 * HD]
            qp = halves(pair[:half], pair[half:], h % 2 == 1)
        pieces.append(jnp.concatenate([kv, qp * (1.0 / math.sqrt(HD))], axis=0).astype(BF))
    for g in range(groups):
        for h in range(groups):

            @pl.when(zi == g ^ h)
            def _(g=g, h=h):
                out_refs[g][...] = pieces[h]


def queries(own):
    band = own[0].shape[0] * 2 // 3
    half = band // 2
    lane = lax.broadcasted_iota(jnp.int32, (half, 2 * HD), 1)
    qs = []
    for r in own:
        qp = r[band:, :].astype(F32)
        qs.append(jnp.where(lane < HD, qp, 0.0))
        qs.append(jnp.where(lane < HD, pltpu.roll(qp, HD, 1), 0.0))
    return jnp.concatenate(qs, axis=0).astype(BF)


def values(kv):
    lane = lax.broadcasted_iota(jnp.int32, kv.shape, 1)
    return jnp.where(lane < HD, jnp.ones_like(kv), kv)


def near_kernel(groups, *refs):
    own, others, (acc_ref, max_ref) = refs[:groups], refs[groups:-2], refs[-2:]
    band = own[0].shape[0] * 2 // 3
    kv = jnp.concatenate([r[:band, :] for r in own] + [r[...] for r in others], axis=0)
    s = mm_t(queries(own), kv)
    top = jnp.max(s, axis=1, keepdims=True)
    p = jnp.exp(s - top)
    acc_ref[...] = mm(p.astype(BF), values(kv))
    max_ref[...] = jnp.broadcast_to(top, max_ref.shape)


def far_kernel(steps, parts, *refs):
    groups = len(steps)
    own, others = refs[:groups], refs[groups:-3]
    acc_ref, max_ref, out_ref = refs[-3:]
    kv = jnp.concatenate([r[...] for r in others], axis=0)
    s = mm_t(queries(own), kv)
    before = max_ref[...]
    top = jnp.maximum(before[:, :1], jnp.max(s, axis=1, keepdims=True))
    p = jnp.exp(s - top)
    acc = acc_ref[...] * jnp.exp(before - top) + mm(p.astype(BF), values(kv))
    count = acc.shape[0] // (groups * parts)
    zi, ii = lax.axis_index("head"), lax.axis_index("inner")
    for g in range(groups):
        for k in range(parts):
            at = (g * parts + k) * count
            low, high = acc[at : at + count // 2], acc[at + count // 2 : at + count]
            block = halves(low, high, True) / halves(low, high, False)
            out_ref[(zi ^ steps[g]) * parts + (ii ^ k)] = block.astype(BF)


def project_kernel(groups, parts, cin_ref, att_ref, *refs):
    ws, out_ref = refs[:-1], refs[-1]
    ii = lax.axis_index("inner")
    total = cin_ref[...].astype(F32)
    for k in range(parts):
        xs = [att_ref[g * parts + (ii ^ k)].astype(F32) for g in range(groups)]
        if groups % 2:
            cols = [jnp.concatenate([x[:, :HD], x[:, HD:]], axis=0) for x in xs]
        else:
            cols = [
                jnp.concatenate([halves(a, b, False), halves(a, b, True)], axis=0)
                for a, b in zip(xs[::2], xs[1::2])
            ]
        total = total + mm(jnp.concatenate(cols, axis=1).astype(BF), ws[k][...])
    out_ref[...] = total.astype(BF).reshape(out_ref.shape)


def call(kernel, out, in_specs, scratch=(), out_specs=None, limit=12, flops=None, name=None):
    cost = flops and pl.CostEstimate(flops=flops, bytes_accessed=MIB, transcendentals=0)
    return pl.pallas_call(
        kernel,
        out_shape=out,
        in_specs=in_specs,
        out_specs=[VM for _ in out] if out_specs is None else out_specs,
        scratch_shapes=list(scratch),
        compiler_params=pltpu.CompilerParams(vmem_limit_bytes=limit * MIB),
        cost_estimate=cost,
        name=name,
    )


def swap(x, axis, step):
    size = lax.axis_size(axis)
    return lax.ppermute(x, axis, [(i, i ^ step) for i in range(size)])


def body(
    tokens,
    timestep,
    mod_weight,
    fine_qkv_weight,
    fine_out_weight,
    merge_one,
    merge_two,
    coarse_qkv_weight,
    coarse_out_weight,
):
    S = jax.ShapeDtypeStruct
    rows, cols, width = tokens.shape
    cw = merge_two.shape[1]
    no, ni = lax.axis_size(OUTER), lax.axis_size("inner")
    odd = lax.axis_index(OUTER) % 2 == 1
    bottom, top = tokens[rows - WIN :], tokens[:WIN]
    pairs = []
    for i in range(no * ni):
        band, column = i // ni, i % ni
        if band in (0, no - 1):
            pairs.append((i, band * ni + (column ^ 1)))
        else:
            pairs.append((i, i + ni if band % 2 else i - ni))
    far = lax.ppermute(jnp.where(odd, bottom, top), OUTER + ("inner",), pairs)
    near = swap(jnp.where(odd, top, bottom), OUTER, 1)

    emb = embed(timestep, mod_weight.shape[0])
    mod = mm(emb, mod_weight)
    tall = rows + 2 * WIN
    heads = width // HD
    q, kv, bias, kvw, outw = call(
        own_kernel,
        [
            S((rows, cols, width), F32),
            S((rows, cols + BLOCK, 2 * width), F32),
            S((heads * rows * BLOCK, tall * SPAN), F32),
            S((width, 2 * width), BF),
            S((width, width), BF),
        ],
        [VM] * 4,
        limit=16,
        flops=1000000000,
        name="own",
    )(mod, tokens, fine_qkv_weight, fine_out_weight)

    strip = S((tall, BLOCK, width // 2), BF)
    chip, link = call(columns_kernel, [strip] * 2, [VM] * 3, name="columns")(
        far, near, tokens
    )
    chip = swap(chip, "inner", 1)
    link = lax.ppermute(link, "inner", [(i, (i + (1 if i % 2 else -1)) % ni) for i in range(ni)])
    nkv, skv, res = call(
        inner_kernel,
        [S((WIN, cols + BLOCK, 2 * width), F32)] * 2 + [S((rows, cols, width), F32)],
        [VM] * 8,
        limit=16,
        flops=1000000000,
        name="inside",
    )(mod, far, near, kvw, outw, q, kv, bias)
    count = (rows // 4) * (cols // 4)
    skip, coarse_in = call(
        edge_kernel,
        [S(tokens.shape, BF), S((count, cw), BF)],
        [VM] * 14,
        scratch=[
            pltpu.VMEM((width // 128, rows, cols + BLOCK, 128), F32),
        ],
        limit=20,
        name="edge",
    )(
        mod, chip, link, tokens, kvw, outw, q, kv, bias, nkv, skv, res, merge_one, merge_two
    )

    groups = coarse_qkv_weight.shape[1] // (3 * HD)
    sub = no // groups
    band = ni * count
    order, keep, fine_skip = call(
        order_kernel,
        [S(coarse_qkv_weight.shape, BF), S(coarse_in.shape, BF), S(tokens.shape, BF)],
        [VM] * 3,
        scratch=[pltpu.SemaphoreType.DMA],
        out_specs=[VM, VM, HB],
        flops=1000000000,
        name="order",
    )(coarse_in, skip, coarse_qkv_weight)
    gathered, step = [coarse_in], ni // 2
    beside = swap(coarse_in, "inner", 1)
    while step > 1:
        gathered = [w for x in gathered for w in (x, swap(x, "inner", step))]
        step //= 2
    weight, order, beside, gathered[1] = lax.optimization_barrier((coarse_out_weight, order, beside, gathered[1]))
    gathered = [w for x in gathered for w in (x, beside if x is coarse_in else swap(x, "inner", 1))]
    step = ni // 2
    whole = [weight, swap(weight, "inner", step)]
    pieces = call(
        lambda *r: qkv_kernel(groups, *r),
        [S((band + band // 2, 2 * HD), BF)] * groups,
        [VM] * (ni + 2),
        name="qkv",
    )(mod, *gathered, order)
    steps = sorted(range(groups), key=lambda g: (g > 0, g != groups - 1, g))
    own = [swap(pieces[g], OUTER, g * sub) if g else pieces[0] for g in steps]
    aside = swap(weight, "inner", 1)
    held = [own[0][:band]]
    if groups > 1:
        held.append(jnp.concatenate([p[:band] for p in own[1:]], axis=0))
    others = [swap(p, OUTER, k) for k in range(1, sub) for p in held]
    aside, others[0] = lax.optimization_barrier((aside, others[0]))
    acc, top = call(
        lambda *r: near_kernel(groups, *r),
        [S((groups * band, 2 * HD), F32)] * 2,
        [VM] * (groups + EARLY),
        limit=16,
        flops=1000000000,
        name="near",
    )(*own, *others[:EARLY])
    others = others[EARLY:]
    att = call(
        lambda *r: far_kernel(steps, ni, *r),
        [S((groups * ni, count // 2, 2 * HD), BF)],
        [VM] * (groups + len(others) + 2),
        limit=16 if no * band <= 1024 else 56,
        name="far",
    )(*own, *others, acc, top)
    far_weight, att = lax.optimization_barrier((whole[1], att))
    whole[1] = far_weight
    while step > 1:
        step //= 2
        whole = [w for x in whole for w in (x, aside if step == 1 and x is weight else swap(x, "inner", step))]
    att = lax.all_to_all(att[0], ("head", "inner"), 0, 0, tiled=True)
    (coarse_out,) = call(
        lambda *r: project_kernel(groups, ni, *r),
        [S((rows // 4, cols // 4, cw), BF)],
        [VM] * (ni + 2),
        name="project",
    )(keep, att, *whole)
    return (fine_skip, coarse_out)


def solution(mesh):
    inner = mesh.shape["inner"]
    heads = 16 // inner
    devices = mesh.devices.reshape(heads, mesh.shape["outer"] // heads, inner)
    return jax.shard_map(
        body,
        mesh=jax.sharding.Mesh(devices, OUTER + ("inner",)),
        in_specs=(
            P(OUTER, "inner", None),
            P(),
            P(),
            P(),
            P(),
            P(),
            P(),
            P(None, "inner"),
            P("inner", None),
        ),
        out_specs=(P(OUTER, "inner", None), P(OUTER, "inner", None)),
        check_vma=False,
    )
```

```python
import math

import jax
import jax.numpy as jnp
from jax import lax
from jax.experimental import pallas as pl
from jax.experimental.pallas import tpu as pltpu
from jax.sharding import PartitionSpec as P

HD = 64
WIN = 3
BLOCK = 8
SPAN = 16
STAGE = 6
EARLY = 1
BF = jnp.bfloat16
F32 = jnp.float32
VM = pl.BlockSpec(memory_space=pltpu.VMEM)
HB = pl.BlockSpec(memory_space=pl.ANY)
HM = pl.BlockSpec(memory_space=pltpu.HBM)
MIB = 1024 * 1024
OUTER = ("head", "sub")


def embed(timestep, width):
    half = width // 2
    freq = jnp.exp(-math.log(10000.0) * jnp.arange(half, dtype=F32) / half)
    angle = timestep.astype(F32)[0] * freq
    return jnp.concatenate([jnp.cos(angle), jnp.sin(angle)]).astype(BF)[None, :]


def layer_norm(x, scale, shift):
    mean = jnp.mean(x, axis=-1, keepdims=True)
    var = jnp.mean((x - mean) * (x - mean), axis=-1, keepdims=True)
    return ((x - mean) * lax.rsqrt(var + 1e-06) * (1.0 + scale) + shift).astype(BF)


def mm(a, b):
    return jnp.dot(a, b, preferred_element_type=F32)


def mm_t(a, b):
    return lax.dot_general(a, b, (((1,), (1,)), ((), ())), preferred_element_type=F32)


def shifted(x):
    rows, cols, width = x.shape
    left = jnp.zeros((rows, WIN, width), F32)
    right = jnp.zeros((rows, BLOCK - WIN, width), F32)
    return jnp.concatenate([left, x, right], axis=1)


def key_values(x, mod_ref, w_ref):
    rows, cols, width = x.shape
    flat = x.reshape(rows * cols, width)
    n = layer_norm(flat, mod_ref[:, :width], mod_ref[:, width : 2 * width])
    return mm(n, w_ref[...]).reshape(rows, cols, 2 * width)


def place(axes):
    at = 0
    for axis in axes:
        at = at * lax.axis_size(axis) + lax.axis_index(axis)
    return at


def sides(far_ref, near_ref):
    odd = jnp.broadcast_to(place(OUTER) % 2, far_ref.shape) == 1
    far, near = far_ref[...].astype(F32), near_ref[...].astype(F32)
    return jnp.where(odd, near, far), jnp.where(odd, far, near)


def columns_kernel(far_ref, near_ref, tok_ref, chip_ref, link_ref):
    cols, width = tok_ref.shape[1:]
    half = BLOCK // 2
    strips = []
    for at, lead in ((cols - 2 * BLOCK, 2 * BLOCK - WIN), (0, 0)):
        chunk = pl.ds(at, 2 * BLOCK)
        north, south = sides(far_ref.at[:, chunk], near_ref.at[:, chunk])
        x = jnp.concatenate([north, tok_ref[:, chunk].astype(F32), south], axis=0)
        x = jnp.concatenate([x[:, lead : lead + WIN], x[:, : half - WIN]], axis=1)
        strips.append(jnp.concatenate([x[:, :, k : k + width // 2] for k in (0, width // 2)], axis=1))
    odd = jnp.broadcast_to(lax.axis_index("inner") % 2, strips[0].shape) == 1
    chip_ref[...] = jnp.where(odd, strips[1], strips[0]).astype(BF)
    link_ref[...] = jnp.where(odd, strips[0], strips[1]).astype(BF)


def strip_columns(x, lead):
    half = BLOCK // 2
    x = jnp.concatenate([x[:, :half], x[:, half:]], axis=2)[:, :WIN]
    zero = jnp.zeros((x.shape[0], BLOCK, x.shape[2]), F32)
    parts = [zero[:, :lead]] * (lead > 0) + [x, zero[:, lead + WIN :]]
    return jnp.concatenate(parts, axis=1)


def own_kernel(
    mod_ref, tok_ref, w_ref, out_ref, q_ref, kv_ref, bias_ref, kvw_ref, outw_ref
):
    kvw_ref[...] = w_ref[:, tok_ref.shape[2] :]
    outw_ref[...] = out_ref[...]
    rows, cols, width = tok_ref.shape
    tok = tok_ref[...].astype(F32)
    fscale, fshift = mod_ref[:, :width], mod_ref[:, width : 2 * width]
    n = layer_norm(tok.reshape(rows * cols, width), fscale, fshift)
    q = mm(n, w_ref[:, :width]).astype(BF).astype(F32) * (1.0 / math.sqrt(HD))
    q_ref[...] = q.reshape(rows, cols, width)
    kv_ref[...] = key_values(shifted(tok), mod_ref, kvw_ref)

    nq, nk = bias_ref.shape
    per = rows * BLOCK
    band, bands = place(OUTER), lax.axis_size(OUTER)
    lo = jnp.where(band == 0, WIN, 0)
    hi = jnp.where(band == bands - 1, rows + WIN, rows + 2 * WIN)
    qi = lax.broadcasted_iota(jnp.int32, (nq, nk), 0) % per
    ki = lax.broadcasted_iota(jnp.int32, (nq, nk), 1)
    kr, kc = ki // SPAN, ki % SPAN
    dr, dc = kr - qi // BLOCK, kc - qi % BLOCK
    ok = (dr >= 0) & (dr <= 2 * WIN) & (dc >= 0) & (dc <= 2 * WIN) & (kr >= lo) & (kr < hi)
    bias_ref[...] = jnp.where(ok, 0.0, -1e30).astype(F32)


def order_kernel(cin_ref, skip_ref, cw_ref, order_ref, keep_ref, skip_hbm, sem):
    copy_skip = pltpu.make_async_copy(skip_ref, skip_hbm, sem)
    copy_skip.start()
    keep_ref[...] = cin_ref[...]
    groups = cw_ref.shape[1] // (3 * HD)
    kvs, qs = [], []
    for h in range(groups):
        qs.append(cw_ref[:, h * 3 * HD : h * 3 * HD + HD].astype(F32))
        kvs.append(cw_ref[:, h * 3 * HD + HD : (h + 1) * 3 * HD].astype(F32))
    order_ref[...] = jnp.concatenate(kvs + qs, axis=1).astype(BF)
    copy_skip.wait()


def attend(q_ref, wins, bias_ref, outw_ref, blocks):
    rows, cols, width = q_ref.shape
    heads, nq = width // HD, rows * BLOCK
    lane_head = lax.broadcasted_iota(jnp.int32, (nq, width), 1) // HD
    kvs, scores = [], []
    for j, win in zip(blocks, wins):
        qb = q_ref[:, j * BLOCK : (j + 1) * BLOCK, :].reshape(nq, width)
        qs = jnp.concatenate([jnp.where(lane_head == h, qb, 0.0) for h in range(heads)], axis=0)
        kvs.append(win.reshape(win.shape[0] * SPAN, 2 * width).astype(BF))
        scores.append(mm_t(qs.astype(BF), kvs[-1][:, :width]) + bias_ref[...])
    ps = [jnp.exp(s - jnp.max(s, axis=1, keepdims=True)) for s in scores]
    outs = [mm(p.astype(BF), kv[:, width:]) for p, kv in zip(ps, kvs)]
    atts = []
    for p, o in zip(ps, outs):
        o = o / jnp.sum(p, axis=1, keepdims=True)
        att = o[:nq]
        for h in range(1, heads):
            att = jnp.where(lane_head == h, o[h * nq : (h + 1) * nq], att)
        atts.append(att.astype(BF))
    proj = mm(jnp.concatenate(atts, axis=0), outw_ref[...])
    return [proj[i * nq : (i + 1) * nq].reshape(rows, BLOCK, width) for i in range(len(atts))]


def inner_kernel(
    mod_ref,
    far_ref,
    near_ref,
    w_ref,
    outw_ref,
    q_ref,
    kv_ref,
    bias_ref,
    nkv_ref,
    skv_ref,
    res_ref,
):
    north, south = sides(far_ref, near_ref)
    nkv_ref[...] = key_values(shifted(north), mod_ref, w_ref)
    skv_ref[...] = key_values(shifted(south), mod_ref, w_ref)
    cols = q_ref.shape[1]
    for lead in range(1, cols // BLOCK - 1, STAGE):
        blocks = range(lead, min(lead + STAGE, cols // BLOCK - 1))
        wins = [
            jnp.concatenate(
                [r[:, j * BLOCK : j * BLOCK + SPAN, :] for r in (nkv_ref, kv_ref, skv_ref)], axis=0
            )
            for j in blocks
        ]
        for j, proj in zip(blocks, attend(q_ref, wins, bias_ref, outw_ref, blocks)):
            res_ref[:, j * BLOCK : (j + 1) * BLOCK, :] = proj


def edge_kernel(
    mod_ref,
    chip_ref,
    link_ref,
    tok_ref,
    w_ref,
    outw_ref,
    q_ref,
    kv_ref,
    bias_ref,
    nkv_ref,
    skv_ref,
    res_ref,
    one_ref,
    two_ref,
    skip_ref,
    cin_ref,
    lane_ref,
):
    rows, cols, width = tok_ref.shape
    side = lax.broadcasted_iota(jnp.int32, (rows + 2 * WIN, BLOCK, 2 * width), 1)
    kvs = (nkv_ref, kv_ref, skv_ref)

    def tile(at):
        return jnp.concatenate([r[:, at : at + BLOCK, :] for r in kvs], axis=0)

    odd = jnp.broadcast_to(lax.axis_index("inner") % 2, chip_ref.shape) == 1
    chip, link = chip_ref[...].astype(F32), link_ref[...].astype(F32)
    west, east = jnp.where(odd, chip, link), jnp.where(odd, link, chip)
    strips = [strip_columns(west, 0), strip_columns(east, WIN)]
    strips = key_values(jnp.concatenate(strips, axis=0), mod_ref, w_ref)
    wkv, ekv = strips[: rows + 2 * WIN], strips[rows + 2 * WIN :]
    first = jnp.concatenate([jnp.where(side < WIN, wkv, tile(0)), tile(BLOCK)], axis=1)
    last = jnp.concatenate([tile(cols - BLOCK), jnp.where(side >= WIN, ekv, tile(cols))], axis=1)
    tok = tok_ref[...].astype(F32)
    ends = (0, cols // BLOCK - 1)
    low, high = attend(q_ref, [first, last], bias_ref, outw_ref, ends)
    proj = jnp.concatenate([low, res_ref[:, BLOCK : cols - BLOCK, :], high], axis=1)
    res = (proj + tok).astype(BF)
    skip_ref[...] = res
    for k in range(width // 128):
        lane_ref[k, :, :cols, :] = res[:, :, k * 128 : (k + 1) * 128].astype(F32)

    groups = []
    for a in range(2):
        for b in range(2):
            parts = []
            for dr in range(2):
                for dc in range(2):
                    r, c = 2 * a + dr, 2 * b + dc
                    for k in range(width // 128):
                        strips = [
                            lane_ref[k, rr, pl.ds(c, cols // 4, stride=4), :]
                            for rr in range(r, rows, 4)
                        ]
                        parts.append(jnp.concatenate(strips, axis=0))
            groups.append(jnp.concatenate(parts, axis=1))
    count = (rows // 4) * (cols // 4)
    mid = mm(jnp.concatenate(groups, axis=0).astype(BF), one_ref[...]).astype(BF)
    mid = jnp.concatenate([mid[g * count : (g + 1) * count] for g in range(4)], axis=1)
    cin_ref[...] = mm(mid, two_ref[...]).astype(BF)


def halves(low, high, swap_low):
    lane = lax.broadcasted_iota(jnp.int32, low.shape, 1)
    if swap_low:
        return jnp.where(lane < HD, pltpu.roll(low, HD, 1), high)
    return jnp.where(lane < HD, low, pltpu.roll(high, HD, 1))


def qkv_kernel(groups, mod_ref, *refs):
    xs, w_ref, out_refs = refs[: -1 - groups], refs[-1 - groups], refs[-groups:]
    x = jnp.concatenate([r[...] for r in xs], axis=0)
    at = mod_ref.shape[1] - 2 * x.shape[1]
    scale, shift = mod_ref[:, at : at + x.shape[1]], mod_ref[:, at + x.shape[1] :]
    y = mm(layer_norm(x.astype(F32), scale, shift), w_ref[...])
    half = x.shape[0] // 2
    zi = lax.axis_index("head")
    pieces = []
    for h in range(groups):
        kv = y[:, h * 2 * HD : (h + 1) * 2 * HD]
        if groups % 2:
            q = y[:, groups * 2 * HD + h * HD : groups * 2 * HD + (h + 1) * HD]
            qp = jnp.concatenate([q[:half], q[half:]], axis=1)
        else:
            at = groups * 2 * HD + (h // 2) * 2 * HD
            pair = y[:, at : at + 2 * HD]
            qp = halves(pair[:half], pair[half:], h % 2 == 1)
        pieces.append(jnp.concatenate([kv, qp * (1.0 / math.sqrt(HD))], axis=0).astype(BF))
    for g in range(groups):
        for h in range(groups):

            @pl.when(zi == g ^ h)
            def _(g=g, h=h):
                out_refs[g][...] = pieces[h]


def queries(own):
    band = own[0].shape[0] * 2 // 3
    half = band // 2
    lane = lax.broadcasted_iota(jnp.int32, (half, 2 * HD), 1)
    qs = []
    for r in own:
        qp = r[band:, :].astype(F32)
        qs.append(jnp.where(lane < HD, qp, 0.0))
        qs.append(jnp.where(lane < HD, pltpu.roll(qp, HD, 1), 0.0))
    return jnp.concatenate(qs, axis=0).astype(BF)


def values(kv):
    lane = lax.broadcasted_iota(jnp.int32, kv.shape, 1)
    return jnp.where(lane < HD, jnp.ones_like(kv), kv)


def near_kernel(groups, *refs):
    own, others, (acc_ref, max_ref, ask_ref) = refs[:groups], refs[groups:-3], refs[-3:]
    ask_ref[...] = queries(own)
    band = own[0].shape[0] * 2 // 3
    kv = jnp.concatenate([r[:band, :] for r in own] + [r[...] for r in others], axis=0)
    s = mm_t(ask_ref[...], kv)
    top = jnp.max(s, axis=1, keepdims=True)
    p = jnp.exp(s - top)
    acc_ref[...] = mm(p.astype(BF), values(kv))
    max_ref[...] = jnp.broadcast_to(top, max_ref.shape)


def far_kernel(steps, parts, *refs):
    groups = len(steps)
    others, (acc_ref, max_ref, ask_ref, out_ref) = refs[:-4], refs[-4:]
    kv = jnp.concatenate([r[...] for r in others], axis=0)
    s = mm_t(ask_ref[...], kv)
    before = max_ref[...]
    top = jnp.maximum(before[:, :1], jnp.max(s, axis=1, keepdims=True))
    p = jnp.exp(s - top)
    acc = acc_ref[...] * jnp.exp(before - top) + mm(p.astype(BF), values(kv))
    count = acc.shape[0] // (groups * parts)
    zi, ii = lax.axis_index("head"), lax.axis_index("inner")
    for g in range(groups):
        for k in range(parts):
            at = (g * parts + k) * count
            low, high = acc[at : at + count // 2], acc[at + count // 2 : at + count]
            block = halves(low, high, True) / halves(low, high, False)
            out_ref[(zi ^ steps[g]) * parts + (ii ^ k)] = block.astype(BF)


def project_kernel(groups, parts, cin_ref, att_ref, *refs):
    ws, out_ref = refs[:-1], refs[-1]
    ii = lax.axis_index("inner")
    total = cin_ref[...].astype(F32)
    for k in range(parts):
        xs = [att_ref[g * parts + (ii ^ k)].astype(F32) for g in range(groups)]
        if groups % 2:
            cols = [jnp.concatenate([x[:, :HD], x[:, HD:]], axis=0) for x in xs]
        else:
            cols = [
                jnp.concatenate([halves(a, b, False), halves(a, b, True)], axis=0)
                for a, b in zip(xs[::2], xs[1::2])
            ]
        total = total + mm(jnp.concatenate(cols, axis=1).astype(BF), ws[k][...])
    out_ref[...] = total.astype(BF).reshape(out_ref.shape)


def call(kernel, out, in_specs, scratch=(), out_specs=None, limit=12, flops=None, name=None):
    cost = flops and pl.CostEstimate(flops=flops, bytes_accessed=MIB, transcendentals=0)
    return pl.pallas_call(
        kernel,
        out_shape=out,
        in_specs=in_specs,
        out_specs=[VM for _ in out] if out_specs is None else out_specs,
        scratch_shapes=list(scratch),
        compiler_params=pltpu.CompilerParams(vmem_limit_bytes=limit * MIB),
        cost_estimate=cost,
        name=name,
    )


def swap(x, axis, step):
    size = lax.axis_size(axis)
    return lax.ppermute(x, axis, [(i, i ^ step) for i in range(size)])


def body(
    tokens,
    timestep,
    mod_weight,
    fine_qkv_weight,
    fine_out_weight,
    merge_one,
    merge_two,
    coarse_qkv_weight,
    coarse_out_weight,
):
    S = jax.ShapeDtypeStruct
    rows, cols, width = tokens.shape
    cw = merge_two.shape[1]
    no, ni = lax.axis_size(OUTER), lax.axis_size("inner")
    odd = lax.axis_index(OUTER) % 2 == 1
    bottom, top = tokens[rows - WIN :], tokens[:WIN]
    pairs = []
    for i in range(no * ni):
        band, column = i // ni, i % ni
        if band in (0, no - 1):
            pairs.append((i, band * ni + (column ^ 1)))
        else:
            pairs.append((i, i + ni if band % 2 else i - ni))
    far = lax.ppermute(jnp.where(odd, bottom, top), OUTER + ("inner",), pairs)
    near = swap(jnp.where(odd, top, bottom), OUTER, 1)

    emb = embed(timestep, mod_weight.shape[0])
    mod = mm(emb, mod_weight)
    tall = rows + 2 * WIN
    heads = width // HD
    q, kv, bias, kvw, outw = call(
        own_kernel,
        [
            S((rows, cols, width), F32),
            S((rows, cols + BLOCK, 2 * width), F32),
            S((heads * rows * BLOCK, tall * SPAN), F32),
            S((width, 2 * width), BF),
            S((width, width), BF),
        ],
        [VM] * 4,
        limit=16,
        flops=1000000000,
        name="own",
    )(mod, tokens, fine_qkv_weight, fine_out_weight)

    strip = S((tall, BLOCK, width // 2), BF)
    chip, link = call(columns_kernel, [strip] * 2, [VM] * 3, name="columns")(
        far, near, tokens
    )
    chip = swap(chip, "inner", 1)
    link = lax.ppermute(link, "inner", [(i, (i + (1 if i % 2 else -1)) % ni) for i in range(ni)])
    nkv, skv, res = call(
        inner_kernel,
        [S((WIN, cols + BLOCK, 2 * width), F32)] * 2 + [S((rows, cols, width), F32)],
        [VM] * 8,
        limit=16,
        flops=1000000000,
        name="inside",
    )(mod, far, near, kvw, outw, q, kv, bias)
    count = (rows // 4) * (cols // 4)
    skip, coarse_in = call(
        edge_kernel,
        [S(tokens.shape, BF), S((count, cw), BF)],
        [VM] * 14,
        scratch=[
            pltpu.VMEM((width // 128, rows, cols + BLOCK, 128), F32),
        ],
        limit=20,
        name="edge",
    )(
        mod, chip, link, tokens, kvw, outw, q, kv, bias, nkv, skv, res, merge_one, merge_two
    )

    groups = coarse_qkv_weight.shape[1] // (3 * HD)
    sub = no // groups
    band = ni * count
    order, keep, fine_skip = call(
        order_kernel,
        [S(coarse_qkv_weight.shape, BF), S(coarse_in.shape, BF), S(tokens.shape, BF)],
        [VM] * 3,
        scratch=[pltpu.SemaphoreType.DMA],
        out_specs=[VM, VM, HB],
        flops=1000000000,
        name="order",
    )(coarse_in, skip, coarse_qkv_weight)
    gathered, step = [coarse_in], ni // 2
    beside = swap(coarse_in, "inner", 1)
    while step > 1:
        gathered = [w for x in gathered for w in (x, swap(x, "inner", step))]
        step //= 2
    weight, order, beside, gathered[1] = lax.optimization_barrier((coarse_out_weight, order, beside, gathered[1]))
    gathered = [w for x in gathered for w in (x, beside if x is coarse_in else swap(x, "inner", 1))]
    step = ni // 2
    whole = [weight, swap(weight, "inner", step)]
    pieces = call(
        lambda *r: qkv_kernel(groups, *r),
        [S((band + band // 2, 2 * HD), BF)] * groups,
        [VM] * (ni + 2),
        name="qkv",
    )(mod, *gathered, order)
    steps = [0] + list(range(groups - 1, 0, -1))
    own = [swap(pieces[g], OUTER, g * sub) if g else pieces[0] for g in steps]
    aside = swap(weight, "inner", 1)
    held = [own[0][:band]]
    if groups > 1:
        held.append(jnp.concatenate([p[:band] for p in own[1:]], axis=0))
    others = [swap(p, OUTER, k) for k in range(1, sub) for p in held]
    aside, others[0] = lax.optimization_barrier((aside, others[0]))
    acc, top, ask = call(
        lambda *r: near_kernel(groups, *r),
        [S((groups * band, 2 * HD), F32)] * 2 + [S((groups * band, 2 * HD), BF)],
        [VM] * (groups + EARLY),
        limit=16,
        flops=1000000000,
        name="near",
    )(*own, *others[:EARLY])
    others = others[EARLY:]
    att = call(
        lambda *r: far_kernel(steps, ni, *r),
        [S((groups * ni, count // 2, 2 * HD), BF)],
        [VM] * (len(others) + 3),
        limit=16 if no * band <= 1024 else 56,
        name="far",
    )(*others, acc, top, ask)
    far_weight, att = lax.optimization_barrier((whole[1], att))
    whole[1] = far_weight
    while step > 1:
        step //= 2
        whole = [w for x in whole for w in (x, aside if step == 1 and x is weight else swap(x, "inner", step))]
    att = lax.all_to_all(att[0], ("head", "inner"), 0, 0, tiled=True)
    (coarse_out,) = call(
        lambda *r: project_kernel(groups, ni, *r),
        [S((rows // 4, cols // 4, cw), BF)],
        [VM] * (ni + 2),
        name="project",
    )(keep, att, *whole)
    return (fine_skip, coarse_out)


def solution(mesh):
    inner = mesh.shape["inner"]
    heads = 16 // inner
    devices = mesh.devices.reshape(heads, mesh.shape["outer"] // heads, inner)
    return jax.shard_map(
        body,
        mesh=jax.sharding.Mesh(devices, OUTER + ("inner",)),
        in_specs=(
            P(OUTER, "inner", None),
            P(),
            P(),
            P(),
            P(),
            P(),
            P(),
            P(None, "inner"),
            P("inner", None),
        ),
        out_specs=(P(OUTER, "inner", None), P(OUTER, "inner", None)),
        check_vma=False,
    )
```
